32 devices in a mesh: grp: 2 (over x), gx: 8 (over z, y), gy: 2 (over core).
Axes of the slice: x: 2, y: 2, z: 4, core: 2. Of those that a mesh axis runs over, the one named last changes fastest.
Arguments:
- mode_shapes: float32 [36, 64, 32, 256], P('grp', 'gx', 'gy'), parts along dimension 0, may hold values from -2.5 to 2.5
- eigenvalues: float32 [12], P('grp'), parts along dimension 0, may hold values from 2 to 20
- density: float32 [128, 32, 256], P(('grp', 'gx'), 'gy'), parts along dimension 0, may hold values from 0.1 to 1
- filter_mass: float32 [128, 32, 256], P(('grp', 'gx'), 'gy'), parts along dimension 0, may hold values from 0.5 to 4
- passive: int32 [128, 32, 256], P(('grp', 'gx'), 'gy'), parts along dimension 0, may hold values 0 or 1
Outputs:
- filtered: float32 [12, 64, 32, 256], P('grp', 'gx', 'gy'), parts along dimension 0
The draws below stay inside these ranges and needn't reach their ends.
There are 2 independent parts, one for each index of `grp`. The reference program is written for one: setup_inputs(seed, part) draws one part's arguments, and reference() takes and returns one part's arrays. A program takes and returns all parts, laid end to end along the dimension named above; each array names one. Nothing has to cross between parts.
All inputs are finite; a program needn't handle non-finite values. No bound on the sum of `passive` on one device may be relied on, other than what follows from the above.
Results may differ from the reference program's by a relative error of at most 0.0001.
Values sent between devices are 32-bit elements; how exact they have to be, the bound alone decides.
No kernel may reach another device: no remote copies, remote signals or barrier semaphores. Data moves between devices by JAX's collectives and lax.ppermute only.
A program may use at most 128 MiB of HBM per device.

```python
import math
import jax
import jax.numpy as jnp
import numpy as np
from jax import lax

MODES = 6
NZ = 256
ITERS = 3
RMIN = 4
NX = 64
NY = 32


def plant(values, key, low, largest):
    longest = values.shape.index(max(values.shape))
    spots = []
    for shift in (0, 1):
        where = [jax.random.randint(jax.random.fold_in(key, axis), (), 0, length) for axis, length in enumerate(values.shape)]
        where[longest] = (where[longest] + shift) % values.shape[longest]
        spots.append(tuple(where))
    return values.at[spots[0]].set(low).at[spots[1]].set(largest)


def level_of(key, extent, cuts, smallest, top_value):
    gain = 1.0
    for axis_at, blocks in cuts:
        heights = jax.random.uniform(jax.random.fold_in(jax.random.fold_in(key, 6), axis_at), (blocks,), jnp.float32, smallest / len(cuts), top_value / len(cuts))
        gain = gain * jnp.repeat(jnp.exp(heights), extent[axis_at] // blocks).reshape((-1,) + (1,) * (len(extent) - 1 - axis_at))
    return gain


def gaussian(stream_key, extent, scale, limit, split=(), held_as=jnp.bfloat16):
    factor_of = level_of(stream_key, extent, split, -0.22, 0.18) if split else 1.0
    result = jax.random.normal(stream_key, extent, jnp.float32) * scale * factor_of
    return jnp.minimum(jnp.maximum(result, -limit), limit).astype(held_as)


def setup_inputs(seed: int = 0, part: int = 0) -> dict:
    arg_keys = jax.random.split(jax.random.key(seed), 6)
    part_splits = jax.random.split(jax.random.fold_in(arg_keys[5], part), 6)
    return {
        "mode_shapes": gaussian(part_splits[0], (3 * MODES, NX, NY, NZ), 0.3, 2.5, ((1, 8), (2, 2)), jnp.float32),
        "eigenvalues": jnp.clip(jnp.exp(jax.random.uniform(part_splits[1], (MODES,), jnp.float32, math.log(2.0), math.log(20.0))), 2.0, 20.0),
        "density": jnp.clip(0.1 + 0.9 * jax.random.uniform(part_splits[2], (NX, NY, NZ), jnp.float32) ** level_of(part_splits[2], (NX, NY, NZ), ((0, 8), (1, 2)), -0.2, 0.2), 0.1, 1.0),
        "filter_mass": jnp.clip(jnp.exp(math.log(4.0) - 2.0794415 * jax.random.uniform(part_splits[3], (NX, NY, NZ), jnp.float32) ** level_of(part_splits[3], (NX, NY, NZ), ((0, 8), (1, 2)), -0.2, 0.2)), 0.5, 4.0),
        "passive": plant((jax.random.randint(part_splits[4], (NX, NY, NZ), 0, 4) < 1).astype(jnp.int32), jax.random.fold_in(part_splits[4], 1), 0, 1),
    }


void_floor = 0.001

def element_table():
    poisson = 0.3
    lame_first = poisson / ((1.0 + poisson) * (1.0 - 2.0 * poisson))
    shear_mod = 1.0 / (2.0 * (1.0 + poisson))
    elastic = np.zeros((6, 6))
    elastic[:3, :3] = lame_first
    for entry in range(3):
        elastic[entry, entry] += 2.0 * shear_mod
        elastic[entry + 3, entry + 3] = shear_mod
    offset = 1.0 / math.sqrt(3.0)
    gauss_points = [(1.0 - offset) / 2.0, (1.0 + offset) / 2.0]
    stiffness = np.zeros((24, 24))
    inertia = np.zeros((24, 24))
    for point_x in gauss_points:
        for point_y in gauss_points:
            for point_z in gauss_points:
                coords = [point_x, point_y, point_z]
                values = np.zeros(8)
                gradient = np.zeros((8, 3))
                for corner in range(8):
                    corner_bits = [corner % 2, corner // 2 % 2, corner // 4]
                    factors = [coords[dimen] if corner_bits[dimen] else 1.0 - coords[dimen] for dimen in range(3)]
                    sign_list = [1.0 if corner_bits[dimen] else -1.0 for dimen in range(3)]
                    values[corner] = factors[0] * factors[1] * factors[2]
                    for dimen in range(3):
                        others = [factors[other_dim] for other_dim in range(3) if other_dim != dimen]
                        gradient[corner, dimen] = sign_list[dimen] * others[0] * others[1]
                strain = np.zeros((6, 24))
                for corner in range(8):
                    column = 3 * corner
                    grad_x, grad_y, grad_z = gradient[corner]
                    strain[0, column] = grad_x
                    strain[1, column + 1] = grad_y
                    strain[2, column + 2] = grad_z
                    strain[3, column] = grad_y
                    strain[3, column + 1] = grad_x
                    strain[4, column + 1] = grad_z
                    strain[4, column + 2] = grad_y
                    strain[5, column] = grad_z
                    strain[5, column + 2] = grad_x
                stiffness += 0.125 * strain.T @ elastic @ strain
                shape_matrix = np.kron(values[None, :], np.eye(3))
                inertia += 0.125 * shape_matrix.T @ shape_matrix
    return np.concatenate([stiffness, inertia], axis=0).astype(np.float32)

def contract(field, table):
    count_x = field.shape[1] - 1
    count_y = field.shape[2] - 1
    zeros = jnp.zeros_like(field[..., :1])
    raised = jnp.concatenate([field[..., 1:], zeros], axis=-1)
    pieces = []
    for corner in range(8):
        source = raised if corner // 4 else field
        shift_x = corner % 2
        shift_y = corner // 2 % 2
        pieces.append(source[:, shift_x:shift_x + count_x, shift_y:shift_y + count_y, :])
    flat = jnp.concatenate(pieces, axis=0).reshape(24, -1)
    product = jnp.dot(table, flat, precision=lax.Precision.HIGHEST, preferred_element_type=jnp.float32)
    stiff = lax.optimization_barrier(jnp.sum(flat * product[:24], axis=0)).reshape(count_x, count_y, -1)
    inert = lax.optimization_barrier(jnp.sum(flat * product[24:], axis=0)).reshape(count_x, count_y, -1)
    return (stiff, inert)

def boundary_count(pos_x, total_x, pos_y, total_y, depth):
    pos_z = jnp.arange(depth, dtype=jnp.int32)
    missing_x = ((pos_x == 0).astype(jnp.float32) + (pos_x == total_x - 1).astype(jnp.float32))[:, None, None]
    missing_y = ((pos_y == 0).astype(jnp.float32) + (pos_y == total_y - 1).astype(jnp.float32))[None, :, None]
    missing_z = ((pos_z == 0).astype(jnp.float32) + (pos_z == depth - 1).astype(jnp.float32))[None, None, :]
    return 6.0 - missing_x - missing_y - missing_z

def stencil(vector, padded, filter_mass, count, radius_sq):
    beside = padded[:, 2:, 1:-1] + padded[:, :-2, 1:-1] + padded[:, 1:-1, 2:] + padded[:, 1:-1, :-2]
    zeros = jnp.zeros_like(vector[..., :1])
    beside = beside + jnp.concatenate([vector[..., 1:], zeros], axis=-1)
    beside = beside + jnp.concatenate([zeros, vector[..., :-1]], axis=-1)
    return filter_mass * vector + radius_sq * (count * vector - beside)

def expand(values):
    return values[:, None, None, None]

def local_dot(first, second):
    return lax.optimization_barrier(jnp.sum(first * second, axis=(1, 2, 3)))

def reference(mode_shapes, eigenvalues, density, filter_mass, passive):
    table = jnp.asarray(element_table(), jnp.float32)
    design = (1 - passive).astype(jnp.float32)
    slope = 3.0 * (1.0 - void_floor) * density * density
    padded_modes = jnp.pad(mode_shapes, ((0, 0), (0, 1), (0, 1), (0, 0)))
    sens_list = []
    for mode in range(MODES):
        stiff, inert = contract(padded_modes[3 * mode:3 * mode + 3], table)
        sens_list.append((slope * stiff - eigenvalues[mode] * inert) * design)
    sens = jnp.stack(sens_list, axis=0)
    radius_sq = RMIN * RMIN / 12.0
    count = boundary_count(jnp.arange(NX, dtype=jnp.int32), NX, jnp.arange(NY, dtype=jnp.int32), NY, NZ)
    diagonal = filter_mass + radius_sq * count

    def operate(vector):
        padded = jnp.pad(vector, ((0, 0), (1, 1), (1, 1), (0, 0)))
        return stencil(vector, padded, filter_mass, count, radius_sq)
    solution = jnp.zeros_like(sens)
    resid = sens
    precond = resid / diagonal
    direction = precond
    rz_now = local_dot(resid, precond)
    for step in range(ITERS):
        image = operate(direction)
        step_size = rz_now / local_dot(direction, image)
        solution = solution + expand(step_size) * direction
        resid = resid - expand(step_size) * image
        if step + 1 < ITERS:
            precond = resid / diagonal
            rz_next = local_dot(resid, precond)
            direction = precond + expand(rz_next / rz_now) * direction
            rz_now = rz_next
    return solution
```

```python
import math
from functools import partial

import jax
import jax.numpy as jnp
import numpy as np
from jax import lax
from jax.experimental import pallas as pl
from jax.experimental.pallas import tpu as pltpu
from jax.sharding import PartitionSpec as P

ITERS = 3
RMIN = 4
RADIUS_SQ = RMIN * RMIN / 12.0
DOWN = 3
UP = 2
VMEM = 56 * 1024 * 1024

void_floor = 0.001


def element_table():
    poisson = 0.3
    lame_first = poisson / ((1.0 + poisson) * (1.0 - 2.0 * poisson))
    shear_mod = 1.0 / (2.0 * (1.0 + poisson))
    elastic = np.zeros((6, 6))
    elastic[:3, :3] = lame_first
    for entry in range(3):
        elastic[entry, entry] += 2.0 * shear_mod
        elastic[entry + 3, entry + 3] = shear_mod
    offset = 1.0 / math.sqrt(3.0)
    gauss_points = [(1.0 - offset) / 2.0, (1.0 + offset) / 2.0]
    stiffness = np.zeros((24, 24))
    inertia = np.zeros((24, 24))
    for point_x in gauss_points:
        for point_y in gauss_points:
            for point_z in gauss_points:
                coords = [point_x, point_y, point_z]
                values = np.zeros(8)
                gradient = np.zeros((8, 3))
                for corner in range(8):
                    corner_bits = [corner % 2, corner // 2 % 2, corner // 4]
                    factors = [
                        coords[dimen] if corner_bits[dimen] else 1.0 - coords[dimen]
                        for dimen in range(3)
                    ]
                    sign_list = [1.0 if corner_bits[dimen] else -1.0 for dimen in range(3)]
                    values[corner] = factors[0] * factors[1] * factors[2]
                    for dimen in range(3):
                        others = [
                            factors[other_dim] for other_dim in range(3) if other_dim != dimen
                        ]
                        gradient[corner, dimen] = sign_list[dimen] * others[0] * others[1]
                strain = np.zeros((6, 24))
                for corner in range(8):
                    column = 3 * corner
                    grad_x, grad_y, grad_z = gradient[corner]
                    strain[0, column] = grad_x
                    strain[1, column + 1] = grad_y
                    strain[2, column + 2] = grad_z
                    strain[3, column] = grad_y
                    strain[3, column + 1] = grad_x
                    strain[4, column + 1] = grad_z
                    strain[4, column + 2] = grad_y
                    strain[5, column] = grad_z
                    strain[5, column + 2] = grad_x
                stiffness += 0.125 * strain.T @ elastic @ strain
                shape_matrix = np.kron(values[None, :], np.eye(3))
                inertia += 0.125 * shape_matrix.T @ shape_matrix
    return stiffness, inertia


def energy_classes():
    stiffness, inertia = element_table()
    pair = np.array([[1.0, 1.0], [-1.0, 1.0]])
    basis = np.kron(np.kron(np.kron(pair, pair), pair), np.eye(3))
    stiffness = basis @ stiffness @ basis.T / 64.0
    inertia = basis @ inertia @ basis.T / 64.0
    squares, products = {}, {}
    for i in range(24):
        key = (round(stiffness[i, i], 9), round(inertia[i, i], 9))
        squares.setdefault(key, []).append(i)
        for j in range(i + 1, 24):
            if abs(stiffness[i, j]) > 1e-9:
                products.setdefault(round(stiffness[i, j], 9), []).append((i, j))
    squares = [
        (float(stiffness[v[0], v[0]]) if abs(k[0]) > 1e-9 else 0.0, float(inertia[v[0], v[0]]), v)
        for k, v in squares.items()
    ]
    products = [(2.0 * float(stiffness[v[0]]), v) for v in products.values()]
    return squares, products


def element_energies(entries, squares, products):
    stiff, inert = None, {}
    for weight, mass, members in squares:
        total = sum(entries[i] * entries[i] for i in members[1:]) + entries[members[0]] * entries[members[0]]
        if weight:
            stiff = total * weight if stiff is None else stiff + total * weight
        inert[mass] = inert[mass] + total if mass in inert else total
    for weight, members in products:
        stiff = stiff + weight * sum(entries[i] * entries[j] for i, j in members)
    return stiff, sum(total * mass for mass, total in inert.items())


def shift_lane(value, step):
    size = value.shape[1]
    lane = lax.broadcasted_iota(jnp.int32, value.shape, 1)
    edge = size - 1 if step > 0 else 0
    return jnp.where(lane == edge, 0.0, pltpu.roll(value, (-step) % size, 1))


def shift_row(value, step):
    size = value.shape[0]
    row = lax.broadcasted_iota(jnp.int32, value.shape, 0)
    edge = size - 1 if step > 0 else 0
    return jnp.where(row == edge, 0.0, pltpu.roll(value, (-step) % size, 0))


def missing_plane(shape):
    row = lax.broadcasted_iota(jnp.int32, shape, 0)
    lane = lax.broadcasted_iota(jnp.int32, shape, 1)
    count = jnp.zeros(shape, jnp.float32)
    for index, size in ((row, shape[0]), (lane, shape[1])):
        count += (index == 0).astype(jnp.float32) + (index == size - 1).astype(jnp.float32)
    return count


def scalar(flag):
    return jnp.where(flag, 1.0, 0.0).astype(jnp.float32)


def energy_kernel(
    place, eig, modes, swap, field, field_swap, halo, halo_swap,
    z_out, mass_out, ghost_mass, down_out, up_out,
    nodes, fields, sems,
):
    group, layers, half, depth = swap.shape
    width = 2 * half
    core, first, last = place[0], place[1], place[2]
    mine = pl.multiple_of(core * half, half)
    other = pl.multiple_of((1 - core) * half, half)
    start = core * group
    copies = []

    def move(source, target):
        copy = pltpu.make_async_copy(source, target, sems.at[len(copies)])
        copy.start()
        copies.append(copy)

    move(modes.at[pl.ds(start, group)], nodes.at[:, pl.ds(0, layers), pl.ds(mine, half), :])
    move(swap, nodes.at[:, pl.ds(0, layers), pl.ds(other, half), :])
    move(halo.at[pl.ds(0, group)], nodes.at[:, layers, pl.ds(mine, half), :])
    move(halo_swap.at[pl.ds(0, group)], nodes.at[:, layers, pl.ds(other, half), :])
    move(field, fields.at[:, :, pl.ds(mine, half), :])
    move(field_swap, fields.at[:, :, pl.ds(other, half), :])
    move(halo.at[pl.ds(group, 2)], ghost_mass.at[:, pl.ds(mine, half), :])
    move(halo_swap.at[pl.ds(group, 2)], ghost_mass.at[:, pl.ds(other, half), :])
    nodes[:, :, pl.ds(width, 8), :] = jnp.zeros((group, layers + 1, 8, depth), jnp.float32)
    for copy in copies:
        copy.wait()

    squares, products = energy_classes()
    shape = (width, depth)
    missing = missing_plane(shape)
    for x in range(layers):
        mass = fields[1, x]
        count = 6.0 - missing
        if x == 0:
            count -= scalar(first)
        if x == layers - 1:
            count -= scalar(last)
        mass_out[x] = mass
        inverse = 1.0 / (mass + RADIUS_SQ * count)
        design = (1.0 - fields[2, x]) * inverse
        rho = fields[0, x]
        fields[0, x] = 3.0 * (1.0 - void_floor) * rho * rho * design
        fields[2, x] = design
    up_out[UP * (group // 3)] = fields[1, layers - 1]

    tiles = width // 8

    def transform(mode, x, tile):
        entries = []
        for comp in range(3):
            parts = []
            for offset in (0, 1):
                low = nodes[3 * mode + comp, x, pl.ds(tile * 8 + offset, 8), :]
                high = shift_lane(low, 1)
                parts.append((low + high, high - low))
            (sum_0, diff_0), (sum_1, diff_1) = parts
            entries.append(((sum_0 + sum_1, sum_1 - sum_0), (diff_0 + diff_1, diff_1 - diff_0)))
        return entries

    for mode in range(group // 3):
        value = eig[start // 3 + mode]
        for tile in range(tiles):
            rows = pl.ds(tile * 8, 8)
            near = transform(mode, 0, tile)
            for x in range(layers):
                far = transform(mode, x + 1, tile)
                entries = [None] * 24
                for comp in range(3):
                    for z in (0, 1):
                        for y in (0, 1):
                            a, b = near[comp][z][y], far[comp][z][y]
                            entries[3 * (2 * y + 4 * z) + comp] = a + b
                            entries[3 * (1 + 2 * y + 4 * z) + comp] = b - a
                stiff, inert = element_energies(entries, squares, products)
                sens = fields[0, x, rows, :] * stiff - (value * fields[2, x, rows, :]) * inert
                z_out[mode, x, rows, :] = sens
                if x < DOWN:
                    down_out[mode, x, rows, :] = sens
                if x >= layers - UP:
                    up_out[UP * mode + x - (layers - UP), rows, :] = sens
                near = far


def filter_kernel(
    place, z_in, mass_in, ghost_mass, down_in, up_in,
    keep, send, moments,
    first_field, second_field, inverse, count_of,
):
    modes, layers, width, depth = z_in.shape
    half = width // 2
    core, first, last = place[0], place[1], place[2]
    mine = pl.multiple_of(core * half, half)
    other = pl.multiple_of((1 - core) * half, half)
    shape = (width, depth)
    missing = missing_plane(shape)

    def mass_at(x):
        if x < 0:
            return up_in[UP * modes]
        return mass_in[x] if x < layers else ghost_mass[x - layers]

    for x in range(-1, layers + 2):
        count = 6.0 - missing
        if x == 0:
            count -= scalar(first)
        if x == layers - 1:
            count -= scalar(last)
        count_of[x + 1] = count
        value = 1.0 / (mass_at(x) + RADIUS_SQ * count)
        if x < 0:
            value = value * (1.0 - scalar(first))
        if x >= layers:
            value = value * (1.0 - scalar(last))
        inverse[x + 1] = value

    def apply(before, here, after, x):
        beside = before + after
        beside += shift_lane(here, 1) + shift_lane(here, -1)
        beside += shift_row(here, 1) + shift_row(here, -1)
        return mass_at(x) * here + RADIUS_SQ * (count_of[x + 1] * here - beside)

    def fold(value):
        total = None
        for row in range(0, width, 8):
            for lane in range(0, depth, 128):
                piece = value[row : row + 8, lane : lane + 128]
                total = piece if total is None else total + piece
        return total

    moments[...] = jnp.zeros(moments.shape, jnp.float32)

    def one_mode(mode, carry):
        def zeroth(x):
            if x < 0:
                return up_in[UP * mode + UP + x]
            return z_in[mode, x] if x < layers else down_in[mode, x - layers]

        sums = [jnp.zeros((8, 128), jnp.float32) for _ in range(6)]
        for x in range(-1, layers + 2):
            here = zeroth(x)
            image = apply(zeroth(x - 1), here, zeroth(x + 1), x)
            first_field[x + 1] = image * inverse[x + 1]
            if 0 <= x < layers:
                diag = mass_at(x) + RADIUS_SQ * count_of[x + 1]
                sums[0] += fold(here * (diag * here))
                sums[1] += fold(here * image)
                one = first_field[x + 1]
                sums[2] += fold(one * image)
        for x in range(0, layers + 1):
            here = first_field[x + 1]
            image = apply(first_field[x], here, first_field[x + 2], x)
            two = image * inverse[x + 1]
            second_field[x] = two
            if x < layers:
                sums[3] += fold(here * image)
                sums[4] += fold(two * image)
        for x in range(layers):
            here, after = second_field[x], second_field[x + 1]
            sums[5] += fold(mass_at(x) * here * here)
            ahead = after - here
            if x == layers - 1:
                ahead = ahead * (1.0 - scalar(last))
            row = lax.broadcasted_iota(jnp.int32, shape, 0)
            lane = lax.broadcasted_iota(jnp.int32, shape, 1)
            aside = jnp.where(row == width - 1, 0.0, pltpu.roll(here, width - 1, 0) - here)
            above = jnp.where(lane == depth - 1, 0.0, pltpu.roll(here, depth - 1, 1) - here)
            sums[5] += RADIUS_SQ * fold(ahead * ahead + aside * aside + above * above)
        slot = core * modes + mode
        for k in range(6):
            moments[k, pl.ds(slot, 1), :] = jnp.sum(sums[k], axis=0, keepdims=True)
        for target, rows in ((keep, mine), (send, other)):
            span = pl.ds(rows, half)
            for x in range(layers):
                target[0, mode, x] = z_in[mode, x, span, :]
                target[1, mode, x] = first_field[x + 1, span, :]
                target[2, mode, x] = second_field[x, span, :]
        return carry

    lax.fori_loop(0, modes, one_mode, 0)


def combine_kernel(place, moments, keep, swap, out):
    modes, layers = keep.shape[1:3]
    core = place[0]
    shape = moments.shape[1:]
    m = [jnp.broadcast_to(jnp.sum(moments[k], axis=1, keepdims=True), shape) for k in range(6)]
    one, two = m[2] / m[1], m[3] / m[1]
    pivot = m[3] - one * m[2]
    cross = m[4] - two * m[2]
    slope = cross / pivot
    depth = m[5] - two * m[3] - slope * cross
    right_1 = m[1] - one * m[0]
    right_2 = m[2] - two * m[0] - slope * right_1
    c2 = right_2 / depth
    c1 = (right_1 - cross * c2) / pivot
    c0 = (m[0] - m[2] * c1 - m[3] * c2) / m[1]
    reps = keep.shape[4] // 128
    for source, start in ((keep, core * modes), (swap, (1 - core) * modes)):
        for mode in range(modes):
            row = lax.broadcasted_iota(jnp.int32, shape, 0) == start + mode

            def pick(c):
                value = jnp.sum(jnp.where(row, c, 0.0), axis=0, keepdims=True)
                return jnp.concatenate([value] * reps, axis=1)

            a, b, c = pick(c0), pick(c1), pick(c2)
            for x in range(layers):
                out[start + mode, x] = (
                    a * source[0, mode, x] + b * source[1, mode, x] + c * source[2, mode, x]
                )


def all_sums(value, axis):
    size = lax.axis_size(axis)
    stride = 1
    while stride < size:
        radix = 2 if stride == 1 or size // stride < 4 else 4
        total = value
        for step in range(1, radix):
            pairs = [(i, i ^ (step * stride)) for i in range(size)]
            total = total + lax.ppermute(value, axis, pairs)
        value, stride = total, stride * radix
    return value


def local(mode_shapes, eigenvalues, density, filter_mass, passive):
    f32 = jnp.float32
    layers, half, depth = density.shape
    rows = mode_shapes.shape[0]
    group = rows // 2
    modes = group // 3
    width = 2 * half
    core, at = lax.axis_index("gy"), lax.axis_index("gx")
    count = lax.axis_size("gx")
    place = jnp.stack([core, (at == 0).astype(jnp.int32), (at == count - 1).astype(jnp.int32)]).astype(jnp.int32)
    across = [(0, 1), (1, 0)]
    straight = [(2 * i + c, 2 * i - 2 + c) for i in range(1, count) for c in (0, 1)]
    crossed = [(2 * i + c, 2 * i - 1 - c) for i in range(1, count) for c in (0, 1)]
    both = ("gx", "gy")

    mine = lax.dynamic_slice_in_dim(mode_shapes[:, 0], core * group, group, 0)
    theirs = lax.dynamic_slice_in_dim(mode_shapes[:, 0], (1 - core) * group, group, 0)
    halo = lax.ppermute(jnp.concatenate([mine, filter_mass[:2]]), both, straight)
    halo_swap = lax.ppermute(jnp.concatenate([theirs, filter_mass[:2]]), both, crossed)
    field = jnp.stack([density, filter_mass, passive.astype(f32)])
    field_swap = lax.ppermute(field, "gy", across)
    swap = lax.ppermute(
        lax.dynamic_slice_in_dim(mode_shapes, (1 - core) * group, group, 0), "gy", across
    )

    smem = pl.BlockSpec(memory_space=pltpu.SMEM)
    vmem = pl.BlockSpec(memory_space=pltpu.VMEM)
    anywhere = pl.BlockSpec(memory_space=pl.ANY)
    params = pltpu.CompilerParams(vmem_limit_bytes=VMEM)
    z0, mass, ghost_mass, down, up = pl.pallas_call(
        energy_kernel,
        out_shape=(
            jax.ShapeDtypeStruct((modes, layers, width, depth), f32),
            jax.ShapeDtypeStruct((layers, width, depth), f32),
            jax.ShapeDtypeStruct((2, width, depth), f32),
            jax.ShapeDtypeStruct((modes, DOWN, width, depth), f32),
            jax.ShapeDtypeStruct((UP * modes + 1, width, depth), f32),
        ),
        in_specs=[smem, smem] + [anywhere] * 6,
        out_specs=(vmem,) * 5,
        scratch_shapes=[
            pltpu.VMEM((group, layers + 1, width + 8, depth), f32),
            pltpu.VMEM((3, layers, width, depth), f32),
            pltpu.SemaphoreType.DMA((8,)),
        ],
        compiler_params=params,
        name="energies",
    )(place, eigenvalues, mode_shapes, swap, field, field_swap, halo, halo_swap)

    down = lax.ppermute(down, "gx", [(i, i - 1) for i in range(1, count)])
    up = lax.ppermute(up, "gx", [(i, i + 1) for i in range(count - 1)])

    pieces = (3, modes, layers, half, depth)
    keep, send, moments = pl.pallas_call(
        filter_kernel,
        out_shape=(
            jax.ShapeDtypeStruct(pieces, f32),
            jax.ShapeDtypeStruct(pieces, f32),
            jax.ShapeDtypeStruct((6, 8, 128), f32),
        ),
        in_specs=[smem] + [vmem] * 5,
        out_specs=(vmem,) * 3,
        scratch_shapes=[
            pltpu.VMEM((layers + 3, width, depth), f32),
            pltpu.VMEM((layers + 1, width, depth), f32),
            pltpu.VMEM((layers + 3, width, depth), f32),
            pltpu.VMEM((layers + 3, width, depth), f32),
        ],
        compiler_params=params,
        name="krylov",
    )(place, z0, mass, ghost_mass, down, up)

    swapped = lax.ppermute(send, "gy", across)
    moments = moments + lax.ppermute(moments, "gy", across)
    moments = all_sums(moments, "gx")

    return pl.pallas_call(
        combine_kernel,
        out_shape=jax.ShapeDtypeStruct((2 * modes, layers, half, depth), f32),
        in_specs=[smem] + [vmem] * 3,
        out_specs=vmem,
        compiler_params=params,
        name="combine",
    )(place, moments, keep, swapped)


def solution(mesh):
    in_specs = (
        P("grp", "gx", "gy", None),
        P("grp"),
        P(("grp", "gx"), "gy", None),
        P(("grp", "gx"), "gy", None),
        P(("grp", "gx"), "gy", None),
    )
    out_specs = P("grp", "gx", "gy", None)
    return jax.shard_map(local, mesh=mesh, in_specs=in_specs, out_specs=out_specs, check_vma=False)
```

```python
import math
from functools import partial

import jax
import jax.numpy as jnp
import numpy as np
from jax import lax
from jax.experimental import pallas as pl
from jax.experimental.pallas import tpu as pltpu
from jax.sharding import PartitionSpec as P

ITERS = 3
RMIN = 4
RADIUS_SQ = RMIN * RMIN / 12.0
DOWN = 3
UP = 2


void_floor = 0.001


def element_table():
    poisson = 0.3
    lame_first = poisson / ((1.0 + poisson) * (1.0 - 2.0 * poisson))
    shear_mod = 1.0 / (2.0 * (1.0 + poisson))
    elastic = np.zeros((6, 6))
    elastic[:3, :3] = lame_first
    for entry in range(3):
        elastic[entry, entry] += 2.0 * shear_mod
        elastic[entry + 3, entry + 3] = shear_mod
    offset = 1.0 / math.sqrt(3.0)
    gauss_points = [(1.0 - offset) / 2.0, (1.0 + offset) / 2.0]
    stiffness = np.zeros((24, 24))
    inertia = np.zeros((24, 24))
    for point_x in gauss_points:
        for point_y in gauss_points:
            for point_z in gauss_points:
                coords = [point_x, point_y, point_z]
                values = np.zeros(8)
                gradient = np.zeros((8, 3))
                for corner in range(8):
                    corner_bits = [corner % 2, corner // 2 % 2, corner // 4]
                    factors = [
                        coords[dimen] if corner_bits[dimen] else 1.0 - coords[dimen]
                        for dimen in range(3)
                    ]
                    sign_list = [1.0 if corner_bits[dimen] else -1.0 for dimen in range(3)]
                    values[corner] = factors[0] * factors[1] * factors[2]
                    for dimen in range(3):
                        others = [
                            factors[other_dim] for other_dim in range(3) if other_dim != dimen
                        ]
                        gradient[corner, dimen] = sign_list[dimen] * others[0] * others[1]
                strain = np.zeros((6, 24))
                for corner in range(8):
                    column = 3 * corner
                    grad_x, grad_y, grad_z = gradient[corner]
                    strain[0, column] = grad_x
                    strain[1, column + 1] = grad_y
                    strain[2, column + 2] = grad_z
                    strain[3, column] = grad_y
                    strain[3, column + 1] = grad_x
                    strain[4, column + 1] = grad_z
                    strain[4, column + 2] = grad_y
                    strain[5, column] = grad_z
                    strain[5, column + 2] = grad_x
                stiffness += 0.125 * strain.T @ elastic @ strain
                shape_matrix = np.kron(values[None, :], np.eye(3))
                inertia += 0.125 * shape_matrix.T @ shape_matrix
    return stiffness, inertia


def energy_classes():
    stiffness, inertia = element_table()
    pair = np.array([[1.0, 1.0], [-1.0, 1.0]])
    basis = np.kron(np.kron(np.kron(pair, pair), pair), np.eye(3))
    stiffness = basis @ stiffness @ basis.T / 64.0
    inertia = basis @ inertia @ basis.T / 64.0
    squares, products = {}, {}
    for i in range(24):
        key = (round(stiffness[i, i], 9), round(inertia[i, i], 9))
        squares.setdefault(key, []).append(i)
        for j in range(i + 1, 24):
            if abs(stiffness[i, j]) > 1e-9:
                products.setdefault(round(stiffness[i, j], 9), []).append((i, j))
    squares = [
        (float(stiffness[v[0], v[0]]) if abs(k[0]) > 1e-9 else 0.0, float(inertia[v[0], v[0]]), v)
        for k, v in squares.items()
    ]
    products = [(2.0 * float(stiffness[v[0]]), v) for v in products.values()]
    return squares, products


def element_energies(entries, squares, products):
    stiff, inert = None, {}
    for weight, mass, members in squares:
        total = entries[members[0]] * entries[members[0]]
        for i in members[1:]:
            total = total + entries[i] * entries[i]
        if weight:
            stiff = total * weight if stiff is None else stiff + total * weight
        inert[mass] = inert[mass] + total if mass in inert else total
    for weight, members in products:
        total = entries[members[0][0]] * entries[members[0][1]]
        for i, j in members[1:]:
            total = total + entries[i] * entries[j]
        stiff = stiff + weight * total
    return stiff, sum(total * mass for mass, total in inert.items())


def shifted(value, step, dim):
    size = value.shape[dim]
    index = lax.broadcasted_iota(jnp.int32, value.shape, dim)
    edge = size - 1 if step > 0 else 0
    return jnp.where(index == edge, 0.0, pltpu.roll(value, (-step) % size, dim))


def missing_plane(shape):
    count = jnp.zeros(shape, jnp.float32)
    for dim in (0, 1):
        index = lax.broadcasted_iota(jnp.int32, shape, dim)
        count += (index == 0).astype(jnp.float32) + (index == shape[dim] - 1).astype(jnp.float32)
    return count


def scalar(flag):
    return jnp.where(flag, 1.0, 0.0).astype(jnp.float32)


def neighbour_count(missing, x, layers, first, last):
    count = 6.0 - missing
    if x == 0:
        count -= scalar(first)
    if x == layers - 1:
        count -= scalar(last)
    return count


def halves(core, half):
    return pl.multiple_of(core * half, half), pl.multiple_of((1 - core) * half, half)


def pack_kernel(place, modes, density, mass, passive, straight, crossed, swap, field, sems):
    group, layers = modes.shape[0] // 2, modes.shape[1]
    core = place[0]
    mine, theirs = core * group, (1 - core) * group
    copies = [
        pltpu.make_async_copy(modes.at[pl.ds(mine, group), 0], straight.at[pl.ds(0, group)], sems.at[0]),
        pltpu.make_async_copy(modes.at[pl.ds(theirs, group), 0], crossed.at[pl.ds(0, group)], sems.at[1]),
    ]
    copies += [
        pltpu.make_async_copy(modes.at[theirs + i], swap.at[pl.ds(i * layers, layers)], sems.at[2 + i])
        for i in range(group)
    ]
    for copy in copies:
        copy.start()
    base = group * layers
    for x in range(layers):
        rho, weight = density[x], mass[x]
        design = (1 - passive[x]).astype(jnp.float32)
        slope = 3.0 * (1.0 - void_floor) * rho * rho * design
        for k, value in enumerate((slope, weight, design)):
            swap[base + k * layers + x] = value
            field[k * layers + x] = value
        if x < 2:
            straight[group + x] = weight
            crossed[group + x] = weight
    for copy in copies:
        copy.wait()


def energy_kernel(low, high, end, *refs):
    place, eig, modes, swap, field = refs[:5]
    refs = refs[5:]
    if end:
        (halo, halo_swap, _, z_out, mass_out, ghost_mass), refs = refs[:6], refs[6:]
    else:
        (_, z_out, mass_out), refs = refs[:3], refs[3:]
    nodes, fields, sums, sems = refs
    layers, half, depth = modes.shape[1:]
    group = modes.shape[0] // 2
    width, count = 2 * half, high - low
    core, first, last = place[0], place[1], place[2]
    mine, other = halves(core, half)
    start = core * group
    copies = []

    def move(source, target):
        copy = pltpu.make_async_copy(source, target, sems.at[len(copies)])
        copy.start()
        copies.append(copy)

    base = group * layers
    for k in range(3):
        move(field.at[pl.ds(k * layers + low, count)], fields.at[k, :, pl.ds(mine, half), :])
        move(swap.at[pl.ds(base + k * layers + low, count)], fields.at[k, :, pl.ds(other, half), :])
    held = count if end else count + 1
    move(modes.at[pl.ds(start, group), pl.ds(low, held)], nodes.at[:, pl.ds(0, held), pl.ds(mine, half), :])
    for i in range(group):
        move(swap.at[pl.ds(i * layers + low, held)], nodes.at[i, pl.ds(0, held), pl.ds(other, half), :])
    if end:
        move(halo.at[pl.ds(0, group)], nodes.at[:, count, pl.ds(mine, half), :])
        move(halo_swap.at[pl.ds(0, group)], nodes.at[:, count, pl.ds(other, half), :])
        move(halo.at[pl.ds(group, 2)], ghost_mass.at[:, pl.ds(mine, half), :])
        move(halo_swap.at[pl.ds(group, 2)], ghost_mass.at[:, pl.ds(other, half), :])
    for copy in copies:
        copy.wait()

    squares, products = energy_classes()
    missing = missing_plane((width, depth))
    for i in range(count):
        mass = fields[1, i]
        mass_out[i] = mass
        inverse = 1.0 / (mass + RADIUS_SQ * neighbour_count(missing, low + i, layers, first, last))
        fields[0, i] = fields[0, i] * inverse
        fields[2, i] = fields[2, i] * inverse
    if end:
        z_out[z_out.shape[0] - 1] = fields[1, count - 1]

    def transform(mode, i):
        for comp in range(3):
            here = nodes[3 * mode + comp, i]
            above = shifted(here, 1, 1)
            for z, value in ((0, here + above), (1, above - here)):
                beside = shifted(value, 1, 0)
                sums[i % 3, 4 * comp + 2 * z] = value + beside
                sums[i % 3, 4 * comp + 2 * z + 1] = beside - value

    def energies(mode, value, i):
        for row in range(0, width, 8):
            for lane in range(0, depth, 128):
                span = (pl.ds(row, 8), pl.ds(lane, 128))
                entries = [None] * 24
                for comp in range(3):
                    for z in (0, 1):
                        for y in (0, 1):
                            near = sums[(i % 3, 4 * comp + 2 * z + y) + span]
                            far = sums[((i + 1) % 3, 4 * comp + 2 * z + y) + span]
                            entries[3 * (2 * y + 4 * z) + comp] = near + far
                            entries[3 * (2 * y + 4 * z + 1) + comp] = far - near
                stiff, inert = element_energies(entries, squares, products)
                result = fields[(0, i) + span] * stiff - (value * fields[(2, i) + span]) * inert
                z_out[(mode * count + i,) + span] = result

    def one_mode(mode, carry):
        value = eig[core * (group // 3) + mode]
        transform(mode, 0)
        transform(mode, 1)
        for i in range(count):
            if i + 2 <= count:
                transform(mode, i + 2)
            energies(mode, value, i)
        return carry

    lax.fori_loop(0, group // 3, one_mode, 0)


class Layers:
    def __init__(self, *parts):
        self.where = {}
        for low, count, ref, offset, stride in parts:
            for i in range(count):
                self.where[low + i] = (ref, offset + i, stride)

    def __call__(self, mode, x):
        ref, offset, stride = self.where[x]
        return ref[mode * stride + offset]


def krylov_step(place, layers, modes, mass, zeroth, first_in, second_in, first_out, second_out, plan, moments, scratch):
    first, last = place[1], place[2]
    ones, twos, in_0, in_1, in_3, inner, ahead_of = plan
    width, depth = moments.shape[2], None
    inverse, count_of = scratch
    shape = inverse.shape[1:]
    width, depth = shape
    missing = missing_plane(shape)
    slot = {x: i for i, x in enumerate(sorted(set(ones) | set(twos) | set(in_0)))}
    for x, i in slot.items():
        count = neighbour_count(missing, x, layers, first, last)
        count_of[i] = count
        value = 1.0 / (mass(0, x) + RADIUS_SQ * count)
        if x < 0:
            value = value * (1.0 - scalar(first))
        if x >= layers:
            value = value * (1.0 - scalar(last))
        inverse[i] = value

    def apply(field, mode, x):
        here = field(mode, x)
        beside = field(mode, x - 1) + field(mode, x + 1)
        beside += shifted(here, 1, 1) + shifted(here, -1, 1)
        beside += shifted(here, 1, 0) + shifted(here, -1, 0)
        return mass(0, x) * here + RADIUS_SQ * (count_of[slot[x]] * here - beside)

    def fold(value):
        total = None
        for row in range(0, width, 8):
            for lane in range(0, depth, 128):
                piece = value[row : row + 8, lane : lane + 128]
                total = piece if total is None else total + piece
        return total

    row = lax.broadcasted_iota(jnp.int32, shape, 0)
    lane = lax.broadcasted_iota(jnp.int32, shape, 1)

    def one_mode(mode, carry):
        sums = [None] * 6

        def add(k, value):
            sums[k] = fold(value) if sums[k] is None else sums[k] + fold(value)

        for x in in_0:
            here = zeroth(mode, x)
            add(0, here * ((mass(0, x) + RADIUS_SQ * count_of[slot[x]]) * here))
        for x in ones:
            image = apply(zeroth, mode, x)
            one = image * inverse[slot[x]]
            first_out[mode * len(ones) + x - ones[0]] = one
            if x in in_1:
                add(1, zeroth(mode, x) * image)
                add(2, one * image)
        for x in twos:
            image = apply(first_in, mode, x)
            two = image * inverse[slot[x]]
            second_out[mode * len(twos) + x - twos[0]] = two
            if x in in_3:
                add(3, first_in(mode, x) * image)
                add(4, two * image)
        for x in inner:
            here = second_in(mode, x)
            add(5, mass(0, x) * here * here)
            aside = jnp.where(row == width - 1, 0.0, pltpu.roll(here, width - 1, 0) - here)
            above = jnp.where(lane == depth - 1, 0.0, pltpu.roll(here, depth - 1, 1) - here)
            add(5, RADIUS_SQ * (aside * aside + above * above))
        for x in ahead_of:
            edge = second_in(mode, x + 1) - second_in(mode, x)
            if x == layers - 1:
                edge = edge * (1.0 - scalar(last))
            add(5, RADIUS_SQ * (edge * edge))
        for k in range(6):
            if sums[k] is not None:
                moments[mode * 6 + k] = moments[mode * 6 + k] + sums[k]
        return carry

    lax.fori_loop(0, modes, one_mode, 0)


def send_halves(target, core, half, modes, fields):
    _, other = halves(core, half)
    total = target.shape[0] // modes

    def one_mode(mode, carry):
        for i, (field, x) in enumerate(fields):
            ref, offset, stride = field.where[x]
            target[mode * total + i] = ref[mode * stride + offset, pl.ds(other, half), :]
        return carry

    lax.fori_loop(0, modes, one_mode, 0)


def plans(layers):
    inner_ones, inner_twos = list(range(1, layers - 1)), list(range(2, layers - 2))
    inner = (inner_ones, inner_twos, list(range(layers)), inner_ones, inner_twos, inner_twos, inner_twos[:-1])
    right_ones, right_twos = [layers - 1, layers, layers + 1], [layers - 2, layers - 1, layers]
    right = (right_ones, right_twos, [], [layers - 1], right_twos[:2], right_twos[:2], [layers - 3] + right_twos[:2])
    left = ([-1, 0], [0, 1], [], [0], [0, 1], [0, 1], [0, 1])
    return inner, right, left


def inner_kernel(modes, layers, cuts, place, za, zb, zc, ma, mb, mc, ones, twos, send, moments, inverse, counts):
    plan = plans(layers)[0]
    zeroth, mass = z0_layers(cuts, layers, za, zb, zc), mass_layers(cuts, layers, ma, mb, mc)
    first = Layers((1, layers - 2, ones, 0, layers - 2))
    second = Layers((2, layers - 4, twos, 0, layers - 4))
    moments[...] = jnp.zeros(moments.shape, jnp.float32)
    krylov_step(place, layers, modes, mass, zeroth, first, second, ones, twos, plan, moments, (inverse, counts))
    fields = [(zeroth, x) for x in range(layers)] + [(first, x) for x in plan[0]] + [(second, x) for x in plan[1]]
    send_halves(send, place[0], za.shape[1] // 2, modes, fields)


def z0_layers(cuts, layers, za, zb, zc):
    a, b = cuts
    return Layers((0, a, za, 0, a), (a, b - a, zb, 0, b - a), (b, layers - b, zc, 0, layers - b))


def mass_layers(cuts, layers, ma, mb, mc):
    a, b = cuts
    return Layers((0, a, ma, 0, 0), (a, b - a, mb, 0, 0), (b, layers - b, mc, 0, 0))


def right_kernel(modes, layers, cuts, place, zc, mc, down, ghost_mass, ones_in, twos_in, moments_in,
                 ones, twos, send, moments, inverse, counts):
    plan = plans(layers)[1]
    tail = layers - cuts[1]
    zeroth = Layers((cuts[1], tail, zc, 0, tail), (layers, DOWN, down, 0, DOWN))
    mass = Layers((cuts[1], tail, mc, 0, 0), (layers, 2, ghost_mass, 0, 0))
    first = Layers((1, layers - 2, ones_in, 0, layers - 2), (layers - 1, 3, ones, 0, 3))
    second = Layers((2, layers - 4, twos_in, 0, layers - 4), (layers - 2, 3, twos, 0, 3))
    moments[...] = moments_in[...]
    krylov_step(place, layers, modes, mass, zeroth, first, second, ones, twos, plan, moments, (inverse, counts))
    fields = [(first, layers - 1), (second, layers - 2), (second, layers - 1)]
    send_halves(send, place[0], zc.shape[1] // 2, modes, fields)


def left_kernel(modes, layers, cuts, place, za, ma, up, ones_in, twos_in, moments_in,
                ones, twos, send, parts, inverse, counts, moments):
    plan = plans(layers)[2]
    zeroth = Layers((-UP, UP, up, 0, UP), (0, cuts[0], za, 0, cuts[0]))
    mass = Layers((-1, 1, up, UP * modes, 0), (0, cuts[0], ma, 0, 0))
    first = Layers((-1, 2, ones, 0, 2), (1, layers - 2, ones_in, 0, layers - 2))
    second = Layers((0, 2, twos, 0, 2), (2, layers - 4, twos_in, 0, layers - 4))
    moments[...] = moments_in[...]
    krylov_step(place, layers, modes, mass, zeroth, first, second, ones, twos, plan, moments, (inverse, counts))
    fields = [(first, 0), (second, 0), (second, 1)]
    send_halves(send, place[0], za.shape[1] // 2, modes, fields)
    row = lax.broadcasted_iota(jnp.int32, (8, 128), 0)
    lane = lax.broadcasted_iota(jnp.int32, (8, 128), 1)
    block = jnp.zeros((8, 128), jnp.float32)
    for mode in range(modes):
        for k in range(6):
            line = jnp.sum(moments[mode * 6 + k], axis=0, keepdims=True)
            total = jnp.sum(line, axis=1, keepdims=True)
            block = jnp.where((row == mode) & (lane == k), total, block)
    for i in range(parts.shape[0]):
        parts[i] = block


def combine_kernel(modes, layers, cuts, place, parts, za, zb, zc, ones_in, twos_in, ones_right, twos_right,
                   ones_left, twos_left, swap, swap_right, swap_left, out):
    core = place[0]
    half, depth = out.shape[2:]
    mine, _ = halves(core, half)
    shape = (8, 128)
    lane = lax.broadcasted_iota(jnp.int32, shape, 1)
    factors = []
    for c in (0, 1):
        block = parts[c]
        for i in range(2 + c, parts.shape[0], 2):
            block = block + parts[i]
        m = [jnp.sum(jnp.where(lane == k, block, 0.0), axis=1, keepdims=True) for k in range(6)]
        one, two = m[2] / m[1], m[3] / m[1]
        pivot = m[3] - one * m[2]
        cross = m[4] - two * m[2]
        slope = cross / pivot
        rest = m[5] - two * m[3] - slope * cross
        right_1 = m[1] - one * m[0]
        right_2 = m[2] - two * m[0] - slope * right_1
        c2 = right_2 / rest
        c1 = (right_1 - cross * c2) / pivot
        c0 = (m[0] - m[2] * c1 - m[3] * c2) / m[1]
        factors.append([jnp.broadcast_to(c, (8, depth)) for c in (c0, c1, c2)])

    zeroth = z0_layers(cuts, layers, za, zb, zc)
    first = Layers((0, 1, ones_left, 1, 2), (1, layers - 2, ones_in, 0, layers - 2), (layers - 1, 1, ones_right, 0, 3))
    second = Layers((0, 2, twos_left, 0, 2), (2, layers - 4, twos_in, 0, layers - 4), (layers - 2, 2, twos_right, 0, 3))
    total = swap.shape[0] // modes
    theirs = [
        Layers((0, layers, swap, 0, total)),
        Layers((0, 1, swap_left, 0, 3), (1, layers - 2, swap, layers, total), (layers - 1, 1, swap_right, 0, 3)),
        Layers((0, 2, swap_left, 1, 3), (2, layers - 4, swap, 2 * layers - 2, total), (layers - 2, 2, swap_right, 1, 3)),
    ]

    for slot in (0, 1):
        for mode in range(modes):
            target = slot * modes + mode
            a, b, c = (f[mode : mode + 1] for f in factors[slot])

            @pl.when(core == slot)
            def _():
                for x in range(layers):
                    planes = []
                    for field in (zeroth, first, second):
                        ref, offset, stride = field.where[x]
                        planes.append(ref[mode * stride + offset, pl.ds(mine, half), :])
                    out[target, x] = a * planes[0] + b * planes[1] + c * planes[2]

            @pl.when(core != slot)
            def _():
                for x in range(layers):
                    planes = [field(mode, x) for field in theirs]
                    out[target, x] = a * planes[0] + b * planes[1] + c * planes[2]


def local(mode_shapes, eigenvalues, density, filter_mass, passive):
    f32 = jnp.float32
    layers, half, depth = density.shape
    group = mode_shapes.shape[0] // 2
    modes = group // 3
    width = 2 * half
    core, at = lax.axis_index("gy"), lax.axis_index("gx")
    count = lax.axis_size("gx")
    place = jnp.stack([core, (at == 0).astype(jnp.int32), (at == count - 1).astype(jnp.int32)]).astype(jnp.int32)
    across = [(0, 1), (1, 0)]
    straight = [(2 * i + c, 2 * i - 2 + c) for i in range(1, count) for c in (0, 1)]
    crossed = [(2 * i + c, 2 * i - 1 - c) for i in range(1, count) for c in (0, 1)]
    both = ("gx", "gy")
    smem = pl.BlockSpec(memory_space=pltpu.SMEM)
    vmem = pl.BlockSpec(memory_space=pltpu.VMEM)
    anywhere = pl.BlockSpec(memory_space=pl.ANY)

    def planes(n, rows=width):
        return jax.ShapeDtypeStruct((n, rows, depth), f32)

    def kernel(name, body, outs, in_specs, scratch, limit, work):
        return pl.pallas_call(
            body,
            out_shape=outs,
            in_specs=in_specs,
            out_specs=jax.tree.map(lambda _: vmem, outs),
            scratch_shapes=scratch,
            compiler_params=pltpu.CompilerParams(vmem_limit_bytes=limit * 2**20),
            cost_estimate=pl.CostEstimate(flops=work * 2**20, bytes_accessed=2**20, transcendentals=0),
            name=name,
        )

    first_node, first_cross, swap, field = kernel(
        "pack",
        pack_kernel,
        (planes(group + 2, half), planes(group + 2, half), planes((group + 3) * layers, half), planes(3 * layers, half)),
        [smem, anywhere, vmem, vmem, vmem],
        [pltpu.SemaphoreType.DMA((2 + group,))],
        8,
        1,
    )(place, mode_shapes, density, filter_mass, passive)
    swap = lax.ppermute(swap, "gy", across)
    halo = lax.ppermute(first_node, both, straight)
    halo_swap = lax.ppermute(first_cross, both, crossed)

    cuts = (DOWN, layers - UP)

    def energies(name, low, high, *extra):
        end = high == layers
        n = high - low
        outs = (planes(modes * n + end), planes(n))
        return kernel(
            name,
            partial(energy_kernel, low, high, end),
            outs + (planes(2),) if end else outs,
            [smem, smem] + [anywhere] * (3 + len(extra)),
            [
                pltpu.VMEM((group, n + 1, width, depth), f32),
                pltpu.VMEM((3, n, width, depth), f32),
                pltpu.VMEM((3, 12, width, depth), f32),
                pltpu.SemaphoreType.DMA((group + 11,)),
            ],
            12,
            n * 200,
        )(place, eigenvalues, mode_shapes, swap, field, *extra)

    za, ma = energies("energies_first", 0, cuts[0], eigenvalues)
    down = lax.ppermute(za, "gx", [(i, i - 1) for i in range(1, count)])
    zb, mb = energies("energies_inner", cuts[0], cuts[1], ma)
    zc, mc, ghost_mass = energies("energies_last", cuts[1], layers, halo, halo_swap, mb)
    up = lax.ppermute(zc, "gx", [(i, i + 1) for i in range(count - 1)])

    tables = [pltpu.VMEM((layers, width, depth), f32)] * 2
    sums = jax.ShapeDtypeStruct((6 * modes, 8, 128), f32)
    ones_in, twos_in, send, moments = kernel(
        "krylov_inner",
        partial(inner_kernel, modes, layers, cuts),
        (planes(modes * (layers - 2)), planes(modes * (layers - 4)), planes(modes * (3 * layers - 6), half), sums),
        [smem] + [vmem] * 6,
        tables,
        12,
        400,
    )(place, za, zb, zc, ma, mb, mc)
    swap_in = lax.ppermute(send, "gy", across)
    ones_right, twos_right, send, moments = kernel(
        "krylov_right",
        partial(right_kernel, modes, layers, cuts),
        (planes(3 * modes), planes(3 * modes), planes(3 * modes, half), sums),
        [smem] + [vmem] * 7,
        tables,
        12,
        200,
    )(place, zc, mc, down, ghost_mass, ones_in, twos_in, moments)
    swap_right = lax.ppermute(send, "gy", across)
    ones_left, twos_left, send, parts = kernel(
        "krylov_left",
        partial(left_kernel, modes, layers, cuts),
        (planes(2 * modes), planes(2 * modes), planes(3 * modes, half), jax.ShapeDtypeStruct((2 * count, 8, 128), f32)),
        [smem] + [vmem] * 6,
        tables + [pltpu.VMEM((6 * modes, 8, 128), f32)],
        12,
        200,
    )(place, za, ma, up, ones_in, twos_in, moments)
    swap_left = lax.ppermute(send, "gy", across)
    parts = lax.all_to_all(parts, both, 0, 0, tiled=True)

    return kernel(
        "combine",
        partial(combine_kernel, modes, layers, cuts),
        jax.ShapeDtypeStruct((2 * modes, layers, half, depth), f32),
        [smem] + [vmem] * 13,
        [],
        12,
        100,
    )(place, parts, za, zb, zc, ones_in, twos_in, ones_right, twos_right, ones_left, twos_left, swap_in, swap_right, swap_left)


def solution(mesh):
    in_specs = (
        P("grp", "gx", "gy", None),
        P("grp"),
        P(("grp", "gx"), "gy", None),
        P(("grp", "gx"), "gy", None),
        P(("grp", "gx"), "gy", None),
    )
    out_specs = P("grp", "gx", "gy", None)
    return jax.shard_map(local, mesh=mesh, in_specs=in_specs, out_specs=out_specs, check_vma=False)
```

```python
import math
from functools import partial

import jax
import jax.numpy as jnp
import numpy as np
from jax import lax
from jax.experimental import pallas as pl
from jax.experimental.pallas import tpu as pltpu
from jax.sharding import PartitionSpec as P

ITERS = 3
RMIN = 4
RADIUS_SQ = RMIN * RMIN / 12.0
DOWN = 3
UP = 2


void_floor = 0.001


def element_table():
    poisson = 0.3
    lame_first = poisson / ((1.0 + poisson) * (1.0 - 2.0 * poisson))
    shear_mod = 1.0 / (2.0 * (1.0 + poisson))
    elastic = np.zeros((6, 6))
    elastic[:3, :3] = lame_first
    for entry in range(3):
        elastic[entry, entry] += 2.0 * shear_mod
        elastic[entry + 3, entry + 3] = shear_mod
    offset = 1.0 / math.sqrt(3.0)
    gauss_points = [(1.0 - offset) / 2.0, (1.0 + offset) / 2.0]
    stiffness = np.zeros((24, 24))
    inertia = np.zeros((24, 24))
    for point_x in gauss_points:
        for point_y in gauss_points:
            for point_z in gauss_points:
                coords = [point_x, point_y, point_z]
                values = np.zeros(8)
                gradient = np.zeros((8, 3))
                for corner in range(8):
                    corner_bits = [corner % 2, corner // 2 % 2, corner // 4]
                    factors = [
                        coords[dimen] if corner_bits[dimen] else 1.0 - coords[dimen]
                        for dimen in range(3)
                    ]
                    sign_list = [1.0 if corner_bits[dimen] else -1.0 for dimen in range(3)]
                    values[corner] = factors[0] * factors[1] * factors[2]
                    for dimen in range(3):
                        others = [
                            factors[other_dim] for other_dim in range(3) if other_dim != dimen
                        ]
                        gradient[corner, dimen] = sign_list[dimen] * others[0] * others[1]
                strain = np.zeros((6, 24))
                for corner in range(8):
                    column = 3 * corner
                    grad_x, grad_y, grad_z = gradient[corner]
                    strain[0, column] = grad_x
                    strain[1, column + 1] = grad_y
                    strain[2, column + 2] = grad_z
                    strain[3, column] = grad_y
                    strain[3, column + 1] = grad_x
                    strain[4, column + 1] = grad_z
                    strain[4, column + 2] = grad_y
                    strain[5, column] = grad_z
                    strain[5, column + 2] = grad_x
                stiffness += 0.125 * strain.T @ elastic @ strain
                shape_matrix = np.kron(values[None, :], np.eye(3))
                inertia += 0.125 * shape_matrix.T @ shape_matrix
    return stiffness, inertia


def energy_classes():
    stiffness, inertia = element_table()
    pair = np.array([[1.0, 1.0], [-1.0, 1.0]])
    basis = np.kron(np.kron(np.kron(pair, pair), pair), np.eye(3))
    stiffness = basis @ stiffness @ basis.T / 64.0
    inertia = basis @ inertia @ basis.T / 64.0
    squares, products = {}, {}
    for i in range(24):
        key = (round(stiffness[i, i], 9), round(inertia[i, i], 9))
        squares.setdefault(key, []).append(i)
        for j in range(i + 1, 24):
            if abs(stiffness[i, j]) > 1e-9:
                products.setdefault(round(stiffness[i, j], 9), []).append((i, j))
    squares = [
        (float(stiffness[v[0], v[0]]) if abs(k[0]) > 1e-9 else 0.0, float(inertia[v[0], v[0]]), v)
        for k, v in squares.items()
    ]
    products = [(2.0 * float(stiffness[v[0]]), v) for v in products.values()]
    return squares, products


def element_energies(entries, squares, products):
    stiff, inert = None, {}
    for weight, mass, members in squares:
        total = entries[members[0]] * entries[members[0]]
        for i in members[1:]:
            total = total + entries[i] * entries[i]
        if weight:
            stiff = total * weight if stiff is None else stiff + total * weight
        inert[mass] = inert[mass] + total if mass in inert else total
    for weight, members in products:
        total = entries[members[0][0]] * entries[members[0][1]]
        for i, j in members[1:]:
            total = total + entries[i] * entries[j]
        stiff = stiff + weight * total
    return stiff, sum(total * mass for mass, total in inert.items())


def shifted(value, step, dim):
    size = value.shape[dim]
    index = lax.broadcasted_iota(jnp.int32, value.shape, dim)
    edge = size - 1 if step > 0 else 0
    return jnp.where(index == edge, 0.0, pltpu.roll(value, (-step) % size, dim))


def missing_plane(shape):
    count = jnp.zeros(shape, jnp.float32)
    for dim in (0, 1):
        index = lax.broadcasted_iota(jnp.int32, shape, dim)
        count += (index == 0).astype(jnp.float32) + (index == shape[dim] - 1).astype(jnp.float32)
    return count


def scalar(flag):
    return jnp.where(flag, 1.0, 0.0).astype(jnp.float32)


def neighbour_count(missing, x, layers, first, last):
    count = 6.0 - missing
    if x == 0:
        count -= scalar(first)
    if x == layers - 1:
        count -= scalar(last)
    return count


def halves(core, half):
    return pl.multiple_of(core * half, half), pl.multiple_of((1 - core) * half, half)


def pack_kernel(place, modes, density, mass, passive, straight, crossed, swap, field, floats, flags, sems):
    group, layers = modes.shape[0] // 2, modes.shape[1]
    core = place[0]
    mine, theirs = core * group, (1 - core) * group
    copies = [
        pltpu.make_async_copy(modes.at[pl.ds(mine, group), 0], straight.at[pl.ds(0, group)], sems.at[0]),
        pltpu.make_async_copy(modes.at[pl.ds(theirs, group), 0], crossed.at[pl.ds(0, group)], sems.at[1]),
    ]
    copies += [
        pltpu.make_async_copy(modes.at[theirs + i], swap.at[pl.ds(i * layers, layers)], sems.at[2 + i])
        for i in range(group)
    ]
    inputs = [
        pltpu.make_async_copy(source, target, sems.at[2 + group + i])
        for i, (source, target) in enumerate(((density, floats.at[0]), (mass, floats.at[1]), (passive, flags)))
    ]
    for copy in inputs + copies:
        copy.start()
    for copy in inputs:
        copy.wait()
    base = group * layers
    for x in range(layers):
        rho, weight = floats[0, x], floats[1, x]
        design = (1 - flags[x]).astype(jnp.float32)
        slope = 3.0 * (1.0 - void_floor) * rho * rho * design
        for k, value in enumerate((slope, weight, design)):
            swap[base + k * layers + x] = value
            field[k * layers + x] = value
        if x < 2:
            straight[group + x] = weight
            crossed[group + x] = weight
    for copy in copies:
        copy.wait()


def energy_kernel(low, high, end, *refs):
    place, eig, modes, swap, field = refs[:5]
    refs = refs[5:]
    if end:
        (halo, halo_swap, _, z_out, mass_out, ghost_mass), refs = refs[:6], refs[6:]
    else:
        *_, z_out, mass_out = refs[:-4]
        refs = refs[-4:]
    nodes, fields, sums, sems = refs
    layers, half, depth = modes.shape[1:]
    group = modes.shape[0] // 2
    width, count = 2 * half, high - low
    core, first, last = place[0], place[1], place[2]
    mine, other = halves(core, half)
    start = core * group
    copies = []

    def move(source, target):
        copy = pltpu.make_async_copy(source, target, sems.at[len(copies)])
        copy.start()
        copies.append(copy)

    base = group * layers
    for k in range(3):
        move(field.at[pl.ds(k * layers + low, count)], fields.at[k, :, pl.ds(mine, half), :])
        move(swap.at[pl.ds(base + k * layers + low, count)], fields.at[k, :, pl.ds(other, half), :])
    held = count if end else count + 1
    move(modes.at[pl.ds(start, group), pl.ds(low, held)], nodes.at[:, pl.ds(0, held), pl.ds(mine, half), :])
    for i in range(group):
        move(swap.at[pl.ds(i * layers + low, held)], nodes.at[i, pl.ds(0, held), pl.ds(other, half), :])
    if end:
        move(halo.at[pl.ds(0, group)], nodes.at[:, count, pl.ds(mine, half), :])
        move(halo_swap.at[pl.ds(0, group)], nodes.at[:, count, pl.ds(other, half), :])
        move(halo.at[pl.ds(group, 2)], ghost_mass.at[:, pl.ds(mine, half), :])
        move(halo_swap.at[pl.ds(group, 2)], ghost_mass.at[:, pl.ds(other, half), :])
    for copy in copies:
        copy.wait()

    squares, products = energy_classes()
    missing = missing_plane((width, depth))
    for i in range(count):
        mass = fields[1, i]
        mass_out[i] = mass
        inverse = 1.0 / (mass + RADIUS_SQ * neighbour_count(missing, low + i, layers, first, last))
        fields[0, i] = fields[0, i] * inverse
        fields[2, i] = fields[2, i] * inverse
    if end:
        z_out[z_out.shape[0] - 1] = fields[1, count - 1]

    def transform(mode, i):
        for comp in range(3):
            here = nodes[3 * mode + comp, i]
            above = shifted(here, 1, 1)
            for z, value in ((0, here + above), (1, above - here)):
                beside = shifted(value, 1, 0)
                sums[i % 3, 4 * comp + 2 * z] = value + beside
                sums[i % 3, 4 * comp + 2 * z + 1] = beside - value

    def energies(mode, value, i):
        for row in range(0, width, 8):
            for lane in range(0, depth, 128):
                span = (pl.ds(row, 8), pl.ds(lane, 128))
                entries = [None] * 24
                for comp in range(3):
                    for z in (0, 1):
                        for y in (0, 1):
                            near = sums[(i % 3, 4 * comp + 2 * z + y) + span]
                            far = sums[((i + 1) % 3, 4 * comp + 2 * z + y) + span]
                            entries[3 * (2 * y + 4 * z) + comp] = near + far
                            entries[3 * (2 * y + 4 * z + 1) + comp] = far - near
                stiff, inert = element_energies(entries, squares, products)
                result = fields[(0, i) + span] * stiff - (value * fields[(2, i) + span]) * inert
                z_out[(mode * count + i,) + span] = result

    def one_mode(mode, carry):
        value = eig[core * (group // 3) + mode]
        transform(mode, 0)
        transform(mode, 1)
        for i in range(count):
            if i + 2 <= count:
                transform(mode, i + 2)
            energies(mode, value, i)
        return carry

    lax.fori_loop(0, group // 3, one_mode, 0)


class Layers:
    def __init__(self, *parts):
        self.where = {}
        for low, count, ref, offset, stride in parts:
            for i in range(count):
                self.where[low + i] = (ref, offset + i, stride)

    def __call__(self, mode, x):
        ref, offset, stride = self.where[x]
        return ref[mode * stride + offset]


def krylov_step(place, layers, modes, mass, zeroth, first_in, second_in, first_out, second_out, plan, moments, scratch):
    first, last = place[1], place[2]
    ones, twos, in_0, in_1, in_3, inner, ahead_of = plan
    width, depth = moments.shape[2], None
    inverse, count_of = scratch
    shape = inverse.shape[1:]
    width, depth = shape
    missing = missing_plane(shape)
    slot = {x: i for i, x in enumerate(sorted(set(ones) | set(twos) | set(in_0)))}
    for x, i in slot.items():
        count = neighbour_count(missing, x, layers, first, last)
        count_of[i] = count
        value = 1.0 / (mass(0, x) + RADIUS_SQ * count)
        if x < 0:
            value = value * (1.0 - scalar(first))
        if x >= layers:
            value = value * (1.0 - scalar(last))
        inverse[i] = value

    def apply(field, mode, x):
        here = field(mode, x)
        beside = field(mode, x - 1) + field(mode, x + 1)
        beside += shifted(here, 1, 1) + shifted(here, -1, 1)
        beside += shifted(here, 1, 0) + shifted(here, -1, 0)
        return mass(0, x) * here + RADIUS_SQ * (count_of[slot[x]] * here - beside)

    def fold(value):
        total = None
        for row in range(0, width, 8):
            for lane in range(0, depth, 128):
                piece = value[row : row + 8, lane : lane + 128]
                total = piece if total is None else total + piece
        return total

    row = lax.broadcasted_iota(jnp.int32, shape, 0)
    lane = lax.broadcasted_iota(jnp.int32, shape, 1)

    def one_mode(mode, carry):
        sums = [None] * 6

        def add(k, value):
            sums[k] = fold(value) if sums[k] is None else sums[k] + fold(value)

        for x in in_0:
            here = zeroth(mode, x)
            add(0, here * ((mass(0, x) + RADIUS_SQ * count_of[slot[x]]) * here))
        for x in ones:
            image = apply(zeroth, mode, x)
            one = image * inverse[slot[x]]
            first_out[mode * len(ones) + x - ones[0]] = one
            if x in in_1:
                add(1, zeroth(mode, x) * image)
                add(2, one * image)
        for x in twos:
            image = apply(first_in, mode, x)
            two = image * inverse[slot[x]]
            second_out[mode * len(twos) + x - twos[0]] = two
            if x in in_3:
                add(3, first_in(mode, x) * image)
                add(4, two * image)
        for x in inner:
            here = second_in(mode, x)
            add(5, mass(0, x) * here * here)
            aside = jnp.where(row == width - 1, 0.0, pltpu.roll(here, width - 1, 0) - here)
            above = jnp.where(lane == depth - 1, 0.0, pltpu.roll(here, depth - 1, 1) - here)
            add(5, RADIUS_SQ * (aside * aside + above * above))
        for x in ahead_of:
            edge = second_in(mode, x + 1) - second_in(mode, x)
            if x == layers - 1:
                edge = edge * (1.0 - scalar(last))
            add(5, RADIUS_SQ * (edge * edge))
        for k in range(6):
            if sums[k] is not None:
                moments[mode * 6 + k] = moments[mode * 6 + k] + sums[k]
        return carry

    lax.fori_loop(0, modes, one_mode, 0)


def send_halves(target, core, half, modes, parts, sems):
    _, other = halves(core, half)
    total = target.shape[0] // modes
    copies = []
    for mode in range(modes):
        at = mode * total
        for ref, offset, stride, count in parts:
            source = ref.at[pl.ds(mode * stride + offset, count), pl.ds(other, half), :]
            copies.append(pltpu.make_async_copy(source, target.at[pl.ds(at, count)], sems.at[len(copies)]))
            at += count
    for copy in copies:
        copy.start()
    return copies


def plans(layers):
    inner_ones, inner_twos = list(range(1, layers - 1)), list(range(2, layers - 2))
    inner = (inner_ones, inner_twos, list(range(layers)), inner_ones, inner_twos, inner_twos, inner_twos[:-1])
    right_ones, right_twos = [layers - 1, layers, layers + 1], [layers - 2, layers - 1, layers]
    right = (right_ones, right_twos, [], [layers - 1], right_twos[:2], right_twos[:2], [layers - 3] + right_twos[:2])
    left = ([-1, 0], [0, 1], [], [0], [0, 1], [0, 1], [0, 1])
    return inner, right, left


def inner_kernel(modes, layers, cuts, place, za, zb, zc, ma, mb, mc, ones, twos, moments, inverse, counts):
    plan = plans(layers)[0]
    zeroth, mass = z0_layers(cuts, layers, za, zb, zc), mass_layers(cuts, layers, ma, mb, mc)
    first = Layers((1, layers - 2, ones, 0, layers - 2))
    second = Layers((2, layers - 4, twos, 0, layers - 4))
    moments[...] = jnp.zeros(moments.shape, jnp.float32)
    krylov_step(place, layers, modes, mass, zeroth, first, second, ones, twos, plan, moments, (inverse, counts))


def z0_layers(cuts, layers, za, zb, zc):
    a, b = cuts
    return Layers((0, a, za, 0, a), (a, b - a, zb, 0, b - a), (b, layers - b, zc, 0, layers - b))


def mass_layers(cuts, layers, ma, mb, mc):
    a, b = cuts
    return Layers((0, a, ma, 0, 0), (a, b - a, mb, 0, 0), (b, layers - b, mc, 0, 0))


def right_kernel(modes, layers, cuts, place, zc, mc, down, ghost_mass, ones_in, twos_in, moments_in,
                 ones, twos, moments, inverse, counts):
    plan = plans(layers)[1]
    tail = layers - cuts[1]
    zeroth = Layers((cuts[1], tail, zc, 0, tail), (layers, DOWN, down, 0, DOWN))
    mass = Layers((cuts[1], tail, mc, 0, 0), (layers, 2, ghost_mass, 0, 0))
    first = Layers((1, layers - 2, ones_in, 0, layers - 2), (layers - 1, 3, ones, 0, 3))
    second = Layers((2, layers - 4, twos_in, 0, layers - 4), (layers - 2, 3, twos, 0, 3))
    moments[...] = moments_in[...]
    krylov_step(place, layers, modes, mass, zeroth, first, second, ones, twos, plan, moments, (inverse, counts))


def left_kernel(modes, layers, cuts, place, za, zb, zc, ma, up, ones_in, twos_in, ones_right, twos_right, moments_in,
                ones, twos, send, parts, inverse, counts, moments, sems):
    plan = plans(layers)[2]
    half = za.shape[1] // 2
    tail = layers - cuts[1]
    pieces = [(za, 0, cuts[0], cuts[0]), (zb, 0, cuts[1] - cuts[0], cuts[1] - cuts[0]), (zc, 0, tail, tail)]
    pieces += [(ones_in, 0, layers - 2, layers - 2), (ones_right, 0, 3, 1)]
    pieces += [(twos_in, 0, layers - 4, layers - 4), (twos_right, 0, 3, 2)]
    copies = send_halves(send, place[0], half, modes, pieces, sems)
    zeroth = Layers((-UP, UP, up, 0, UP), (0, cuts[0], za, 0, cuts[0]))
    mass = Layers((-1, 1, up, UP * modes, 0), (0, cuts[0], ma, 0, 0))
    first = Layers((-1, 2, ones, 0, 2), (1, layers - 2, ones_in, 0, layers - 2))
    second = Layers((0, 2, twos, 0, 2), (2, layers - 4, twos_in, 0, layers - 4))
    moments[...] = moments_in[...]
    krylov_step(place, layers, modes, mass, zeroth, first, second, ones, twos, plan, moments, (inverse, counts))
    _, other = halves(place[0], half)
    total = send.shape[0] // modes
    for mode in range(modes):
        at = (mode + 1) * total - 3
        send[at] = ones[2 * mode + 1, pl.ds(other, half), :]
        send[at + 1] = twos[2 * mode, pl.ds(other, half), :]
        send[at + 2] = twos[2 * mode + 1, pl.ds(other, half), :]
    row = lax.broadcasted_iota(jnp.int32, (8, 128), 0)
    lane = lax.broadcasted_iota(jnp.int32, (8, 128), 1)
    block = jnp.zeros((8, 128), jnp.float32)
    for mode in range(modes):
        for k in range(6):
            line = jnp.sum(moments[mode * 6 + k], axis=0, keepdims=True)
            total = jnp.sum(line, axis=1, keepdims=True)
            block = jnp.where((row == mode) & (lane == k), total, block)
    for i in range(parts.shape[0]):
        parts[i] = block
    for copy in copies:
        copy.wait()


def combine_kernel(modes, layers, cuts, place, parts, za, zb, zc, ones_in, twos_in, ones_right, twos_right,
                   ones_left, twos_left, swap, out):
    core = place[0]
    half, depth = out.shape[2:]
    mine, _ = halves(core, half)
    shape = (8, 128)
    lane = lax.broadcasted_iota(jnp.int32, shape, 1)
    factors = []
    for c in (0, 1):
        block = parts[c]
        for i in range(2 + c, parts.shape[0], 2):
            block = block + parts[i]
        m = [jnp.sum(jnp.where(lane == k, block, 0.0), axis=1, keepdims=True) for k in range(6)]
        one, two = m[2] / m[1], m[3] / m[1]
        pivot = m[3] - one * m[2]
        cross = m[4] - two * m[2]
        slope = cross / pivot
        rest = m[5] - two * m[3] - slope * cross
        right_1 = m[1] - one * m[0]
        right_2 = m[2] - two * m[0] - slope * right_1
        c2 = right_2 / rest
        c1 = (right_1 - cross * c2) / pivot
        c0 = (m[0] - m[2] * c1 - m[3] * c2) / m[1]
        factors.append([jnp.broadcast_to(c, (8, depth)) for c in (c0, c1, c2)])

    zeroth = z0_layers(cuts, layers, za, zb, zc)
    first = Layers((0, 1, ones_left, 1, 2), (1, layers - 2, ones_in, 0, layers - 2), (layers - 1, 1, ones_right, 0, 3))
    second = Layers((0, 2, twos_left, 0, 2), (2, layers - 4, twos_in, 0, layers - 4), (layers - 2, 2, twos_right, 0, 3))
    total = swap.shape[0] // modes
    theirs = [
        Layers((0, layers, swap, 0, total)),
        Layers((0, 1, swap, 3 * layers - 3, total), (1, layers - 1, swap, layers, total)),
        Layers((0, 2, swap, 3 * layers - 2, total), (2, layers - 2, swap, 2 * layers - 1, total)),
    ]

    for slot in (0, 1):
        for mode in range(modes):
            target = slot * modes + mode
            a, b, c = (f[mode : mode + 1] for f in factors[slot])

            @pl.when(core == slot)
            def _():
                for x in range(layers):
                    planes = []
                    for field in (zeroth, first, second):
                        ref, offset, stride = field.where[x]
                        planes.append(ref[mode * stride + offset, pl.ds(mine, half), :])
                    out[target, x] = a * planes[0] + b * planes[1] + c * planes[2]

            @pl.when(core != slot)
            def _():
                for x in range(layers):
                    planes = [field(mode, x) for field in theirs]
                    out[target, x] = a * planes[0] + b * planes[1] + c * planes[2]


def local(mode_shapes, eigenvalues, density, filter_mass, passive):
    f32 = jnp.float32
    layers, half, depth = density.shape
    group = mode_shapes.shape[0] // 2
    modes = group // 3
    width = 2 * half
    core, at = lax.axis_index("gy"), lax.axis_index("gx")
    count = lax.axis_size("gx")
    place = jnp.stack([core, (at == 0).astype(jnp.int32), (at == count - 1).astype(jnp.int32)]).astype(jnp.int32)
    across = [(0, 1), (1, 0)]
    straight = [(2 * i + c, 2 * i - 2 + c) for i in range(1, count) for c in (0, 1)]
    crossed = [(2 * i + c, 2 * i - 1 - c) for i in range(1, count) for c in (0, 1)]
    both = ("gx", "gy")
    smem = pl.BlockSpec(memory_space=pltpu.SMEM)
    vmem = pl.BlockSpec(memory_space=pltpu.VMEM)
    hbm = pl.BlockSpec(memory_space=pltpu.HBM)
    anywhere = pl.BlockSpec(memory_space=pl.ANY)

    def planes(n, rows=width):
        return jax.ShapeDtypeStruct((n, rows, depth), f32)

    def kernel(name, body, outs, in_specs, scratch, limit, work):
        return pl.pallas_call(
            body,
            out_shape=outs,
            in_specs=in_specs,
            out_specs=jax.tree.map(lambda _: vmem, outs),
            scratch_shapes=scratch,
            compiler_params=pltpu.CompilerParams(vmem_limit_bytes=limit * 2**20),
            cost_estimate=pl.CostEstimate(flops=work * 2**20, bytes_accessed=2**20, transcendentals=0),
            name=name,
        )

    first_node, first_cross, swap, field = kernel(
        "pack",
        pack_kernel,
        (planes(group + 2, half), planes(group + 2, half), planes((group + 3) * layers, half), planes(3 * layers, half)),
        [smem] + [hbm] * 4,
        [
            pltpu.VMEM((2, layers, half, depth), f32),
            pltpu.VMEM((layers, half, depth), jnp.int32),
            pltpu.SemaphoreType.DMA((5 + group,)),
        ],
        8,
        1,
    )(place, *(pltpu.with_memory_space_constraint(x, pltpu.HBM) for x in (mode_shapes, density, filter_mass, passive)))
    swap = lax.ppermute(swap, "gy", across)
    halo = lax.ppermute(first_node, both, straight)
    halo_swap = lax.ppermute(first_cross, both, crossed)

    cuts = (DOWN, layers - UP)

    def energies(name, low, high, *extra):
        end = high == layers
        n = high - low
        outs = (planes(modes * n + end), planes(n))
        return kernel(
            name,
            partial(energy_kernel, low, high, end),
            outs + (planes(2),) if end else outs,
            [smem, smem] + [anywhere] * (3 + len(extra)),
            [
                pltpu.VMEM((group, n + 1, width, depth), f32),
                pltpu.VMEM((3, n, width, depth), f32),
                pltpu.VMEM((3, 12, width, depth), f32),
                pltpu.SemaphoreType.DMA((group + 11,)),
            ],
            12,
            n * 200,
        )(place, eigenvalues, mode_shapes, swap, field, *extra)

    za, ma = energies("energies_first", 0, cuts[0])
    down = lax.ppermute(za, "gx", [(i, i - 1) for i in range(1, count)])
    zb, mb = energies("energies_inner", cuts[0], cuts[1], ma)
    zc, mc, ghost_mass = energies("energies_last", cuts[1], layers, halo, halo_swap, mb)
    up = lax.ppermute(zc, "gx", [(i, i + 1) for i in range(count - 1)])

    tables = [pltpu.VMEM((layers, width, depth), f32)] * 2
    sums = jax.ShapeDtypeStruct((6 * modes, 8, 128), f32)
    ones_in, twos_in, moments = kernel(
        "krylov_inner",
        partial(inner_kernel, modes, layers, cuts),
        (planes(modes * (layers - 2)), planes(modes * (layers - 4)), sums),
        [smem] + [vmem] * 6,
        tables,
        12,
        400,
    )(place, za, zb, zc, ma, mb, mc)
    ones_right, twos_right, moments = kernel(
        "krylov_right",
        partial(right_kernel, modes, layers, cuts),
        (planes(3 * modes), planes(3 * modes), sums),
        [smem] + [vmem] * 7,
        tables,
        12,
        200,
    )(place, zc, mc, down, ghost_mass, ones_in, twos_in, moments)
    ones_left, twos_left, send, parts = kernel(
        "krylov_left",
        partial(left_kernel, modes, layers, cuts),
        (
            planes(2 * modes),
            planes(2 * modes),
            planes(modes * 3 * layers, half),
            jax.ShapeDtypeStruct((2 * count, 8, 128), f32),
        ),
        [smem] + [vmem] * 10,
        tables + [pltpu.VMEM((6 * modes, 8, 128), f32), pltpu.SemaphoreType.DMA((7 * modes,))],
        12,
        200,
    )(place, za, zb, zc, ma, up, ones_in, twos_in, ones_right, twos_right, moments)
    swap_in = lax.ppermute(send, "gy", across)
    parts = lax.all_to_all(parts, both, 0, 0, tiled=True)

    return kernel(
        "combine",
        partial(combine_kernel, modes, layers, cuts),
        jax.ShapeDtypeStruct((2 * modes, layers, half, depth), f32),
        [smem] + [vmem] * 11,
        [],
        12,
        100,
    )(place, parts, za, zb, zc, ones_in, twos_in, ones_right, twos_right, ones_left, twos_left, swap_in)


def solution(mesh):
    in_specs = (
        P("grp", "gx", "gy", None),
        P("grp"),
        P(("grp", "gx"), "gy", None),
        P(("grp", "gx"), "gy", None),
        P(("grp", "gx"), "gy", None),
    )
    out_specs = P("grp", "gx", "gy", None)
    return jax.shard_map(local, mesh=mesh, in_specs=in_specs, out_specs=out_specs, check_vma=False)
```

```python
import math
from functools import partial

import jax
import jax.numpy as jnp
import numpy as np
from jax import lax
from jax.experimental import pallas as pl
from jax.experimental.pallas import tpu as pltpu
from jax.sharding import PartitionSpec as P

ITERS = 3
RMIN = 4
RADIUS_SQ = RMIN * RMIN / 12.0
DOWN = 3
UP = 2


void_floor = 0.001


def element_table():
    poisson = 0.3
    lame_first = poisson / ((1.0 + poisson) * (1.0 - 2.0 * poisson))
    shear_mod = 1.0 / (2.0 * (1.0 + poisson))
    elastic = np.zeros((6, 6))
    elastic[:3, :3] = lame_first
    for entry in range(3):
        elastic[entry, entry] += 2.0 * shear_mod
        elastic[entry + 3, entry + 3] = shear_mod
    offset = 1.0 / math.sqrt(3.0)
    gauss_points = [(1.0 - offset) / 2.0, (1.0 + offset) / 2.0]
    stiffness = np.zeros((24, 24))
    inertia = np.zeros((24, 24))
    for point_x in gauss_points:
        for point_y in gauss_points:
            for point_z in gauss_points:
                coords = [point_x, point_y, point_z]
                values = np.zeros(8)
                gradient = np.zeros((8, 3))
                for corner in range(8):
                    corner_bits = [corner % 2, corner // 2 % 2, corner // 4]
                    factors = [
                        coords[dimen] if corner_bits[dimen] else 1.0 - coords[dimen]
                        for dimen in range(3)
                    ]
                    sign_list = [1.0 if corner_bits[dimen] else -1.0 for dimen in range(3)]
                    values[corner] = factors[0] * factors[1] * factors[2]
                    for dimen in range(3):
                        others = [
                            factors[other_dim] for other_dim in range(3) if other_dim != dimen
                        ]
                        gradient[corner, dimen] = sign_list[dimen] * others[0] * others[1]
                strain = np.zeros((6, 24))
                for corner in range(8):
                    column = 3 * corner
                    grad_x, grad_y, grad_z = gradient[corner]
                    strain[0, column] = grad_x
                    strain[1, column + 1] = grad_y
                    strain[2, column + 2] = grad_z
                    strain[3, column] = grad_y
                    strain[3, column + 1] = grad_x
                    strain[4, column + 1] = grad_z
                    strain[4, column + 2] = grad_y
                    strain[5, column] = grad_z
                    strain[5, column + 2] = grad_x
                stiffness += 0.125 * strain.T @ elastic @ strain
                shape_matrix = np.kron(values[None, :], np.eye(3))
                inertia += 0.125 * shape_matrix.T @ shape_matrix
    return stiffness, inertia


def energy_classes():
    stiffness, inertia = element_table()
    pair = np.array([[1.0, 1.0], [-1.0, 1.0]])
    basis = np.kron(np.kron(np.kron(pair, pair), pair), np.eye(3))
    stiffness = basis @ stiffness @ basis.T / 64.0
    inertia = basis @ inertia @ basis.T / 64.0
    squares, products = {}, {}
    for i in range(24):
        key = (round(stiffness[i, i], 9), round(inertia[i, i], 9))
        squares.setdefault(key, []).append(i)
        for j in range(i + 1, 24):
            if abs(stiffness[i, j]) > 1e-9:
                products.setdefault(round(stiffness[i, j], 9), []).append((i, j))
    squares = [
        (float(stiffness[v[0], v[0]]) if abs(k[0]) > 1e-9 else 0.0, float(inertia[v[0], v[0]]), v)
        for k, v in squares.items()
    ]
    products = [(2.0 * float(stiffness[v[0]]), v) for v in products.values()]
    return squares, products


def element_energies(entries, squares, products):
    stiff, inert = None, {}
    for weight, mass, members in squares:
        total = entries[members[0]] * entries[members[0]]
        for i in members[1:]:
            total = total + entries[i] * entries[i]
        if weight:
            stiff = total * weight if stiff is None else stiff + total * weight
        inert[mass] = inert[mass] + total if mass in inert else total
    for weight, members in products:
        total = entries[members[0][0]] * entries[members[0][1]]
        for i, j in members[1:]:
            total = total + entries[i] * entries[j]
        stiff = stiff + weight * total
    return stiff, sum(total * mass for mass, total in inert.items())


def shifted(value, step, dim):
    size = value.shape[dim]
    index = lax.broadcasted_iota(jnp.int32, value.shape, dim)
    edge = size - 1 if step > 0 else 0
    return jnp.where(index == edge, 0.0, pltpu.roll(value, (-step) % size, dim))


def missing_plane(shape):
    count = jnp.zeros(shape, jnp.float32)
    for dim in (0, 1):
        index = lax.broadcasted_iota(jnp.int32, shape, dim)
        count += (index == 0).astype(jnp.float32) + (index == shape[dim] - 1).astype(jnp.float32)
    return count


def scalar(flag):
    return jnp.where(flag, 1.0, 0.0).astype(jnp.float32)


def neighbour_count(missing, x, layers, first, last):
    count = 6.0 - missing
    if x == 0:
        count -= scalar(first)
    if x == layers - 1:
        count -= scalar(last)
    return count


def halves(core, half):
    return pl.multiple_of(core * half, half), pl.multiple_of((1 - core) * half, half)


def pack_kernel(place, modes, density, mass, passive, straight, crossed, swap, field, floats, flags, sems):
    group, layers = modes.shape[0] // 2, modes.shape[1]
    core = place[0]
    mine, theirs = core * group, (1 - core) * group
    copies = [
        pltpu.make_async_copy(modes.at[pl.ds(mine, group), 0], straight.at[pl.ds(0, group)], sems.at[0]),
        pltpu.make_async_copy(modes.at[pl.ds(theirs, group), 0], crossed.at[pl.ds(0, group)], sems.at[1]),
    ]
    copies += [
        pltpu.make_async_copy(modes.at[theirs + i], swap.at[pl.ds(i * layers, layers)], sems.at[2 + i])
        for i in range(group)
    ]
    inputs = [
        pltpu.make_async_copy(source, target, sems.at[2 + group + i])
        for i, (source, target) in enumerate(((density, floats.at[0]), (mass, floats.at[1]), (passive, flags)))
    ]
    for copy in inputs + copies:
        copy.start()
    for copy in inputs:
        copy.wait()
    base = group * layers
    for x in range(layers):
        rho, weight = floats[0, x], floats[1, x]
        design = (1 - flags[x]).astype(jnp.float32)
        slope = 3.0 * (1.0 - void_floor) * rho * rho * design
        for k, value in enumerate((slope, weight, design)):
            swap[base + k * layers + x] = value
            field[k * layers + x] = value
        if x < 2:
            straight[group + x] = weight
            crossed[group + x] = weight
    for copy in copies:
        copy.wait()


def energy_kernel(low, high, end, *refs):
    place, eig, modes, swap, field = refs[:5]
    refs = refs[5:]
    if end:
        (halo, halo_swap, _, z_out, mass_out, ghost_mass), refs = refs[:6], refs[6:]
    else:
        *_, z_out, mass_out = refs[:-4]
        refs = refs[-4:]
    nodes, fields, sums, sems = refs
    layers, half, depth = modes.shape[1:]
    group = modes.shape[0] // 2
    width, count = 2 * half, high - low
    core, first, last = place[0], place[1], place[2]
    mine, other = halves(core, half)
    start = core * group
    copies = []

    def move(source, target):
        copy = pltpu.make_async_copy(source, target, sems.at[len(copies)])
        copy.start()
        copies.append(copy)

    base = group * layers
    for k in range(3):
        move(field.at[pl.ds(k * layers + low, count)], fields.at[k, :, pl.ds(mine, half), :])
        move(swap.at[pl.ds(base + k * layers + low, count)], fields.at[k, :, pl.ds(other, half), :])
    held = count if end else count + 1
    move(modes.at[pl.ds(start, group), pl.ds(low, held)], nodes.at[:, pl.ds(0, held), pl.ds(mine, half), :])
    for i in range(group):
        move(swap.at[pl.ds(i * layers + low, held)], nodes.at[i, pl.ds(0, held), pl.ds(other, half), :])
    if end:
        move(halo.at[pl.ds(0, group)], nodes.at[:, count, pl.ds(mine, half), :])
        move(halo_swap.at[pl.ds(0, group)], nodes.at[:, count, pl.ds(other, half), :])
        move(halo.at[pl.ds(group, 2)], ghost_mass.at[:, pl.ds(mine, half), :])
        move(halo_swap.at[pl.ds(group, 2)], ghost_mass.at[:, pl.ds(other, half), :])
    for copy in copies:
        copy.wait()

    squares, products = energy_classes()
    missing = missing_plane((width, depth))
    for i in range(count):
        mass = fields[1, i]
        mass_out[i] = mass
        inverse = 1.0 / (mass + RADIUS_SQ * neighbour_count(missing, low + i, layers, first, last))
        fields[0, i] = fields[0, i] * inverse
        fields[2, i] = fields[2, i] * inverse
    if end:
        z_out[z_out.shape[0] - 1] = fields[1, count - 1]

    ring = sums.shape[0]

    def transform(step):
        mode, i = divmod(step, count + 1)
        for comp in range(3):
            here = nodes[3 * mode + comp, i]
            above = shifted(here, 1, 1)
            for z, value in ((0, here + above), (1, above - here)):
                beside = shifted(value, 1, 0)
                sums[step % ring, 4 * comp + 2 * z] = value + beside
                sums[step % ring, 4 * comp + 2 * z + 1] = beside - value

    def energies(step, value):
        mode, i = divmod(step, count + 1)
        for row in range(0, width, 8):
            for lane in range(0, depth, 128):
                span = (pl.ds(row, 8), pl.ds(lane, 128))
                entries = [None] * 24
                for comp in range(3):
                    for z in (0, 1):
                        for y in (0, 1):
                            near = sums[(step % ring, 4 * comp + 2 * z + y) + span]
                            far = sums[((step + 1) % ring, 4 * comp + 2 * z + y) + span]
                            entries[3 * (2 * y + 4 * z) + comp] = near + far
                            entries[3 * (2 * y + 4 * z + 1) + comp] = far - near
                stiff, inert = element_energies(entries, squares, products)
                result = fields[(0, i) + span] * stiff - (value * fields[(2, i) + span]) * inert
                z_out[(mode * count + i,) + span] = result

    total = group // 3 * (count + 1)
    values = [eig[core * (group // 3) + mode] for mode in range(group // 3)]
    transform(0)
    transform(1)
    for step in range(total):
        if step + 2 < total:
            transform(step + 2)
        if step % (count + 1) < count:
            energies(step, values[step // (count + 1)])


class Layers:
    def __init__(self, *parts):
        self.where = {}
        for low, count, ref, offset, stride in parts:
            for i in range(count):
                self.where[low + i] = (ref, offset + i, stride)

    def __call__(self, mode, x):
        ref, offset, stride = self.where[x]
        return ref[mode * stride + offset]


def krylov_step(place, layers, modes, mass, zeroth, first_in, second_in, first_out, second_out, plan, moments, scratch):
    first, last = place[1], place[2]
    ones, twos, in_0, in_1, in_3, inner, ahead_of = plan
    width, depth = moments.shape[2], None
    inverse, count_of = scratch
    shape = inverse.shape[1:]
    width, depth = shape
    missing = missing_plane(shape)
    slot = {x: i for i, x in enumerate(sorted(set(ones) | set(twos) | set(in_0)))}
    for x, i in slot.items():
        count = neighbour_count(missing, x, layers, first, last)
        count_of[i] = count
        value = 1.0 / (mass(0, x) + RADIUS_SQ * count)
        if x < 0:
            value = value * (1.0 - scalar(first))
        if x >= layers:
            value = value * (1.0 - scalar(last))
        inverse[i] = value

    def apply(field, mode, x):
        here = field(mode, x)
        beside = field(mode, x - 1) + field(mode, x + 1)
        beside += shifted(here, 1, 1) + shifted(here, -1, 1)
        beside += shifted(here, 1, 0) + shifted(here, -1, 0)
        return mass(0, x) * here + RADIUS_SQ * (count_of[slot[x]] * here - beside)

    def fold(value):
        total = None
        for row in range(0, width, 8):
            for lane in range(0, depth, 128):
                piece = value[row : row + 8, lane : lane + 128]
                total = piece if total is None else total + piece
        return total

    row = lax.broadcasted_iota(jnp.int32, shape, 0)
    lane = lax.broadcasted_iota(jnp.int32, shape, 1)

    def one_mode(mode, carry):
        sums = [None] * 6

        def add(k, value):
            sums[k] = fold(value) if sums[k] is None else sums[k] + fold(value)

        for x in in_0:
            here = zeroth(mode, x)
            add(0, here * ((mass(0, x) + RADIUS_SQ * count_of[slot[x]]) * here))
        for x in ones:
            image = apply(zeroth, mode, x)
            one = image * inverse[slot[x]]
            first_out[mode * len(ones) + x - ones[0]] = one
            if x in in_1:
                add(1, zeroth(mode, x) * image)
                add(2, one * image)
        for x in twos:
            image = apply(first_in, mode, x)
            two = image * inverse[slot[x]]
            second_out[mode * len(twos) + x - twos[0]] = two
            if x in in_3:
                add(3, first_in(mode, x) * image)
                add(4, two * image)
        for x in inner:
            here = second_in(mode, x)
            add(5, mass(0, x) * here * here)
            aside = jnp.where(row == width - 1, 0.0, pltpu.roll(here, width - 1, 0) - here)
            above = jnp.where(lane == depth - 1, 0.0, pltpu.roll(here, depth - 1, 1) - here)
            add(5, RADIUS_SQ * (aside * aside + above * above))
        for x in ahead_of:
            edge = second_in(mode, x + 1) - second_in(mode, x)
            if x == layers - 1:
                edge = edge * (1.0 - scalar(last))
            add(5, RADIUS_SQ * (edge * edge))
        for k in range(6):
            if sums[k] is not None:
                moments[mode * 6 + k] = moments[mode * 6 + k] + sums[k]
        return carry

    lax.fori_loop(0, modes, one_mode, 0)


def send_halves(target, core, half, modes, parts, sems):
    _, other = halves(core, half)
    total = target.shape[0] // modes
    copies = []
    for mode in range(modes):
        at = mode * total
        for ref, offset, stride, count in parts:
            source = ref.at[pl.ds(mode * stride + offset, count), pl.ds(other, half), :]
            copies.append(pltpu.make_async_copy(source, target.at[pl.ds(at, count)], sems.at[len(copies)]))
            at += count
    for copy in copies:
        copy.start()
    return copies


def plans(layers):
    inner_ones, inner_twos = list(range(1, layers - 1)), list(range(2, layers - 2))
    inner = (inner_ones, inner_twos, list(range(layers)), inner_ones, inner_twos, inner_twos, inner_twos[:-1])
    right_ones, right_twos = [layers - 1, layers, layers + 1], [layers - 2, layers - 1, layers]
    right = (right_ones, right_twos, [], [layers - 1], right_twos[:2], right_twos[:2], [layers - 3] + right_twos[:2])
    left = ([-1, 0], [0, 1], [], [0], [0, 1], [0, 1], [0, 1])
    return inner, right, left


def inner_kernel(modes, layers, cuts, place, za, zb, zc, ma, mb, mc, ones, twos, moments, inverse, counts):
    plan = plans(layers)[0]
    zeroth, mass = z0_layers(cuts, layers, za, zb, zc), mass_layers(cuts, layers, ma, mb, mc)
    first = Layers((1, layers - 2, ones, 0, layers - 2))
    second = Layers((2, layers - 4, twos, 0, layers - 4))
    moments[...] = jnp.zeros(moments.shape, jnp.float32)
    krylov_step(place, layers, modes, mass, zeroth, first, second, ones, twos, plan, moments, (inverse, counts))


def z0_layers(cuts, layers, za, zb, zc):
    a, b = cuts
    return Layers((0, a, za, 0, a), (a, b - a, zb, 0, b - a), (b, layers - b, zc, 0, layers - b))


def mass_layers(cuts, layers, ma, mb, mc):
    a, b = cuts
    return Layers((0, a, ma, 0, 0), (a, b - a, mb, 0, 0), (b, layers - b, mc, 0, 0))


def right_kernel(modes, layers, cuts, place, zc, mc, down, ghost_mass, ones_in, twos_in, moments_in,
                 ones, twos, moments, inverse, counts):
    plan = plans(layers)[1]
    tail = layers - cuts[1]
    zeroth = Layers((cuts[1], tail, zc, 0, tail), (layers, DOWN, down, 0, DOWN))
    mass = Layers((cuts[1], tail, mc, 0, 0), (layers, 2, ghost_mass, 0, 0))
    first = Layers((1, layers - 2, ones_in, 0, layers - 2), (layers - 1, 3, ones, 0, 3))
    second = Layers((2, layers - 4, twos_in, 0, layers - 4), (layers - 2, 3, twos, 0, 3))
    moments[...] = moments_in[...]
    krylov_step(place, layers, modes, mass, zeroth, first, second, ones, twos, plan, moments, (inverse, counts))


def left_kernel(modes, layers, cuts, place, za, zb, zc, ma, up, ones_in, twos_in, ones_right, twos_right, moments_in,
                ones, twos, send, parts, inverse, counts, moments, sems):
    plan = plans(layers)[2]
    half = za.shape[1] // 2
    tail = layers - cuts[1]
    pieces = [(za, 0, cuts[0], cuts[0]), (zb, 0, cuts[1] - cuts[0], cuts[1] - cuts[0]), (zc, 0, tail, tail)]
    pieces += [(ones_in, 0, layers - 2, layers - 2), (ones_right, 0, 3, 1)]
    pieces += [(twos_in, 0, layers - 4, layers - 4), (twos_right, 0, 3, 2)]
    copies = send_halves(send, place[0], half, modes, pieces, sems)
    zeroth = Layers((-UP, UP, up, 0, UP), (0, cuts[0], za, 0, cuts[0]))
    mass = Layers((-1, 1, up, UP * modes, 0), (0, cuts[0], ma, 0, 0))
    first = Layers((-1, 2, ones, 0, 2), (1, layers - 2, ones_in, 0, layers - 2))
    second = Layers((0, 2, twos, 0, 2), (2, layers - 4, twos_in, 0, layers - 4))
    moments[...] = moments_in[...]
    krylov_step(place, layers, modes, mass, zeroth, first, second, ones, twos, plan, moments, (inverse, counts))
    _, other = halves(place[0], half)
    total = send.shape[0] // modes
    for mode in range(modes):
        at = (mode + 1) * total - 3
        send[at] = ones[2 * mode + 1, pl.ds(other, half), :]
        send[at + 1] = twos[2 * mode, pl.ds(other, half), :]
        send[at + 2] = twos[2 * mode + 1, pl.ds(other, half), :]
    row = lax.broadcasted_iota(jnp.int32, (8, 128), 0)
    lane = lax.broadcasted_iota(jnp.int32, (8, 128), 1)
    block = jnp.zeros((8, 128), jnp.float32)
    for mode in range(modes):
        for k in range(6):
            line = jnp.sum(moments[mode * 6 + k], axis=0, keepdims=True)
            total = jnp.sum(line, axis=1, keepdims=True)
            block = jnp.where((row == mode) & (lane == k), total, block)
    for i in range(parts.shape[0]):
        parts[i] = block
    for copy in copies:
        copy.wait()


def combine_kernel(modes, layers, cuts, place, parts, za, zb, zc, ones_in, twos_in, ones_right, twos_right,
                   ones_left, twos_left, swap, out):
    core = place[0]
    half, depth = out.shape[2:]
    mine, _ = halves(core, half)
    shape = (8, 128)
    lane = lax.broadcasted_iota(jnp.int32, shape, 1)
    factors = []
    for c in (0, 1):
        block = parts[c]
        for i in range(2 + c, parts.shape[0], 2):
            block = block + parts[i]
        m = [jnp.sum(jnp.where(lane == k, block, 0.0), axis=1, keepdims=True) for k in range(6)]
        one, two = m[2] / m[1], m[3] / m[1]
        pivot = m[3] - one * m[2]
        cross = m[4] - two * m[2]
        slope = cross / pivot
        rest = m[5] - two * m[3] - slope * cross
        right_1 = m[1] - one * m[0]
        right_2 = m[2] - two * m[0] - slope * right_1
        c2 = right_2 / rest
        c1 = (right_1 - cross * c2) / pivot
        c0 = (m[0] - m[2] * c1 - m[3] * c2) / m[1]
        factors.append([jnp.broadcast_to(c, (8, depth)) for c in (c0, c1, c2)])

    zeroth = z0_layers(cuts, layers, za, zb, zc)
    first = Layers((0, 1, ones_left, 1, 2), (1, layers - 2, ones_in, 0, layers - 2), (layers - 1, 1, ones_right, 0, 3))
    second = Layers((0, 2, twos_left, 0, 2), (2, layers - 4, twos_in, 0, layers - 4), (layers - 2, 2, twos_right, 0, 3))
    total = swap.shape[0] // modes
    theirs = [
        Layers((0, layers, swap, 0, total)),
        Layers((0, 1, swap, 3 * layers - 3, total), (1, layers - 1, swap, layers, total)),
        Layers((0, 2, swap, 3 * layers - 2, total), (2, layers - 2, swap, 2 * layers - 1, total)),
    ]

    for slot in (0, 1):
        for mode in range(modes):
            target = slot * modes + mode
            a, b, c = (f[mode : mode + 1] for f in factors[slot])

            @pl.when(core == slot)
            def _():
                for x in range(layers):
                    planes = []
                    for field in (zeroth, first, second):
                        ref, offset, stride = field.where[x]
                        planes.append(ref[mode * stride + offset, pl.ds(mine, half), :])
                    out[target, x] = a * planes[0] + b * planes[1] + c * planes[2]

            @pl.when(core != slot)
            def _():
                for x in range(layers):
                    planes = [field(mode, x) for field in theirs]
                    out[target, x] = a * planes[0] + b * planes[1] + c * planes[2]


def local(mode_shapes, eigenvalues, density, filter_mass, passive):
    f32 = jnp.float32
    layers, half, depth = density.shape
    group = mode_shapes.shape[0] // 2
    modes = group // 3
    width = 2 * half
    core, at = lax.axis_index("gy"), lax.axis_index("gx")
    count = lax.axis_size("gx")
    place = jnp.stack([core, (at == 0).astype(jnp.int32), (at == count - 1).astype(jnp.int32)]).astype(jnp.int32)
    across = [(0, 1), (1, 0)]
    straight = [(2 * i + c, 2 * i - 2 + c) for i in range(1, count) for c in (0, 1)]
    crossed = [(2 * i + c, 2 * i - 1 - c) for i in range(1, count) for c in (0, 1)]
    both = ("gx", "gy")
    smem = pl.BlockSpec(memory_space=pltpu.SMEM)
    vmem = pl.BlockSpec(memory_space=pltpu.VMEM)
    hbm = pl.BlockSpec(memory_space=pltpu.HBM)
    anywhere = pl.BlockSpec(memory_space=pl.ANY)

    def planes(n, rows=width):
        return jax.ShapeDtypeStruct((n, rows, depth), f32)

    def kernel(name, body, outs, in_specs, scratch, limit, work):
        return pl.pallas_call(
            body,
            out_shape=outs,
            in_specs=in_specs,
            out_specs=jax.tree.map(lambda _: vmem, outs),
            scratch_shapes=scratch,
            compiler_params=pltpu.CompilerParams(vmem_limit_bytes=limit * 2**20),
            cost_estimate=pl.CostEstimate(flops=work * 2**20, bytes_accessed=2**20, transcendentals=0),
            name=name,
        )

    first_node, first_cross, swap, field = kernel(
        "pack",
        pack_kernel,
        (planes(group + 2, half), planes(group + 2, half), planes((group + 3) * layers, half), planes(3 * layers, half)),
        [smem] + [hbm] * 4,
        [
            pltpu.VMEM((2, layers, half, depth), f32),
            pltpu.VMEM((layers, half, depth), jnp.int32),
            pltpu.SemaphoreType.DMA((5 + group,)),
        ],
        8,
        1,
    )(place, *(pltpu.with_memory_space_constraint(x, pltpu.HBM) for x in (mode_shapes, density, filter_mass, passive)))
    swap = lax.ppermute(swap, "gy", across)
    halo = lax.ppermute(first_node, both, straight)
    halo_swap = lax.ppermute(first_cross, both, crossed)

    cuts = (DOWN, layers - UP)

    def energies(name, low, high, *extra):
        end = high == layers
        n = high - low
        outs = (planes(modes * n + end), planes(n))
        return kernel(
            name,
            partial(energy_kernel, low, high, end),
            outs + (planes(2),) if end else outs,
            [smem, smem] + [anywhere] * (3 + len(extra)),
            [
                pltpu.VMEM((group, n + 1, width, depth), f32),
                pltpu.VMEM((3, n, width, depth), f32),
                pltpu.VMEM((4, 12, width, depth), f32),
                pltpu.SemaphoreType.DMA((group + 11,)),
            ],
            12,
            n * 200,
        )(place, eigenvalues, mode_shapes, swap, field, *extra)

    za, ma = energies("energies_first", 0, cuts[0])
    down, halo, halo_swap = lax.optimization_barrier((za, halo, halo_swap))
    down = lax.ppermute(down, "gx", [(i, i - 1) for i in range(1, count)])
    zc, mc, ghost_mass = energies("energies_last", cuts[1], layers, halo, halo_swap, ma)
    up = lax.ppermute(zc, "gx", [(i, i + 1) for i in range(count - 1)])
    zb, mb = energies("energies_inner", cuts[0], cuts[1], mc)

    tables = [pltpu.VMEM((layers, width, depth), f32)] * 2
    sums = jax.ShapeDtypeStruct((6 * modes, 8, 128), f32)
    ones_in, twos_in, moments = kernel(
        "krylov_inner",
        partial(inner_kernel, modes, layers, cuts),
        (planes(modes * (layers - 2)), planes(modes * (layers - 4)), sums),
        [smem] + [vmem] * 6,
        tables,
        12,
        400,
    )(place, za, zb, zc, ma, mb, mc)
    ones_right, twos_right, moments = kernel(
        "krylov_right",
        partial(right_kernel, modes, layers, cuts),
        (planes(3 * modes), planes(3 * modes), sums),
        [smem] + [vmem] * 7,
        tables,
        12,
        200,
    )(place, zc, mc, down, ghost_mass, ones_in, twos_in, moments)
    ones_left, twos_left, send, parts = kernel(
        "krylov_left",
        partial(left_kernel, modes, layers, cuts),
        (
            planes(2 * modes),
            planes(2 * modes),
            planes(modes * 3 * layers, half),
            jax.ShapeDtypeStruct((2 * count, 8, 128), f32),
        ),
        [smem] + [vmem] * 10,
        tables + [pltpu.VMEM((6 * modes, 8, 128), f32), pltpu.SemaphoreType.DMA((7 * modes,))],
        12,
        200,
    )(place, za, zb, zc, ma, up, ones_in, twos_in, ones_right, twos_right, moments)
    swap_in = lax.ppermute(send, "gy", across)
    parts = lax.all_to_all(parts, both, 0, 0, tiled=True)

    return kernel(
        "combine",
        partial(combine_kernel, modes, layers, cuts),
        jax.ShapeDtypeStruct((2 * modes, layers, half, depth), f32),
        [smem] + [vmem] * 11,
        [],
        12,
        100,
    )(place, parts, za, zb, zc, ones_in, twos_in, ones_right, twos_right, ones_left, twos_left, swap_in)


def solution(mesh):
    in_specs = (
        P("grp", "gx", "gy", None),
        P("grp"),
        P(("grp", "gx"), "gy", None),
        P(("grp", "gx"), "gy", None),
        P(("grp", "gx"), "gy", None),
    )
    out_specs = P("grp", "gx", "gy", None)
    return jax.shard_map(local, mesh=mesh, in_specs=in_specs, out_specs=out_specs, check_vma=False)
```

```python
import math
from functools import partial

import jax
import jax.numpy as jnp
import numpy as np
from jax import lax
from jax.experimental import pallas as pl
from jax.experimental.pallas import tpu as pltpu
from jax.sharding import PartitionSpec as P

ITERS = 3
RMIN = 4
RADIUS_SQ = RMIN * RMIN / 12.0
DOWN = 3
UP = 2


void_floor = 0.001


def element_table():
    poisson = 0.3
    lame_first = poisson / ((1.0 + poisson) * (1.0 - 2.0 * poisson))
    shear_mod = 1.0 / (2.0 * (1.0 + poisson))
    elastic = np.zeros((6, 6))
    elastic[:3, :3] = lame_first
    for entry in range(3):
        elastic[entry, entry] += 2.0 * shear_mod
        elastic[entry + 3, entry + 3] = shear_mod
    offset = 1.0 / math.sqrt(3.0)
    gauss_points = [(1.0 - offset) / 2.0, (1.0 + offset) / 2.0]
    stiffness = np.zeros((24, 24))
    inertia = np.zeros((24, 24))
    for point_x in gauss_points:
        for point_y in gauss_points:
            for point_z in gauss_points:
                coords = [point_x, point_y, point_z]
                values = np.zeros(8)
                gradient = np.zeros((8, 3))
                for corner in range(8):
                    corner_bits = [corner % 2, corner // 2 % 2, corner // 4]
                    factors = [
                        coords[dimen] if corner_bits[dimen] else 1.0 - coords[dimen]
                        for dimen in range(3)
                    ]
                    sign_list = [1.0 if corner_bits[dimen] else -1.0 for dimen in range(3)]
                    values[corner] = factors[0] * factors[1] * factors[2]
                    for dimen in range(3):
                        others = [
                            factors[other_dim] for other_dim in range(3) if other_dim != dimen
                        ]
                        gradient[corner, dimen] = sign_list[dimen] * others[0] * others[1]
                strain = np.zeros((6, 24))
                for corner in range(8):
                    column = 3 * corner
                    grad_x, grad_y, grad_z = gradient[corner]
                    strain[0, column] = grad_x
                    strain[1, column + 1] = grad_y
                    strain[2, column + 2] = grad_z
                    strain[3, column] = grad_y
                    strain[3, column + 1] = grad_x
                    strain[4, column + 1] = grad_z
                    strain[4, column + 2] = grad_y
                    strain[5, column] = grad_z
                    strain[5, column + 2] = grad_x
                stiffness += 0.125 * strain.T @ elastic @ strain
                shape_matrix = np.kron(values[None, :], np.eye(3))
                inertia += 0.125 * shape_matrix.T @ shape_matrix
    return stiffness, inertia


def energy_classes():
    stiffness, inertia = element_table()
    pair = np.array([[1.0, 1.0], [-1.0, 1.0]])
    basis = np.kron(np.kron(np.kron(pair, pair), pair), np.eye(3))
    stiffness = basis @ stiffness @ basis.T / 64.0
    inertia = basis @ inertia @ basis.T / 64.0
    squares, products = {}, {}
    for i in range(24):
        key = (round(stiffness[i, i], 9), round(inertia[i, i], 9))
        squares.setdefault(key, []).append(i)
        for j in range(i + 1, 24):
            if abs(stiffness[i, j]) > 1e-9:
                products.setdefault(round(stiffness[i, j], 9), []).append((i, j))
    squares = [
        (float(stiffness[v[0], v[0]]) if abs(k[0]) > 1e-9 else 0.0, float(inertia[v[0], v[0]]), v)
        for k, v in squares.items()
    ]
    products = [(2.0 * float(stiffness[v[0]]), v) for v in products.values()]
    return squares, products


def element_energies(entries, squares, products):
    stiff, inert = None, {}
    for weight, mass, members in squares:
        total = entries[members[0]] * entries[members[0]]
        for i in members[1:]:
            total = total + entries[i] * entries[i]
        if weight:
            stiff = total * weight if stiff is None else stiff + total * weight
        inert[mass] = inert[mass] + total if mass in inert else total
    for weight, members in products:
        total = entries[members[0][0]] * entries[members[0][1]]
        for i, j in members[1:]:
            total = total + entries[i] * entries[j]
        stiff = stiff + weight * total
    return stiff, sum(total * mass for mass, total in inert.items())


def shifted(value, step, dim):
    size = value.shape[dim]
    index = lax.broadcasted_iota(jnp.int32, value.shape, dim)
    edge = size - 1 if step > 0 else 0
    return jnp.where(index == edge, 0.0, pltpu.roll(value, (-step) % size, dim))


def missing_plane(shape):
    count = jnp.zeros(shape, jnp.float32)
    for dim in (0, 1):
        index = lax.broadcasted_iota(jnp.int32, shape, dim)
        count += (index == 0).astype(jnp.float32) + (index == shape[dim] - 1).astype(jnp.float32)
    return count


def scalar(flag):
    return jnp.where(flag, 1.0, 0.0).astype(jnp.float32)


def neighbour_count(missing, x, layers, first, last):
    count = 6.0 - missing
    if x == 0:
        count -= scalar(first)
    if x == layers - 1:
        count -= scalar(last)
    return count


def halves(core, half):
    return pl.multiple_of(core * half, half), pl.multiple_of((1 - core) * half, half)


def first_kernel(place, modes, mass, straight, crossed, sems):
    group = modes.shape[0] // 2
    core = place[0]
    copies = []
    for target, start in ((straight, core * group), (crossed, (1 - core) * group)):
        for source, at, count in ((modes.at[pl.ds(start, group), 0], 0, group), (mass.at[pl.ds(0, 2)], group, 2)):
            copies.append(pltpu.make_async_copy(source, target.at[pl.ds(at, count)], sems.at[len(copies)]))
    for copy in copies:
        copy.start()
    for copy in copies:
        copy.wait()


def energy_kernel(low, high, end, *refs):
    place, eig, modes, modes_swap, density, density_swap, mass, mass_swap, passive, passive_swap = refs[:10]
    if end:
        halo, halo_swap = refs[10:12]
        z_out, mass_out, ghost_mass, nodes, floats, flags, sums, sems = refs[-8:]
    else:
        z_out, mass_out, nodes, floats, flags, sums, sems = refs[-7:]
    layers, half, depth = modes.shape[1:]
    group = modes.shape[0] // 2
    width, count = 2 * half, high - low
    core, first, last = place[0], place[1], place[2]
    mine, other = halves(core, half)
    start = core * group
    copies = []

    def move(source, target):
        copy = pltpu.make_async_copy(source, target, sems.at[len(copies)])
        copy.start()
        copies.append(copy)

    span = pl.ds(low, count)
    for i, (own, theirs) in enumerate(((density, density_swap), (mass, mass_swap))):
        move(own.at[span], floats.at[i, :, pl.ds(mine, half), :])
        move(theirs.at[span], floats.at[i, :, pl.ds(other, half), :])
    move(passive.at[span], flags.at[:, pl.ds(mine, half), :])
    move(passive_swap.at[span], flags.at[:, pl.ds(other, half), :])
    if end:
        move(halo.at[pl.ds(group, 2)], ghost_mass.at[:, pl.ds(mine, half), :])
        move(halo_swap.at[pl.ds(group, 2)], ghost_mass.at[:, pl.ds(other, half), :])
    fields_end = len(copies)
    held = count if end else count + 1
    arrivals = []
    for mode in range(group // 3):
        before = len(copies)
        comps, rows = pl.ds(3 * mode, 3), pl.ds(start + 3 * mode, 3)
        for source, far, at in ((modes, halo if end else None, mine), (modes_swap, halo_swap if end else None, other)):
            move(source.at[rows, pl.ds(low, held)], nodes.at[comps, pl.ds(0, held), pl.ds(at, half), :])
            if end:
                move(far.at[comps], nodes.at[comps, count, pl.ds(at, half), :])
        arrivals.append(copies[before:])
    for copy in copies[:fields_end]:
        copy.wait()

    squares, products = energy_classes()
    missing = missing_plane((width, depth))
    for i in range(count):
        weight = floats[1, i]
        mass_out[i] = weight
        inverse = 1.0 / (weight + RADIUS_SQ * neighbour_count(missing, low + i, layers, first, last))
        design = (1 - flags[i]).astype(jnp.float32) * inverse
        rho = floats[0, i]
        floats[0, i] = 3.0 * (1.0 - void_floor) * rho * rho * design
        floats[1, i] = design
    if end:
        z_out[z_out.shape[0] - 1] = mass_out[count - 1]

    ring = sums.shape[0]

    def transform(step):
        mode, i = divmod(step, count + 1)
        if i == 0:
            for copy in arrivals[mode]:
                copy.wait()
        for comp in range(3):
            here = nodes[3 * mode + comp, i]
            above = shifted(here, 1, 1)
            for z, value in ((0, here + above), (1, above - here)):
                beside = shifted(value, 1, 0)
                sums[step % ring, 4 * comp + 2 * z] = value + beside
                sums[step % ring, 4 * comp + 2 * z + 1] = beside - value

    def energies(step, value):
        mode, i = divmod(step, count + 1)
        for row in range(0, width, 8):
            for lane in range(0, depth, 128):
                span = (pl.ds(row, 8), pl.ds(lane, 128))
                entries = [None] * 24
                for comp in range(3):
                    for z in (0, 1):
                        for y in (0, 1):
                            near = sums[(step % ring, 4 * comp + 2 * z + y) + span]
                            far = sums[((step + 1) % ring, 4 * comp + 2 * z + y) + span]
                            entries[3 * (2 * y + 4 * z) + comp] = near + far
                            entries[3 * (2 * y + 4 * z + 1) + comp] = far - near
                stiff, inert = element_energies(entries, squares, products)
                result = floats[(0, i) + span] * stiff - (value * floats[(1, i) + span]) * inert
                z_out[(mode * count + i,) + span] = result

    total = group // 3 * (count + 1)
    values = [eig[core * (group // 3) + mode] for mode in range(group // 3)]
    transform(0)
    transform(1)
    for step in range(total):
        if step + 2 < total:
            transform(step + 2)
        if step % (count + 1) < count:
            energies(step, values[step // (count + 1)])


class Layers:
    def __init__(self, *parts):
        self.where = {}
        for low, count, ref, offset, stride in parts:
            for i in range(count):
                self.where[low + i] = (ref, offset + i, stride)

    def __call__(self, mode, x):
        ref, offset, stride = self.where[x]
        return ref[mode * stride + offset]


def krylov_step(place, layers, modes, mass, zeroth, first_in, second_in, first_out, second_out, plan, moments, scratch):
    first, last = place[1], place[2]
    ones, twos, in_0, in_1, in_3, inner, ahead_of = plan
    width, depth = moments.shape[2], None
    inverse, count_of = scratch
    shape = inverse.shape[1:]
    width, depth = shape
    missing = missing_plane(shape)
    slot = {x: i for i, x in enumerate(sorted(set(ones) | set(twos) | set(in_0)))}
    for x, i in slot.items():
        count = neighbour_count(missing, x, layers, first, last)
        count_of[i] = count
        value = 1.0 / (mass(0, x) + RADIUS_SQ * count)
        if x < 0:
            value = value * (1.0 - scalar(first))
        if x >= layers:
            value = value * (1.0 - scalar(last))
        inverse[i] = value

    def apply(field, mode, x):
        here = field(mode, x)
        beside = field(mode, x - 1) + field(mode, x + 1)
        beside += shifted(here, 1, 1) + shifted(here, -1, 1)
        beside += shifted(here, 1, 0) + shifted(here, -1, 0)
        return mass(0, x) * here + RADIUS_SQ * (count_of[slot[x]] * here - beside)

    def fold(value):
        total = None
        for row in range(0, width, 8):
            for lane in range(0, depth, 128):
                piece = value[row : row + 8, lane : lane + 128]
                total = piece if total is None else total + piece
        return total

    row = lax.broadcasted_iota(jnp.int32, shape, 0)
    lane = lax.broadcasted_iota(jnp.int32, shape, 1)

    def one_mode(mode, carry):
        sums = [None] * 6

        def add(k, value):
            sums[k] = fold(value) if sums[k] is None else sums[k] + fold(value)

        for x in in_0:
            here = zeroth(mode, x)
            add(0, here * ((mass(0, x) + RADIUS_SQ * count_of[slot[x]]) * here))
        for x in ones:
            image = apply(zeroth, mode, x)
            one = image * inverse[slot[x]]
            first_out[mode * len(ones) + x - ones[0]] = one
            if x in in_1:
                add(1, zeroth(mode, x) * image)
                add(2, one * image)
        for x in twos:
            image = apply(first_in, mode, x)
            two = image * inverse[slot[x]]
            second_out[mode * len(twos) + x - twos[0]] = two
            if x in in_3:
                add(3, first_in(mode, x) * image)
                add(4, two * image)
        for x in inner:
            here = second_in(mode, x)
            add(5, mass(0, x) * here * here)
            aside = jnp.where(row == width - 1, 0.0, pltpu.roll(here, width - 1, 0) - here)
            above = jnp.where(lane == depth - 1, 0.0, pltpu.roll(here, depth - 1, 1) - here)
            add(5, RADIUS_SQ * (aside * aside + above * above))
        for x in ahead_of:
            edge = second_in(mode, x + 1) - second_in(mode, x)
            if x == layers - 1:
                edge = edge * (1.0 - scalar(last))
            add(5, RADIUS_SQ * (edge * edge))
        for k in range(6):
            if sums[k] is not None:
                moments[mode * 6 + k] = moments[mode * 6 + k] + sums[k]
        return carry

    lax.fori_loop(0, modes, one_mode, 0)


def send_halves(target, core, half, modes, parts, sems):
    _, other = halves(core, half)
    total = target.shape[0] // modes
    copies = []
    for mode in range(modes):
        at = mode * total
        for ref, offset, stride, count in parts:
            source = ref.at[pl.ds(mode * stride + offset, count), pl.ds(other, half), :]
            copies.append(pltpu.make_async_copy(source, target.at[pl.ds(at, count)], sems.at[len(copies)]))
            at += count
    for copy in copies:
        copy.start()
    return copies


def plans(layers):
    inner_ones, inner_twos = list(range(1, layers - 1)), list(range(2, layers - 2))
    inner = (inner_ones, inner_twos, list(range(layers)), inner_ones, inner_twos, inner_twos, inner_twos[:-1])
    right_ones, right_twos = [layers - 1, layers, layers + 1], [layers - 2, layers - 1, layers]
    right = (right_ones, right_twos, [], [layers - 1], right_twos[:2], right_twos[:2], [layers - 3] + right_twos[:2])
    left = ([-1, 0], [0, 1], [], [0], [0, 1], [0, 1], [0, 1])
    return inner, right, left


def inner_kernel(modes, layers, cuts, place, za, zb, zc, ma, mb, mc, ones, twos, moments, inverse, counts):
    plan = plans(layers)[0]
    zeroth, mass = z0_layers(cuts, layers, za, zb, zc), mass_layers(cuts, layers, ma, mb, mc)
    first = Layers((1, layers - 2, ones, 0, layers - 2))
    second = Layers((2, layers - 4, twos, 0, layers - 4))
    moments[...] = jnp.zeros(moments.shape, jnp.float32)
    krylov_step(place, layers, modes, mass, zeroth, first, second, ones, twos, plan, moments, (inverse, counts))


def z0_layers(cuts, layers, za, zb, zc):
    a, b = cuts
    return Layers((0, a, za, 0, a), (a, b - a, zb, 0, b - a), (b, layers - b, zc, 0, layers - b))


def mass_layers(cuts, layers, ma, mb, mc):
    a, b = cuts
    return Layers((0, a, ma, 0, 0), (a, b - a, mb, 0, 0), (b, layers - b, mc, 0, 0))


def right_kernel(modes, layers, cuts, place, zc, mc, down, ghost_mass, ones_in, twos_in, moments_in,
                 ones, twos, moments, inverse, counts):
    plan = plans(layers)[1]
    tail = layers - cuts[1]
    zeroth = Layers((cuts[1], tail, zc, 0, tail), (layers, DOWN, down, 0, DOWN))
    mass = Layers((cuts[1], tail, mc, 0, 0), (layers, 2, ghost_mass, 0, 0))
    first = Layers((1, layers - 2, ones_in, 0, layers - 2), (layers - 1, 3, ones, 0, 3))
    second = Layers((2, layers - 4, twos_in, 0, layers - 4), (layers - 2, 3, twos, 0, 3))
    moments[...] = moments_in[...]
    krylov_step(place, layers, modes, mass, zeroth, first, second, ones, twos, plan, moments, (inverse, counts))


def left_kernel(modes, layers, cuts, place, za, zb, zc, ma, up, ones_in, twos_in, ones_right, twos_right, moments_in,
                ones, twos, send, parts, inverse, counts, moments, sems):
    plan = plans(layers)[2]
    half = za.shape[1] // 2
    tail = layers - cuts[1]
    pieces = [(za, 0, cuts[0], cuts[0]), (zb, 0, cuts[1] - cuts[0], cuts[1] - cuts[0]), (zc, 0, tail, tail)]
    pieces += [(ones_in, 0, layers - 2, layers - 2), (ones_right, 0, 3, 1)]
    pieces += [(twos_in, 0, layers - 4, layers - 4), (twos_right, 0, 3, 2)]
    copies = send_halves(send, place[0], half, modes, pieces, sems)
    zeroth = Layers((-UP, UP, up, 0, UP), (0, cuts[0], za, 0, cuts[0]))
    mass = Layers((-1, 1, up, UP * modes, 0), (0, cuts[0], ma, 0, 0))
    first = Layers((-1, 2, ones, 0, 2), (1, layers - 2, ones_in, 0, layers - 2))
    second = Layers((0, 2, twos, 0, 2), (2, layers - 4, twos_in, 0, layers - 4))
    moments[...] = moments_in[...]
    krylov_step(place, layers, modes, mass, zeroth, first, second, ones, twos, plan, moments, (inverse, counts))
    _, other = halves(place[0], half)
    total = send.shape[0] // modes
    for mode in range(modes):
        at = (mode + 1) * total - 3
        send[at] = ones[2 * mode + 1, pl.ds(other, half), :]
        send[at + 1] = twos[2 * mode, pl.ds(other, half), :]
        send[at + 2] = twos[2 * mode + 1, pl.ds(other, half), :]
    row = lax.broadcasted_iota(jnp.int32, (8, 128), 0)
    lane = lax.broadcasted_iota(jnp.int32, (8, 128), 1)
    block = jnp.zeros((8, 128), jnp.float32)
    for mode in range(modes):
        for k in range(6):
            line = jnp.sum(moments[mode * 6 + k], axis=0, keepdims=True)
            total = jnp.sum(line, axis=1, keepdims=True)
            block = jnp.where((row == mode) & (lane == k), total, block)
    for i in range(parts.shape[0]):
        parts[i] = block
    for copy in copies:
        copy.wait()


def combine_kernel(modes, layers, cuts, place, parts, za, zb, zc, ones_in, twos_in, ones_right, twos_right,
                   ones_left, twos_left, swap, out):
    core = place[0]
    half, depth = out.shape[2:]
    mine, _ = halves(core, half)
    shape = (8, 128)
    lane = lax.broadcasted_iota(jnp.int32, shape, 1)
    factors = []
    for c in (0, 1):
        block = parts[c]
        for i in range(2 + c, parts.shape[0], 2):
            block = block + parts[i]
        m = [jnp.sum(jnp.where(lane == k, block, 0.0), axis=1, keepdims=True) for k in range(6)]
        one, two = m[2] / m[1], m[3] / m[1]
        pivot = m[3] - one * m[2]
        cross = m[4] - two * m[2]
        slope = cross / pivot
        rest = m[5] - two * m[3] - slope * cross
        right_1 = m[1] - one * m[0]
        right_2 = m[2] - two * m[0] - slope * right_1
        c2 = right_2 / rest
        c1 = (right_1 - cross * c2) / pivot
        c0 = (m[0] - m[2] * c1 - m[3] * c2) / m[1]
        factors.append([jnp.broadcast_to(c, (8, depth)) for c in (c0, c1, c2)])

    zeroth = z0_layers(cuts, layers, za, zb, zc)
    first = Layers((0, 1, ones_left, 1, 2), (1, layers - 2, ones_in, 0, layers - 2), (layers - 1, 1, ones_right, 0, 3))
    second = Layers((0, 2, twos_left, 0, 2), (2, layers - 4, twos_in, 0, layers - 4), (layers - 2, 2, twos_right, 0, 3))
    total = swap.shape[0] // modes
    theirs = [
        Layers((0, layers, swap, 0, total)),
        Layers((0, 1, swap, 3 * layers - 3, total), (1, layers - 1, swap, layers, total)),
        Layers((0, 2, swap, 3 * layers - 2, total), (2, layers - 2, swap, 2 * layers - 1, total)),
    ]

    for slot in (0, 1):
        for mode in range(modes):
            target = slot * modes + mode
            a, b, c = (f[mode : mode + 1] for f in factors[slot])

            @pl.when(core == slot)
            def _():
                for x in range(layers):
                    planes = []
                    for field in (zeroth, first, second):
                        ref, offset, stride = field.where[x]
                        planes.append(ref[mode * stride + offset, pl.ds(mine, half), :])
                    out[target, x] = a * planes[0] + b * planes[1] + c * planes[2]

            @pl.when(core != slot)
            def _():
                for x in range(layers):
                    planes = [field(mode, x) for field in theirs]
                    out[target, x] = a * planes[0] + b * planes[1] + c * planes[2]


def local(mode_shapes, eigenvalues, density, filter_mass, passive):
    f32 = jnp.float32
    layers, half, depth = density.shape
    group = mode_shapes.shape[0] // 2
    modes = group // 3
    width = 2 * half
    core, at = lax.axis_index("gy"), lax.axis_index("gx")
    count = lax.axis_size("gx")
    place = jnp.stack([core, (at == 0).astype(jnp.int32), (at == count - 1).astype(jnp.int32)]).astype(jnp.int32)
    across = [(0, 1), (1, 0)]
    downward = [(i, i - 1) for i in range(1, count)]
    upward = [(i, i + 1) for i in range(count - 1)]
    smem = pl.BlockSpec(memory_space=pltpu.SMEM)
    vmem = pl.BlockSpec(memory_space=pltpu.VMEM)
    anywhere = pl.BlockSpec(memory_space=pl.ANY)

    def planes(n, rows=width):
        return jax.ShapeDtypeStruct((n, rows, depth), f32)

    def kernel(name, body, outs, in_specs, scratch, limit, work):
        return pl.pallas_call(
            body,
            out_shape=outs,
            in_specs=in_specs,
            out_specs=jax.tree.map(lambda _: vmem, outs),
            scratch_shapes=scratch,
            compiler_params=pltpu.CompilerParams(vmem_limit_bytes=limit * 2**20),
            cost_estimate=pl.CostEstimate(flops=work * 2**20, bytes_accessed=2**20, transcendentals=0),
            name=name,
        )

    operands = []
    for x in (mode_shapes, density, filter_mass, passive):
        operands += [pltpu.with_memory_space_constraint(x, pltpu.HBM), lax.ppermute(x, "gy", across)]
    node, node_crossed = kernel(
        "first_layer",
        first_kernel,
        (planes(group + 2, half), planes(group + 2, half)),
        [smem] + [anywhere] * 2,
        [pltpu.SemaphoreType.DMA((4,))],
        4,
        1,
    )(place, operands[0], operands[4])
    straight = [(2 * i + c, 2 * i - 2 + c) for i in range(1, count) for c in (0, 1)]
    crossed = [(2 * i + c, 2 * i - 1 - c) for i in range(1, count) for c in (0, 1)]
    halo = lax.ppermute(node, ("gx", "gy"), straight)
    halo_swap = lax.ppermute(node_crossed, ("gx", "gy"), crossed)

    cuts = (DOWN, layers - UP)

    def energies(name, low, high, *extra):
        end = high == layers
        n = high - low
        outs = (planes(modes * n + end), planes(n))
        return kernel(
            name,
            partial(energy_kernel, low, high, end),
            outs + (planes(2),) if end else outs,
            [smem, smem] + [anywhere] * (8 + len(extra)),
            [
                pltpu.VMEM((group, n + 1, width, depth), f32),
                pltpu.VMEM((2, n, width, depth), f32),
                pltpu.VMEM((n, width, depth), jnp.int32),
                pltpu.VMEM((4, 12, width, depth), f32),
                pltpu.SemaphoreType.DMA((8 + 4 * modes,)),
            ],
            12,
            n * 200,
        )(place, eigenvalues, *operands, *extra)

    za, ma = energies("energies_first", 0, cuts[0])
    down = lax.ppermute(za, "gx", downward)
    zb, mb = energies("energies_inner", cuts[0], cuts[1], ma)
    zc, mc, ghost_mass = energies("energies_last", cuts[1], layers, halo, halo_swap, mb)
    up = lax.ppermute(zc, "gx", upward)

    tables = [pltpu.VMEM((layers, width, depth), f32)] * 2
    sums = jax.ShapeDtypeStruct((6 * modes, 8, 128), f32)
    ones_in, twos_in, moments = kernel(
        "krylov_inner",
        partial(inner_kernel, modes, layers, cuts),
        (planes(modes * (layers - 2)), planes(modes * (layers - 4)), sums),
        [smem] + [vmem] * 6,
        tables,
        12,
        400,
    )(place, za, zb, zc, ma, mb, mc)
    ones_right, twos_right, moments = kernel(
        "krylov_right",
        partial(right_kernel, modes, layers, cuts),
        (planes(3 * modes), planes(3 * modes), sums),
        [smem] + [vmem] * 7,
        tables,
        12,
        200,
    )(place, zc, mc, down, ghost_mass, ones_in, twos_in, moments)
    ones_left, twos_left, send, parts = kernel(
        "krylov_left",
        partial(left_kernel, modes, layers, cuts),
        (
            planes(2 * modes),
            planes(2 * modes),
            planes(modes * 3 * layers, half),
            jax.ShapeDtypeStruct((2 * count, 8, 128), f32),
        ),
        [smem] + [vmem] * 10,
        tables + [pltpu.VMEM((6 * modes, 8, 128), f32), pltpu.SemaphoreType.DMA((7 * modes,))],
        12,
        200,
    )(place, za, zb, zc, ma, up, ones_in, twos_in, ones_right, twos_right, moments)
    swap_in = lax.ppermute(send, "gy", across)
    parts = lax.all_to_all(parts, ("gx", "gy"), 0, 0, tiled=True)

    return kernel(
        "combine",
        partial(combine_kernel, modes, layers, cuts),
        jax.ShapeDtypeStruct((2 * modes, layers, half, depth), f32),
        [smem] + [vmem] * 11,
        [],
        12,
        100,
    )(place, parts, za, zb, zc, ones_in, twos_in, ones_right, twos_right, ones_left, twos_left, swap_in)


def solution(mesh):
    in_specs = (
        P("grp", "gx", "gy", None),
        P("grp"),
        P(("grp", "gx"), "gy", None),
        P(("grp", "gx"), "gy", None),
        P(("grp", "gx"), "gy", None),
    )
    out_specs = P("grp", "gx", "gy", None)
    return jax.shard_map(local, mesh=mesh, in_specs=in_specs, out_specs=out_specs, check_vma=False)
```

```python
import math
from functools import partial

import jax
import jax.numpy as jnp
import numpy as np
from jax import lax
from jax.experimental import pallas as pl
from jax.experimental.pallas import tpu as pltpu
from jax.sharding import PartitionSpec as P

ITERS = 3
RMIN = 4
RADIUS_SQ = RMIN * RMIN / 12.0
DOWN = 3
UP = 2


void_floor = 0.001


def element_table():
    poisson = 0.3
    lame_first = poisson / ((1.0 + poisson) * (1.0 - 2.0 * poisson))
    shear_mod = 1.0 / (2.0 * (1.0 + poisson))
    elastic = np.zeros((6, 6))
    elastic[:3, :3] = lame_first
    for entry in range(3):
        elastic[entry, entry] += 2.0 * shear_mod
        elastic[entry + 3, entry + 3] = shear_mod
    offset = 1.0 / math.sqrt(3.0)
    gauss_points = [(1.0 - offset) / 2.0, (1.0 + offset) / 2.0]
    stiffness = np.zeros((24, 24))
    inertia = np.zeros((24, 24))
    for point_x in gauss_points:
        for point_y in gauss_points:
            for point_z in gauss_points:
                coords = [point_x, point_y, point_z]
                values = np.zeros(8)
                gradient = np.zeros((8, 3))
                for corner in range(8):
                    corner_bits = [corner % 2, corner // 2 % 2, corner // 4]
                    factors = [
                        coords[dimen] if corner_bits[dimen] else 1.0 - coords[dimen]
                        for dimen in range(3)
                    ]
                    sign_list = [1.0 if corner_bits[dimen] else -1.0 for dimen in range(3)]
                    values[corner] = factors[0] * factors[1] * factors[2]
                    for dimen in range(3):
                        others = [
                            factors[other_dim] for other_dim in range(3) if other_dim != dimen
                        ]
                        gradient[corner, dimen] = sign_list[dimen] * others[0] * others[1]
                strain = np.zeros((6, 24))
                for corner in range(8):
                    column = 3 * corner
                    grad_x, grad_y, grad_z = gradient[corner]
                    strain[0, column] = grad_x
                    strain[1, column + 1] = grad_y
                    strain[2, column + 2] = grad_z
                    strain[3, column] = grad_y
                    strain[3, column + 1] = grad_x
                    strain[4, column + 1] = grad_z
                    strain[4, column + 2] = grad_y
                    strain[5, column] = grad_z
                    strain[5, column + 2] = grad_x
                stiffness += 0.125 * strain.T @ elastic @ strain
                shape_matrix = np.kron(values[None, :], np.eye(3))
                inertia += 0.125 * shape_matrix.T @ shape_matrix
    return stiffness, inertia


def energy_classes():
    stiffness, inertia = element_table()
    pair = np.array([[1.0, 1.0], [-1.0, 1.0]])
    basis = np.kron(np.kron(np.kron(pair, pair), pair), np.eye(3))
    stiffness = basis @ stiffness @ basis.T / 64.0
    inertia = basis @ inertia @ basis.T / 64.0
    squares, products = {}, {}
    for i in range(24):
        key = (round(stiffness[i, i], 9), round(inertia[i, i], 9))
        squares.setdefault(key, []).append(i)
        for j in range(i + 1, 24):
            if abs(stiffness[i, j]) > 1e-9:
                products.setdefault(round(stiffness[i, j], 9), []).append((i, j))
    squares = [
        (float(stiffness[v[0], v[0]]) if abs(k[0]) > 1e-9 else 0.0, float(inertia[v[0], v[0]]), v)
        for k, v in squares.items()
    ]
    products = [(2.0 * float(stiffness[v[0]]), v) for v in products.values()]
    return squares, products


def element_energies(entries, squares, products):
    stiff, inert = None, {}
    for weight, mass, members in squares:
        total = entries[members[0]] * entries[members[0]]
        for i in members[1:]:
            total = total + entries[i] * entries[i]
        if weight:
            stiff = total * weight if stiff is None else stiff + total * weight
        inert[mass] = inert[mass] + total if mass in inert else total
    for weight, members in products:
        total = entries[members[0][0]] * entries[members[0][1]]
        for i, j in members[1:]:
            total = total + entries[i] * entries[j]
        stiff = stiff + weight * total
    return stiff, sum(total * mass for mass, total in inert.items())


def shifted(value, step, dim):
    size = value.shape[dim]
    index = lax.broadcasted_iota(jnp.int32, value.shape, dim)
    edge = size - 1 if step > 0 else 0
    return jnp.where(index == edge, 0.0, pltpu.roll(value, (-step) % size, dim))


def missing_plane(shape):
    count = jnp.zeros(shape, jnp.float32)
    for dim in (0, 1):
        index = lax.broadcasted_iota(jnp.int32, shape, dim)
        count += (index == 0).astype(jnp.float32) + (index == shape[dim] - 1).astype(jnp.float32)
    return count


def scalar(flag):
    return jnp.where(flag, 1.0, 0.0).astype(jnp.float32)


def neighbour_count(missing, x, layers, first, last):
    count = 6.0 - missing
    if x == 0:
        count -= scalar(first)
    if x == layers - 1:
        count -= scalar(last)
    return count


def halves(core, half):
    return pl.multiple_of(core * half, half), pl.multiple_of((1 - core) * half, half)


def first_kernel(place, modes, density, mass, passive, straight, crossed, own, own_density, own_mass, own_passive, sems):
    group = modes.shape[0] // 2
    mine, theirs = pl.ds(place[0] * group, group), pl.ds((1 - place[0]) * group, group)
    moves = [
        (modes.at[mine, 0], straight.at[pl.ds(0, group)]),
        (mass.at[pl.ds(0, 2)], straight.at[pl.ds(group, 2)]),
        (modes.at[theirs, 0], crossed.at[pl.ds(0, group)]),
        (mass.at[pl.ds(0, 2)], crossed.at[pl.ds(group, 2)]),
        (modes.at[mine], own),
        (density, own_density),
        (mass, own_mass),
        (passive, own_passive),
    ]
    copies = [pltpu.make_async_copy(*move, sems.at[i]) for i, move in enumerate(moves)]
    for copy in copies:
        copy.start()
    for copy in copies:
        copy.wait()


def energy_kernel(low, high, end, *refs):
    place, eig, modes, modes_swap, density, density_swap, mass, mass_swap, passive, passive_swap = refs[:10]
    if end:
        halo, halo_swap = refs[10:12]
        z_out, mass_out, ghost_mass, floats, sums = refs[-5:]
    else:
        z_out, mass_out, floats, sums = refs[-4:]
    group, layers, half, depth = modes.shape
    width, count = 2 * half, high - low
    core, first, last = place[0], place[1], place[2]
    start = core * group
    lower = core == 0

    def whole(own, other):
        return jnp.concatenate([jnp.where(lower, own, other), jnp.where(lower, other, own)], axis=0)

    squares, products = energy_classes()
    missing = missing_plane((width, depth))
    for i in range(count):
        x = low + i
        weight = whole(mass[x], mass_swap[x])
        mass_out[i] = weight
        inverse = 1.0 / (weight + RADIUS_SQ * neighbour_count(missing, x, layers, first, last))
        design = (1 - whole(passive[x], passive_swap[x])).astype(jnp.float32) * inverse
        rho = whole(density[x], density_swap[x])
        floats[0, i] = 3.0 * (1.0 - void_floor) * rho * rho * design
        floats[1, i] = design
    if end:
        z_out[z_out.shape[0] - 1] = mass_out[count - 1]
        for i in (0, 1):
            ghost_mass[i] = whole(halo[group + i], halo_swap[group + i])

    def node(row, x):
        if x == layers:
            return whole(halo[row], halo_swap[row])
        return whole(modes[row, x], modes_swap[start + row, x])

    ring = sums.shape[0]

    def transform(step):
        mode, i = divmod(step, count + 1)
        for comp in range(3):
            here = node(3 * mode + comp, low + i)
            above = shifted(here, 1, 1)
            for z, value in ((0, here + above), (1, above - here)):
                beside = shifted(value, 1, 0)
                sums[step % ring, 4 * comp + 2 * z] = value + beside
                sums[step % ring, 4 * comp + 2 * z + 1] = beside - value

    def energies(step, value):
        mode, i = divmod(step, count + 1)
        for row in range(0, width, 8):
            for lane in range(0, depth, 128):
                span = (pl.ds(row, 8), pl.ds(lane, 128))
                entries = [None] * 24
                for comp in range(3):
                    for z in (0, 1):
                        for y in (0, 1):
                            near = sums[(step % ring, 4 * comp + 2 * z + y) + span]
                            far = sums[((step + 1) % ring, 4 * comp + 2 * z + y) + span]
                            entries[3 * (2 * y + 4 * z) + comp] = near + far
                            entries[3 * (2 * y + 4 * z + 1) + comp] = far - near
                stiff, inert = element_energies(entries, squares, products)
                result = floats[(0, i) + span] * stiff - (value * floats[(1, i) + span]) * inert
                z_out[(mode * count + i,) + span] = result

    total = group // 3 * (count + 1)
    values = [eig[core * (group // 3) + mode] for mode in range(group // 3)]
    transform(0)
    transform(1)
    for step in range(total):
        if step + 2 < total:
            transform(step + 2)
        if step % (count + 1) < count:
            energies(step, values[step // (count + 1)])


class Layers:
    def __init__(self, *parts):
        self.where = {}
        for low, count, ref, offset, stride in parts:
            for i in range(count):
                self.where[low + i] = (ref, offset + i, stride)

    def __call__(self, mode, x):
        ref, offset, stride = self.where[x]
        return ref[mode * stride + offset]


def krylov_step(place, layers, modes, mass, zeroth, first_in, second_in, first_out, second_out, plan, moments, scratch):
    first, last = place[1], place[2]
    ones, twos, in_0, in_1, in_3, inner, ahead_of = plan
    width, depth = moments.shape[2], None
    inverse, count_of = scratch
    shape = inverse.shape[1:]
    width, depth = shape
    missing = missing_plane(shape)
    slot = {x: i for i, x in enumerate(sorted(set(ones) | set(twos) | set(in_0)))}
    for x, i in slot.items():
        count = neighbour_count(missing, x, layers, first, last)
        count_of[i] = count
        value = 1.0 / (mass(0, x) + RADIUS_SQ * count)
        if x < 0:
            value = value * (1.0 - scalar(first))
        if x >= layers:
            value = value * (1.0 - scalar(last))
        inverse[i] = value

    def apply(field, mode, x):
        here = field(mode, x)
        beside = field(mode, x - 1) + field(mode, x + 1)
        beside += shifted(here, 1, 1) + shifted(here, -1, 1)
        beside += shifted(here, 1, 0) + shifted(here, -1, 0)
        return mass(0, x) * here + RADIUS_SQ * (count_of[slot[x]] * here - beside)

    def fold(value):
        total = None
        for row in range(0, width, 8):
            for lane in range(0, depth, 128):
                piece = value[row : row + 8, lane : lane + 128]
                total = piece if total is None else total + piece
        return total

    row = lax.broadcasted_iota(jnp.int32, shape, 0)
    lane = lax.broadcasted_iota(jnp.int32, shape, 1)

    def one_mode(mode, carry):
        sums = [None] * 6

        def add(k, value):
            sums[k] = fold(value) if sums[k] is None else sums[k] + fold(value)

        for x in in_0:
            here = zeroth(mode, x)
            add(0, here * ((mass(0, x) + RADIUS_SQ * count_of[slot[x]]) * here))
        for x in ones:
            image = apply(zeroth, mode, x)
            one = image * inverse[slot[x]]
            first_out[mode * len(ones) + x - ones[0]] = one
            if x in in_1:
                add(1, zeroth(mode, x) * image)
                add(2, one * image)
        for x in twos:
            image = apply(first_in, mode, x)
            two = image * inverse[slot[x]]
            second_out[mode * len(twos) + x - twos[0]] = two
            if x in in_3:
                add(3, first_in(mode, x) * image)
                add(4, two * image)
        for x in inner:
            here = second_in(mode, x)
            add(5, mass(0, x) * here * here)
            aside = jnp.where(row == width - 1, 0.0, pltpu.roll(here, width - 1, 0) - here)
            above = jnp.where(lane == depth - 1, 0.0, pltpu.roll(here, depth - 1, 1) - here)
            add(5, RADIUS_SQ * (aside * aside + above * above))
        for x in ahead_of:
            edge = second_in(mode, x + 1) - second_in(mode, x)
            if x == layers - 1:
                edge = edge * (1.0 - scalar(last))
            add(5, RADIUS_SQ * (edge * edge))
        for k in range(6):
            if sums[k] is not None:
                moments[mode * 6 + k] = moments[mode * 6 + k] + sums[k]
        return carry

    lax.fori_loop(0, modes, one_mode, 0)


def send_halves(target, core, half, modes, parts, sems):
    _, other = halves(core, half)
    total = target.shape[0] // modes
    copies = []
    for mode in range(modes):
        at = mode * total
        for ref, offset, stride, count in parts:
            source = ref.at[pl.ds(mode * stride + offset, count), pl.ds(other, half), :]
            copies.append(pltpu.make_async_copy(source, target.at[pl.ds(at, count)], sems.at[len(copies)]))
            at += count
    for copy in copies:
        copy.start()
    return copies


def plans(layers):
    ones, twos = list(range(1, layers + 2)), list(range(2, layers + 1))
    inner = twos[:-1]
    main = (ones, twos, list(range(layers)), list(range(1, layers)), inner, inner, inner)
    left = ([-1, 0], [0, 1], [], [0], [0, 1], [0, 1], [0, 1])
    return main, left


def main_kernel(modes, layers, cuts, place, za, zb, zc, ma, mb, mc, down, ghost_mass, ones, twos, moments, inverse, counts):
    plan = plans(layers)[0]
    zeroth = z0_layers(cuts, layers, za, zb, zc)
    zeroth.where.update(Layers((layers, DOWN, down, 0, DOWN)).where)
    mass = mass_layers(cuts, layers, ma, mb, mc)
    mass.where.update(Layers((layers, 2, ghost_mass, 0, 0)).where)
    first = Layers((1, layers + 1, ones, 0, layers + 1))
    second = Layers((2, layers - 1, twos, 0, layers - 1))
    moments[...] = jnp.zeros(moments.shape, jnp.float32)
    krylov_step(place, layers, modes, mass, zeroth, first, second, ones, twos, plan, moments, (inverse, counts))


def z0_layers(cuts, layers, za, zb, zc):
    a, b = cuts
    return Layers((0, a, za, 0, a), (a, b - a, zb, 0, b - a), (b, layers - b, zc, 0, layers - b))


def mass_layers(cuts, layers, ma, mb, mc):
    a, b = cuts
    return Layers((0, a, ma, 0, 0), (a, b - a, mb, 0, 0), (b, layers - b, mc, 0, 0))


def left_kernel(modes, layers, cuts, place, za, zb, zc, ma, up, ones_in, twos_in, moments_in,
                ones, twos, send, parts, inverse, counts, moments, sems):
    plan = plans(layers)[1]
    half = za.shape[1] // 2
    tail = layers - cuts[1]
    pieces = [(za, 0, cuts[0], cuts[0]), (zb, 0, cuts[1] - cuts[0], cuts[1] - cuts[0]), (zc, 0, tail, tail)]
    pieces += [(ones_in, 0, layers + 1, layers - 1), (twos_in, 0, layers - 1, layers - 2)]
    copies = send_halves(send, place[0], half, modes, pieces, sems)
    zeroth = Layers((-UP, UP, up, 0, UP), (0, cuts[0], za, 0, cuts[0]))
    mass = Layers((-1, 1, up, UP * modes, 0), (0, cuts[0], ma, 0, 0))
    first = Layers((-1, 2, ones, 0, 2), (1, layers - 1, ones_in, 0, layers + 1))
    second = Layers((0, 2, twos, 0, 2), (2, layers - 2, twos_in, 0, layers - 1))
    moments[...] = moments_in[...]
    krylov_step(place, layers, modes, mass, zeroth, first, second, ones, twos, plan, moments, (inverse, counts))
    _, other = halves(place[0], half)
    total = send.shape[0] // modes
    for mode in range(modes):
        at = (mode + 1) * total - 3
        send[at] = ones[2 * mode + 1, pl.ds(other, half), :]
        send[at + 1] = twos[2 * mode, pl.ds(other, half), :]
        send[at + 2] = twos[2 * mode + 1, pl.ds(other, half), :]
    row = lax.broadcasted_iota(jnp.int32, (8, 128), 0)
    lane = lax.broadcasted_iota(jnp.int32, (8, 128), 1)
    block = jnp.zeros((8, 128), jnp.float32)
    for mode in range(modes):
        for k in range(6):
            line = jnp.sum(moments[mode * 6 + k], axis=0, keepdims=True)
            total = jnp.sum(line, axis=1, keepdims=True)
            block = jnp.where((row == mode) & (lane == k), total, block)
    for i in range(parts.shape[0]):
        parts[i] = block
    for copy in copies:
        copy.wait()


def combine_kernel(modes, layers, cuts, place, parts, za, zb, zc, ones_in, twos_in,
                   ones_left, twos_left, swap, out):
    core = place[0]
    half, depth = out.shape[2:]
    mine, _ = halves(core, half)
    shape = (8, 128)
    lane = lax.broadcasted_iota(jnp.int32, shape, 1)
    factors = []
    for c in (0, 1):
        block = parts[c]
        for i in range(2 + c, parts.shape[0], 2):
            block = block + parts[i]
        m = [jnp.sum(jnp.where(lane == k, block, 0.0), axis=1, keepdims=True) for k in range(6)]
        one, two = m[2] / m[1], m[3] / m[1]
        pivot = m[3] - one * m[2]
        cross = m[4] - two * m[2]
        slope = cross / pivot
        rest = m[5] - two * m[3] - slope * cross
        right_1 = m[1] - one * m[0]
        right_2 = m[2] - two * m[0] - slope * right_1
        c2 = right_2 / rest
        c1 = (right_1 - cross * c2) / pivot
        c0 = (m[0] - m[2] * c1 - m[3] * c2) / m[1]
        factors.append([jnp.broadcast_to(c, (8, depth)) for c in (c0, c1, c2)])

    zeroth = z0_layers(cuts, layers, za, zb, zc)
    first = Layers((0, 1, ones_left, 1, 2), (1, layers - 1, ones_in, 0, layers + 1))
    second = Layers((0, 2, twos_left, 0, 2), (2, layers - 2, twos_in, 0, layers - 1))
    total = swap.shape[0] // modes
    theirs = [
        Layers((0, layers, swap, 0, total)),
        Layers((0, 1, swap, 3 * layers - 3, total), (1, layers - 1, swap, layers, total)),
        Layers((0, 2, swap, 3 * layers - 2, total), (2, layers - 2, swap, 2 * layers - 1, total)),
    ]

    for slot in (0, 1):
        for mode in range(modes):
            target = slot * modes + mode
            a, b, c = (f[mode : mode + 1] for f in factors[slot])

            @pl.when(core == slot)
            def _():
                for x in range(layers):
                    planes = []
                    for field in (zeroth, first, second):
                        ref, offset, stride = field.where[x]
                        planes.append(ref[mode * stride + offset, pl.ds(mine, half), :])
                    out[target, x] = a * planes[0] + b * planes[1] + c * planes[2]

            @pl.when(core != slot)
            def _():
                for x in range(layers):
                    planes = [field(mode, x) for field in theirs]
                    out[target, x] = a * planes[0] + b * planes[1] + c * planes[2]


def local(mode_shapes, eigenvalues, density, filter_mass, passive):
    f32 = jnp.float32
    layers, half, depth = density.shape
    group = mode_shapes.shape[0] // 2
    modes = group // 3
    width = 2 * half
    core, at = lax.axis_index("gy"), lax.axis_index("gx")
    count = lax.axis_size("gx")
    place = jnp.stack([core, (at == 0).astype(jnp.int32), (at == count - 1).astype(jnp.int32)]).astype(jnp.int32)
    across = [(0, 1), (1, 0)]
    downward = [(i, i - 1) for i in range(1, count)]
    upward = [(i, i + 1) for i in range(count - 1)]
    smem = pl.BlockSpec(memory_space=pltpu.SMEM)
    vmem = pl.BlockSpec(memory_space=pltpu.VMEM)
    anywhere = pl.BlockSpec(memory_space=pl.ANY)

    def planes(n, rows=width):
        return jax.ShapeDtypeStruct((n, rows, depth), f32)

    def kernel(name, body, outs, in_specs, scratch, limit, work):
        return pl.pallas_call(
            body,
            out_shape=outs,
            in_specs=in_specs,
            out_specs=jax.tree.map(lambda _: vmem, outs),
            scratch_shapes=scratch,
            compiler_params=pltpu.CompilerParams(vmem_limit_bytes=limit * 2**20),
            cost_estimate=pl.CostEstimate(flops=work * 2**20, bytes_accessed=2**20, transcendentals=0),
            name=name,
        )

    stored = [pltpu.with_memory_space_constraint(x, pltpu.HBM) for x in (mode_shapes, density, filter_mass, passive)]
    node, node_crossed, *own = kernel(
        "first_layer",
        first_kernel,
        (
            planes(group + 2, half),
            planes(group + 2, half),
            jax.ShapeDtypeStruct((group, layers, half, depth), f32),
            planes(layers, half),
            planes(layers, half),
            jax.ShapeDtypeStruct(passive.shape, passive.dtype),
        ),
        [smem] + [anywhere] * 4,
        [pltpu.SemaphoreType.DMA((8,))],
        4,
        1,
    )(place, *stored)
    operands = []
    for mine, x in zip(own, (mode_shapes, density, filter_mass, passive)):
        operands += [mine, lax.ppermute(x, "gy", across)]
    straight = [(2 * i + c, 2 * i - 2 + c) for i in range(1, count) for c in (0, 1)]
    crossed = [(2 * i + c, 2 * i - 1 - c) for i in range(1, count) for c in (0, 1)]
    halo = lax.ppermute(node, ("gx", "gy"), straight)
    halo_swap = lax.ppermute(node_crossed, ("gx", "gy"), crossed)

    cuts = (DOWN, layers - UP)

    def energies(name, low, high, *extra):
        end = high == layers
        n = high - low
        outs = (planes(modes * n + end), planes(n))
        return kernel(
            name,
            partial(energy_kernel, low, high, end),
            outs + (planes(2),) if end else outs,
            [smem, smem] + [vmem] * (8 + 2 * end) + [anywhere] * (len(extra) - 2 * end),
            [
                pltpu.VMEM((2, n, width, depth), f32),
                pltpu.VMEM((4, 12, width, depth), f32),
            ],
            12,
            n * 200,
        )(place, eigenvalues, *operands, *extra)

    za, ma = energies("energies_first", 0, cuts[0])
    down = lax.ppermute(za, "gx", downward)
    zb, mb = energies("energies_inner", cuts[0], cuts[1], ma)
    zc, mc, ghost_mass = energies("energies_last", cuts[1], layers, halo, halo_swap, mb)
    up = lax.ppermute(zc, "gx", upward)

    tables = [pltpu.VMEM((layers + 2, width, depth), f32)] * 2
    sums = jax.ShapeDtypeStruct((6 * modes, 8, 128), f32)
    ones_in, twos_in, moments = kernel(
        "krylov_main",
        partial(main_kernel, modes, layers, cuts),
        (planes(modes * (layers + 1)), planes(modes * (layers - 1)), sums),
        [smem] + [vmem] * 8,
        tables,
        12,
        400,
    )(place, za, zb, zc, ma, mb, mc, down, ghost_mass)
    ones_left, twos_left, send, parts = kernel(
        "krylov_left",
        partial(left_kernel, modes, layers, cuts),
        (
            planes(2 * modes),
            planes(2 * modes),
            planes(modes * 3 * layers, half),
            jax.ShapeDtypeStruct((2 * count, 8, 128), f32),
        ),
        [smem] + [vmem] * 8,
        tables + [pltpu.VMEM((6 * modes, 8, 128), f32), pltpu.SemaphoreType.DMA((5 * modes,))],
        12,
        200,
    )(place, za, zb, zc, ma, up, ones_in, twos_in, moments)
    swap_in = lax.ppermute(send, "gy", across)
    parts = lax.all_to_all(parts, ("gx", "gy"), 0, 0, tiled=True)

    return kernel(
        "combine",
        partial(combine_kernel, modes, layers, cuts),
        jax.ShapeDtypeStruct((2 * modes, layers, half, depth), f32),
        [smem] + [vmem] * 9,
        [],
        12,
        100,
    )(place, parts, za, zb, zc, ones_in, twos_in, ones_left, twos_left, swap_in)


def solution(mesh):
    in_specs = (
        P("grp", "gx", "gy", None),
        P("grp"),
        P(("grp", "gx"), "gy", None),
        P(("grp", "gx"), "gy", None),
        P(("grp", "gx"), "gy", None),
    )
    out_specs = P("grp", "gx", "gy", None)
    return jax.shard_map(local, mesh=mesh, in_specs=in_specs, out_specs=out_specs, check_vma=False)
```

```python
import math
from functools import partial

import jax
import jax.numpy as jnp
import numpy as np
from jax import lax
from jax.experimental import pallas as pl
from jax.experimental.pallas import tpu as pltpu
from jax.sharding import PartitionSpec as P

ITERS = 3
RMIN = 4
RADIUS_SQ = RMIN * RMIN / 12.0
DOWN = 3
UP = 2


void_floor = 0.001


def element_table():
    poisson = 0.3
    lame_first = poisson / ((1.0 + poisson) * (1.0 - 2.0 * poisson))
    shear_mod = 1.0 / (2.0 * (1.0 + poisson))
    elastic = np.zeros((6, 6))
    elastic[:3, :3] = lame_first
    for entry in range(3):
        elastic[entry, entry] += 2.0 * shear_mod
        elastic[entry + 3, entry + 3] = shear_mod
    offset = 1.0 / math.sqrt(3.0)
    gauss_points = [(1.0 - offset) / 2.0, (1.0 + offset) / 2.0]
    stiffness = np.zeros((24, 24))
    inertia = np.zeros((24, 24))
    for point_x in gauss_points:
        for point_y in gauss_points:
            for point_z in gauss_points:
                coords = [point_x, point_y, point_z]
                values = np.zeros(8)
                gradient = np.zeros((8, 3))
                for corner in range(8):
                    corner_bits = [corner % 2, corner // 2 % 2, corner // 4]
                    factors = [
                        coords[dimen] if corner_bits[dimen] else 1.0 - coords[dimen]
                        for dimen in range(3)
                    ]
                    sign_list = [1.0 if corner_bits[dimen] else -1.0 for dimen in range(3)]
                    values[corner] = factors[0] * factors[1] * factors[2]
                    for dimen in range(3):
                        others = [
                            factors[other_dim] for other_dim in range(3) if other_dim != dimen
                        ]
                        gradient[corner, dimen] = sign_list[dimen] * others[0] * others[1]
                strain = np.zeros((6, 24))
                for corner in range(8):
                    column = 3 * corner
                    grad_x, grad_y, grad_z = gradient[corner]
                    strain[0, column] = grad_x
                    strain[1, column + 1] = grad_y
                    strain[2, column + 2] = grad_z
                    strain[3, column] = grad_y
                    strain[3, column + 1] = grad_x
                    strain[4, column + 1] = grad_z
                    strain[4, column + 2] = grad_y
                    strain[5, column] = grad_z
                    strain[5, column + 2] = grad_x
                stiffness += 0.125 * strain.T @ elastic @ strain
                shape_matrix = np.kron(values[None, :], np.eye(3))
                inertia += 0.125 * shape_matrix.T @ shape_matrix
    return stiffness, inertia


def energy_classes():
    stiffness, inertia = element_table()
    pair = np.array([[1.0, 1.0], [-1.0, 1.0]])
    basis = np.kron(np.kron(np.kron(pair, pair), pair), np.eye(3))
    stiffness = basis @ stiffness @ basis.T / 64.0
    inertia = basis @ inertia @ basis.T / 64.0
    squares, products = {}, {}
    for i in range(24):
        key = (round(stiffness[i, i], 9), round(inertia[i, i], 9))
        squares.setdefault(key, []).append(i)
        for j in range(i + 1, 24):
            if abs(stiffness[i, j]) > 1e-9:
                products.setdefault(round(stiffness[i, j], 9), []).append((i, j))
    squares = [
        (float(stiffness[v[0], v[0]]) if abs(k[0]) > 1e-9 else 0.0, float(inertia[v[0], v[0]]), v)
        for k, v in squares.items()
    ]
    products = [(2.0 * float(stiffness[v[0]]), v) for v in products.values()]
    return squares, products


def element_energies(entries, squares, products):
    stiff, inert = None, {}
    for weight, mass, members in squares:
        total = entries[members[0]] * entries[members[0]]
        for i in members[1:]:
            total = total + entries[i] * entries[i]
        if weight:
            stiff = total * weight if stiff is None else stiff + total * weight
        inert[mass] = inert[mass] + total if mass in inert else total
    for weight, members in products:
        total = entries[members[0][0]] * entries[members[0][1]]
        for i, j in members[1:]:
            total = total + entries[i] * entries[j]
        stiff = stiff + weight * total
    return stiff, sum(total * mass for mass, total in inert.items())


def shifted(value, step, dim):
    size = value.shape[dim]
    index = lax.broadcasted_iota(jnp.int32, value.shape, dim)
    edge = size - 1 if step > 0 else 0
    return jnp.where(index == edge, 0.0, pltpu.roll(value, (-step) % size, dim))


def missing_plane(shape):
    count = jnp.zeros(shape, jnp.float32)
    for dim in (0, 1):
        index = lax.broadcasted_iota(jnp.int32, shape, dim)
        count += (index == 0).astype(jnp.float32) + (index == shape[dim] - 1).astype(jnp.float32)
    return count


def scalar(flag):
    return jnp.where(flag, 1.0, 0.0).astype(jnp.float32)


def neighbour_count(missing, x, layers, first, last):
    count = 6.0 - missing
    if x == 0:
        count -= scalar(first)
    if x == layers - 1:
        count -= scalar(last)
    return count


def halves(core, half):
    return pl.multiple_of(core * half, half), pl.multiple_of((1 - core) * half, half)


def first_kernel(place, modes, density, mass, passive, halo, own, own_density, own_mass, own_passive, sems):
    group = modes.shape[0] // 2
    moves = []
    for core in (0, 1):
        at = core * (group + 2)
        moves.append((modes.at[pl.ds(core * group, group), 0], halo.at[pl.ds(at, group)]))
        moves.append((mass.at[pl.ds(0, 2)], halo.at[pl.ds(at + group, 2)]))
    moves += [
        (modes.at[pl.ds(place[0] * group, group)], own),
        (density, own_density),
        (mass, own_mass),
        (passive, own_passive),
    ]
    copies = [pltpu.make_async_copy(*move, sems.at[i]) for i, move in enumerate(moves)]
    for copy in copies:
        copy.start()
    for copy in copies:
        copy.wait()


def energy_kernel(low, high, end, *refs):
    place, eig, modes, modes_swap, density, density_swap, mass, mass_swap, passive, passive_swap = refs[:10]
    if end:
        halo = refs[10]
        z_out, mass_out, ghost_mass, floats, sums = refs[-5:]
    else:
        z_out, mass_out, floats, sums = refs[-4:]
    group, layers, half, depth = modes.shape
    width, count = 2 * half, high - low
    core, first, last = place[0], place[1], place[2]
    start = core * group
    lower = core == 0

    def whole(own, other):
        return jnp.concatenate([jnp.where(lower, own, other), jnp.where(lower, other, own)], axis=0)

    squares, products = energy_classes()
    missing = missing_plane((width, depth))
    for i in range(count):
        x = low + i
        weight = whole(mass[x], mass_swap[x])
        mass_out[i] = weight
        inverse = 1.0 / (weight + RADIUS_SQ * neighbour_count(missing, x, layers, first, last))
        design = (1 - whole(passive[x], passive_swap[x])).astype(jnp.float32) * inverse
        rho = whole(density[x], density_swap[x])
        floats[0, i] = 3.0 * (1.0 - void_floor) * rho * rho * design
        floats[1, i] = design
    if end:
        z_out[z_out.shape[0] - 1] = mass_out[count - 1]
        for i in (0, 1):
            ghost_mass[i] = jnp.concatenate([halo[group + i], halo[2 * group + 2 + i]], axis=0)

    def node(row, x):
        if x == layers:
            return jnp.concatenate([halo[row], halo[group + 2 + row]], axis=0)
        return whole(modes[row, x], modes_swap[start + row, x])

    ring = sums.shape[0]

    def transform(step):
        mode, i = divmod(step, count + 1)
        for comp in range(3):
            here = node(3 * mode + comp, low + i)
            above = shifted(here, 1, 1)
            for z, value in ((0, here + above), (1, above - here)):
                beside = shifted(value, 1, 0)
                sums[step % ring, 4 * comp + 2 * z] = value + beside
                sums[step % ring, 4 * comp + 2 * z + 1] = beside - value

    def energies(step, value):
        mode, i = divmod(step, count + 1)
        for row in range(0, width, 8):
            for lane in range(0, depth, 128):
                span = (pl.ds(row, 8), pl.ds(lane, 128))
                entries = [None] * 24
                for comp in range(3):
                    for z in (0, 1):
                        for y in (0, 1):
                            near = sums[(step % ring, 4 * comp + 2 * z + y) + span]
                            far = sums[((step + 1) % ring, 4 * comp + 2 * z + y) + span]
                            entries[3 * (2 * y + 4 * z) + comp] = near + far
                            entries[3 * (2 * y + 4 * z + 1) + comp] = far - near
                stiff, inert = element_energies(entries, squares, products)
                result = floats[(0, i) + span] * stiff - (value * floats[(1, i) + span]) * inert
                z_out[(mode * count + i,) + span] = result

    total = group // 3 * (count + 1)
    values = [eig[core * (group // 3) + mode] for mode in range(group // 3)]
    transform(0)
    transform(1)
    for step in range(total):
        if step + 2 < total:
            transform(step + 2)
        if step % (count + 1) < count:
            energies(step, values[step // (count + 1)])


class Layers:
    def __init__(self, *parts):
        self.where = {}
        for low, count, ref, offset, stride in parts:
            for i in range(count):
                self.where[low + i] = (ref, offset + i, stride)

    def __call__(self, mode, x):
        ref, offset, stride = self.where[x]
        return ref[mode * stride + offset]


def krylov_step(place, layers, modes, mass, zeroth, first_in, second_in, first_out, second_out, plan, moments, scratch):
    first, last = place[1], place[2]
    ones, twos, in_0, in_1, in_3, inner, ahead_of = plan
    width, depth = moments.shape[2], None
    inverse, count_of = scratch
    shape = inverse.shape[1:]
    width, depth = shape
    missing = missing_plane(shape)
    slot = {x: i for i, x in enumerate(sorted(set(ones) | set(twos) | set(in_0)))}
    for x, i in slot.items():
        count = neighbour_count(missing, x, layers, first, last)
        count_of[i] = count
        value = 1.0 / (mass(0, x) + RADIUS_SQ * count)
        if x < 0:
            value = value * (1.0 - scalar(first))
        if x >= layers:
            value = value * (1.0 - scalar(last))
        inverse[i] = value

    def apply(field, mode, x):
        here = field(mode, x)
        beside = field(mode, x - 1) + field(mode, x + 1)
        beside += shifted(here, 1, 1) + shifted(here, -1, 1)
        beside += shifted(here, 1, 0) + shifted(here, -1, 0)
        return mass(0, x) * here + RADIUS_SQ * (count_of[slot[x]] * here - beside)

    def fold(value):
        total = None
        for row in range(0, width, 8):
            for lane in range(0, depth, 128):
                piece = value[row : row + 8, lane : lane + 128]
                total = piece if total is None else total + piece
        return total

    row = lax.broadcasted_iota(jnp.int32, shape, 0)
    lane = lax.broadcasted_iota(jnp.int32, shape, 1)

    def one_mode(mode, carry):
        sums = [None] * 6

        def add(k, value):
            sums[k] = fold(value) if sums[k] is None else sums[k] + fold(value)

        for x in in_0:
            here = zeroth(mode, x)
            add(0, here * ((mass(0, x) + RADIUS_SQ * count_of[slot[x]]) * here))
        for x in ones:
            image = apply(zeroth, mode, x)
            one = image * inverse[slot[x]]
            first_out[mode * len(ones) + x - ones[0]] = one
            if x in in_1:
                add(1, zeroth(mode, x) * image)
                add(2, one * image)
        for x in twos:
            image = apply(first_in, mode, x)
            two = image * inverse[slot[x]]
            second_out[mode * len(twos) + x - twos[0]] = two
            if x in in_3:
                add(3, first_in(mode, x) * image)
                add(4, two * image)
        for x in inner:
            here = second_in(mode, x)
            add(5, mass(0, x) * here * here)
            aside = jnp.where(row == width - 1, 0.0, pltpu.roll(here, width - 1, 0) - here)
            above = jnp.where(lane == depth - 1, 0.0, pltpu.roll(here, depth - 1, 1) - here)
            add(5, RADIUS_SQ * (aside * aside + above * above))
        for x in ahead_of:
            edge = second_in(mode, x + 1) - second_in(mode, x)
            if x == layers - 1:
                edge = edge * (1.0 - scalar(last))
            add(5, RADIUS_SQ * (edge * edge))
        for k in range(6):
            if sums[k] is not None:
                moments[mode * 6 + k] = moments[mode * 6 + k] + sums[k]
        return carry

    lax.fori_loop(0, modes, one_mode, 0)


def send_halves(target, core, half, modes, parts, sems, used):
    _, other = halves(core, half)
    total = target.shape[0] // modes
    copies = []
    for mode in range(modes):
        for ref, offset, stride, count, at in parts:
            source = ref.at[pl.ds(mode * stride + offset, count), pl.ds(other, half), :]
            sem = sems.at[used + len(copies)]
            copies.append(pltpu.make_async_copy(source, target.at[pl.ds(mode * total + at, count)], sem))
            copies[-1].start()
    return copies


def plans(layers):
    ones, twos = list(range(1, layers + 2)), list(range(2, layers + 1))
    inner = twos[:-1]
    main = (ones, twos, list(range(layers)), list(range(1, layers)), inner, inner, inner)
    left = ([-1, 0], [0, 1], [], [0], [0, 1], [0, 1], [0, 1])
    return main, left


def main_kernel(modes, layers, cuts, place, za, zb, zc, ma, mb, mc, down, ghost_mass,
                ones, twos, moments, send, inverse, counts, sems):
    plan = plans(layers)[0]
    zeroth = z0_layers(cuts, layers, za, zb, zc)
    zeroth.where.update(Layers((layers, DOWN, down, 0, DOWN)).where)
    mass = mass_layers(cuts, layers, ma, mb, mc)
    mass.where.update(Layers((layers, 2, ghost_mass, 0, 0)).where)
    first = Layers((1, layers + 1, ones, 0, layers + 1))
    second = Layers((2, layers - 1, twos, 0, layers - 1))
    moments[...] = jnp.zeros(moments.shape, jnp.float32)
    a, b = cuts
    half = za.shape[1] // 2
    known = [(za, 0, a, a, 0), (zb, 0, b - a, b - a, a), (zc, 0, layers - b, layers - b, b)]
    copies = send_halves(send, place[0], half, modes, known, sems, 0)
    krylov_step(place, layers, modes, mass, zeroth, first, second, ones, twos, plan, moments, (inverse, counts))
    made = [(ones, 0, layers + 1, layers - 1, layers), (twos, 0, layers - 1, layers - 2, 2 * layers - 1)]
    copies += send_halves(send, place[0], half, modes, made, sems, len(copies))
    for copy in copies:
        copy.wait()


def z0_layers(cuts, layers, za, zb, zc):
    a, b = cuts
    return Layers((0, a, za, 0, a), (a, b - a, zb, 0, b - a), (b, layers - b, zc, 0, layers - b))


def mass_layers(cuts, layers, ma, mb, mc):
    a, b = cuts
    return Layers((0, a, ma, 0, 0), (a, b - a, mb, 0, 0), (b, layers - b, mc, 0, 0))


def left_kernel(modes, layers, cuts, place, za, ma, up, ones_in, twos_in, moments_in, _,
                ones, twos, send, parts, inverse, counts, moments):
    plan = plans(layers)[1]
    zeroth = Layers((-UP, UP, up, 0, UP), (0, cuts[0], za, 0, cuts[0]))
    mass = Layers((-1, 1, up, UP * modes, 0), (0, cuts[0], ma, 0, 0))
    first = Layers((-1, 2, ones, 0, 2), (1, layers - 1, ones_in, 0, layers + 1))
    second = Layers((0, 2, twos, 0, 2), (2, layers - 2, twos_in, 0, layers - 1))
    moments[...] = moments_in[...]
    krylov_step(place, layers, modes, mass, zeroth, first, second, ones, twos, plan, moments, (inverse, counts))
    half = za.shape[1] // 2
    _, other = halves(place[0], half)
    total = send.shape[0] // modes
    for mode in range(modes):
        at = (mode + 1) * total - 3
        send[at] = ones[2 * mode + 1, pl.ds(other, half), :]
        send[at + 1] = twos[2 * mode, pl.ds(other, half), :]
        send[at + 2] = twos[2 * mode + 1, pl.ds(other, half), :]
    lines = [jnp.sum(moments[i], axis=0, keepdims=True) for i in range(6 * modes)]
    lines = jnp.concatenate(lines + [jnp.zeros((-len(lines) % 8, 128), jnp.float32)], axis=0)
    totals = jnp.sum(lines, axis=1, keepdims=True)
    row = lax.broadcasted_iota(jnp.int32, lines.shape, 0)
    lane = lax.broadcasted_iota(jnp.int32, lines.shape, 1)
    line = jnp.sum(jnp.where(row == lane, totals, 0.0), axis=0, keepdims=True)
    block = jnp.broadcast_to(line, (8, 128))
    for i in range(parts.shape[0]):
        parts[i] = block


def combine_kernel(modes, layers, cuts, place, parts, za, zb, zc, ones_in, twos_in,
                   ones_left, twos_left, swap, out_hbm, out, sems):
    core = place[0]
    half, depth = out.shape[2:]
    mine, _ = halves(core, half)
    shape = (8, 128)
    lane = lax.broadcasted_iota(jnp.int32, shape, 1)
    row = lax.broadcasted_iota(jnp.int32, shape, 0)
    factors = []
    for c in (0, 1):
        block = parts[c]
        for i in range(2 + c, parts.shape[0], 2):
            block = block + parts[i]
        m = [jnp.sum(jnp.where(lane == 6 * row + k, block, 0.0), axis=1, keepdims=True) for k in range(6)]
        one, two = m[2] / m[1], m[3] / m[1]
        pivot = m[3] - one * m[2]
        cross = m[4] - two * m[2]
        slope = cross / pivot
        rest = m[5] - two * m[3] - slope * cross
        right_1 = m[1] - one * m[0]
        right_2 = m[2] - two * m[0] - slope * right_1
        c2 = right_2 / rest
        c1 = (right_1 - cross * c2) / pivot
        c0 = (m[0] - m[2] * c1 - m[3] * c2) / m[1]
        factors.append([jnp.broadcast_to(c, (8, depth)) for c in (c0, c1, c2)])

    zeroth = z0_layers(cuts, layers, za, zb, zc)
    first = Layers((0, 1, ones_left, 1, 2), (1, layers - 1, ones_in, 0, layers + 1))
    second = Layers((0, 2, twos_left, 0, 2), (2, layers - 2, twos_in, 0, layers - 1))
    total = swap.shape[0] // modes
    theirs = [
        Layers((0, layers, swap, 0, total)),
        Layers((0, 1, swap, 3 * layers - 3, total), (1, layers - 1, swap, layers, total)),
        Layers((0, 2, swap, 3 * layers - 2, total), (2, layers - 2, swap, 2 * layers - 1, total)),
    ]

    copies = []
    for slot in (0, 1):
        for mode in range(modes):
            target = slot * modes + mode
            a, b, c = (f[mode : mode + 1] for f in factors[slot])

            @pl.when(core == slot)
            def _():
                for x in range(layers):
                    planes = []
                    for field in (zeroth, first, second):
                        ref, offset, stride = field.where[x]
                        planes.append(ref[mode * stride + offset, pl.ds(mine, half), :])
                    out[target, x] = a * planes[0] + b * planes[1] + c * planes[2]

            @pl.when(core != slot)
            def _():
                for x in range(layers):
                    planes = [field(mode, x) for field in theirs]
                    out[target, x] = a * planes[0] + b * planes[1] + c * planes[2]

            copies.append(pltpu.make_async_copy(out.at[target], out_hbm.at[target], sems.at[target]))
            copies[-1].start()
    for copy in copies:
        copy.wait()


def local(mode_shapes, eigenvalues, density, filter_mass, passive):
    f32 = jnp.float32
    layers, half, depth = density.shape
    group = mode_shapes.shape[0] // 2
    modes = group // 3
    width = 2 * half
    core, at = lax.axis_index("gy"), lax.axis_index("gx")
    count = lax.axis_size("gx")
    place = jnp.stack([core, (at == 0).astype(jnp.int32), (at == count - 1).astype(jnp.int32)]).astype(jnp.int32)
    across = [(0, 1), (1, 0)]
    downward = [(i, i - 1) for i in range(1, count)]
    upward = [(i, i + 1) for i in range(count - 1)]
    smem = pl.BlockSpec(memory_space=pltpu.SMEM)
    vmem = pl.BlockSpec(memory_space=pltpu.VMEM)
    anywhere = pl.BlockSpec(memory_space=pl.ANY)

    def planes(n, rows=width):
        return jax.ShapeDtypeStruct((n, rows, depth), f32)

    def kernel(name, body, outs, in_specs, scratch, limit, work, out_spec=vmem, aliases={}):
        return pl.pallas_call(
            body,
            out_shape=outs,
            in_specs=in_specs,
            out_specs=jax.tree.map(lambda _: out_spec, outs),
            input_output_aliases=aliases,
            scratch_shapes=scratch,
            compiler_params=pltpu.CompilerParams(vmem_limit_bytes=limit * 2**20),
            cost_estimate=pl.CostEstimate(flops=work * 2**20, bytes_accessed=2**20, transcendentals=0),
            name=name,
        )

    stored = [pltpu.with_memory_space_constraint(x, pltpu.HBM) for x in (mode_shapes, density, filter_mass, passive)]
    halo, *own = kernel(
        "first_layer",
        first_kernel,
        (
            planes(2 * group + 4, half),
            jax.ShapeDtypeStruct((group, layers, half, depth), f32),
            planes(layers, half),
            planes(layers, half),
            jax.ShapeDtypeStruct(passive.shape, passive.dtype),
        ),
        [smem] + [anywhere] * 4,
        [pltpu.SemaphoreType.DMA((8,))],
        4,
        1,
    )(place, *stored)
    operands = []
    for mine, x in zip(own, (mode_shapes, density, filter_mass, passive)):
        operands += [mine, lax.ppermute(x, "gy", across)]
    halo = lax.ppermute(halo, "gx", downward)

    cuts = (DOWN, layers - UP)

    def energies(name, low, high, *extra):
        end = high == layers
        n = high - low
        outs = (planes(modes * n + end), planes(n))
        return kernel(
            name,
            partial(energy_kernel, low, high, end),
            outs + (planes(2),) if end else outs,
            [smem, smem] + [vmem] * (8 + end) + [anywhere] * (len(extra) - end),
            [
                pltpu.VMEM((2, n, width, depth), f32),
                pltpu.VMEM((4, 12, width, depth), f32),
            ],
            12,
            n * 200,
        )(place, eigenvalues, *operands, *extra)

    za, ma = energies("energies_first", 0, cuts[0])
    down = lax.ppermute(za, "gx", downward)
    zb, mb = energies("energies_inner", cuts[0], cuts[1], ma)
    halo, _ = lax.optimization_barrier((halo, mb))
    halo = lax.all_to_all(halo, "gy", 0, 0, tiled=True)
    zc, mc, ghost_mass = energies("energies_last", cuts[1], layers, halo, mb)
    up = lax.ppermute(zc, "gx", upward)

    tables = [pltpu.VMEM((layers + 2, width, depth), f32)] * 2
    sums = jax.ShapeDtypeStruct((6 * modes, 8, 128), f32)
    ones_in, twos_in, moments, send = kernel(
        "krylov_main",
        partial(main_kernel, modes, layers, cuts),
        (planes(modes * (layers + 1)), planes(modes * (layers - 1)), sums, planes(modes * 3 * layers, half)),
        [smem] + [vmem] * 8,
        tables + [pltpu.SemaphoreType.DMA((5 * modes,))],
        12,
        400,
    )(place, za, zb, zc, ma, mb, mc, down, ghost_mass)
    ones_left, twos_left, send, parts = kernel(
        "krylov_left",
        partial(left_kernel, modes, layers, cuts),
        (
            planes(2 * modes),
            planes(2 * modes),
            planes(modes * 3 * layers, half),
            jax.ShapeDtypeStruct((2 * count, 8, 128), f32),
        ),
        [smem] + [vmem] * 7,
        tables + [pltpu.VMEM((6 * modes, 8, 128), f32)],
        12,
        200,
        aliases={7: 2},
    )(place, za, ma, up, ones_in, twos_in, moments, send)
    swap_in = lax.ppermute(send, "gy", across)
    parts = lax.all_to_all(parts, ("gx", "gy"), 0, 0, tiled=True)

    return kernel(
        "combine",
        partial(combine_kernel, modes, layers, cuts),
        jax.ShapeDtypeStruct((2 * modes, layers, half, depth), f32),
        [smem] + [vmem] * 9,
        [pltpu.VMEM((2 * modes, layers, half, depth), f32), pltpu.SemaphoreType.DMA((2 * modes,))],
        12,
        100,
        anywhere,
    )(place, parts, za, zb, zc, ones_in, twos_in, ones_left, twos_left, swap_in)


def solution(mesh):
    in_specs = (
        P("grp", "gx", "gy", None),
        P("grp"),
        P(("grp", "gx"), "gy", None),
        P(("grp", "gx"), "gy", None),
        P(("grp", "gx"), "gy", None),
    )
    out_specs = P("grp", "gx", "gy", None)
    return jax.shard_map(local, mesh=mesh, in_specs=in_specs, out_specs=out_specs, check_vma=False)
```

```python
import math
from functools import partial

import jax
import jax.numpy as jnp
import numpy as np
from jax import lax
from jax.experimental import pallas as pl
from jax.experimental.pallas import tpu as pltpu
from jax.sharding import PartitionSpec as P

ITERS = 3
RMIN = 4
RADIUS_SQ = RMIN * RMIN / 12.0
DOWN = 3
UP = 2


void_floor = 0.001


def element_table():
    poisson = 0.3
    lame_first = poisson / ((1.0 + poisson) * (1.0 - 2.0 * poisson))
    shear_mod = 1.0 / (2.0 * (1.0 + poisson))
    elastic = np.zeros((6, 6))
    elastic[:3, :3] = lame_first
    for entry in range(3):
        elastic[entry, entry] += 2.0 * shear_mod
        elastic[entry + 3, entry + 3] = shear_mod
    offset = 1.0 / math.sqrt(3.0)
    gauss_points = [(1.0 - offset) / 2.0, (1.0 + offset) / 2.0]
    stiffness = np.zeros((24, 24))
    inertia = np.zeros((24, 24))
    for point_x in gauss_points:
        for point_y in gauss_points:
            for point_z in gauss_points:
                coords = [point_x, point_y, point_z]
                values = np.zeros(8)
                gradient = np.zeros((8, 3))
                for corner in range(8):
                    corner_bits = [corner % 2, corner // 2 % 2, corner // 4]
                    factors = [
                        coords[dimen] if corner_bits[dimen] else 1.0 - coords[dimen]
                        for dimen in range(3)
                    ]
                    sign_list = [1.0 if corner_bits[dimen] else -1.0 for dimen in range(3)]
                    values[corner] = factors[0] * factors[1] * factors[2]
                    for dimen in range(3):
                        others = [
                            factors[other_dim] for other_dim in range(3) if other_dim != dimen
                        ]
                        gradient[corner, dimen] = sign_list[dimen] * others[0] * others[1]
                strain = np.zeros((6, 24))
                for corner in range(8):
                    column = 3 * corner
                    grad_x, grad_y, grad_z = gradient[corner]
                    strain[0, column] = grad_x
                    strain[1, column + 1] = grad_y
                    strain[2, column + 2] = grad_z
                    strain[3, column] = grad_y
                    strain[3, column + 1] = grad_x
                    strain[4, column + 1] = grad_z
                    strain[4, column + 2] = grad_y
                    strain[5, column] = grad_z
                    strain[5, column + 2] = grad_x
                stiffness += 0.125 * strain.T @ elastic @ strain
                shape_matrix = np.kron(values[None, :], np.eye(3))
                inertia += 0.125 * shape_matrix.T @ shape_matrix
    return stiffness, inertia


def energy_classes():
    stiffness, inertia = element_table()
    pair = np.array([[1.0, 1.0], [-1.0, 1.0]])
    basis = np.kron(np.kron(np.kron(pair, pair), pair), np.eye(3))
    stiffness = basis @ stiffness @ basis.T / 64.0
    inertia = basis @ inertia @ basis.T / 64.0
    squares, products = {}, {}
    for i in range(24):
        key = (round(stiffness[i, i], 9), round(inertia[i, i], 9))
        squares.setdefault(key, []).append(i)
        for j in range(i + 1, 24):
            if abs(stiffness[i, j]) > 1e-9:
                products.setdefault(round(stiffness[i, j], 9), []).append((i, j))
    squares = [
        (float(stiffness[v[0], v[0]]) if abs(k[0]) > 1e-9 else 0.0, float(inertia[v[0], v[0]]), v)
        for k, v in squares.items()
    ]
    products = [(2.0 * float(stiffness[v[0]]), v) for v in products.values()]
    return squares, products


def element_energies(entries, squares, products):
    stiff, inert = None, {}
    for weight, mass, members in squares:
        total = entries[members[0]] * entries[members[0]]
        for i in members[1:]:
            total = total + entries[i] * entries[i]
        if weight:
            stiff = total * weight if stiff is None else stiff + total * weight
        inert[mass] = inert[mass] + total if mass in inert else total
    for weight, members in products:
        total = entries[members[0][0]] * entries[members[0][1]]
        for i, j in members[1:]:
            total = total + entries[i] * entries[j]
        stiff = stiff + weight * total
    return stiff, sum(total * mass for mass, total in inert.items())


def shifted(value, step, dim):
    size = value.shape[dim]
    index = lax.broadcasted_iota(jnp.int32, value.shape, dim)
    edge = size - 1 if step > 0 else 0
    return jnp.where(index == edge, 0.0, pltpu.roll(value, (-step) % size, dim))


def missing_plane(shape):
    count = jnp.zeros(shape, jnp.float32)
    for dim in (0, 1):
        index = lax.broadcasted_iota(jnp.int32, shape, dim)
        count += (index == 0).astype(jnp.float32) + (index == shape[dim] - 1).astype(jnp.float32)
    return count


def scalar(flag):
    return jnp.where(flag, 1.0, 0.0).astype(jnp.float32)


def neighbour_count(missing, x, layers, first, last):
    count = 6.0 - missing
    if x == 0:
        count -= scalar(first)
    if x == layers - 1:
        count -= scalar(last)
    return count


def halves(core, half):
    return pl.multiple_of(core * half, half), pl.multiple_of((1 - core) * half, half)


def first_kernel(place, modes, density, mass, passive, straight, crossed, fields, signed, flags, sems):
    group = modes.shape[0] // 2
    layers = density.shape[0]
    moves = [(density, signed), (passive, flags), (mass, fields.at[pl.ds(layers, layers)])]
    for target, core in ((straight, place[0]), (crossed, 1 - place[0])):
        moves.append((modes.at[pl.ds(core * group, group), 0], target.at[pl.ds(0, group)]))
        moves.append((mass.at[pl.ds(0, 2)], target.at[pl.ds(group, 2)]))
    copies = [pltpu.make_async_copy(*move, sems.at[i]) for i, move in enumerate(moves)]
    for copy in copies:
        copy.start()
    for copy in copies[:2]:
        copy.wait()
    for x in range(layers):
        fields[x] = jnp.where(flags[x] == 0, signed[x], -signed[x])
    for copy in copies[2:]:
        copy.wait()


def energy_kernel(low, high, end, *refs):
    place, eig, modes, modes_swap, fields, fields_swap = refs[:6]
    if end:
        halo, halo_swap = refs[6:8]
        z_out, mass_out, ghost_mass, floats, sums = refs[-5:]
    else:
        z_out, mass_out, floats, sums = refs[-4:]
    layers, half, depth = modes.shape[1:]
    group = modes.shape[0] // 2
    width, count = 2 * half, high - low
    core, first, last = place[0], place[1], place[2]
    start = core * group
    lower = core == 0

    def whole(own, other):
        return jnp.concatenate([jnp.where(lower, own, other), jnp.where(lower, other, own)], axis=0)

    squares, products = energy_classes()
    missing = missing_plane((width, depth))
    for i in range(count):
        x = low + i
        weight = whole(fields[layers + x], fields_swap[layers + x])
        mass_out[i] = weight
        inverse = 1.0 / (weight + RADIUS_SQ * neighbour_count(missing, x, layers, first, last))
        rho = whole(fields[x], fields_swap[x])
        design = jnp.where(rho > 0.0, inverse, 0.0)
        floats[0, i] = 3.0 * (1.0 - void_floor) * rho * rho * design
        floats[1, i] = design
    if end:
        z_out[z_out.shape[0] - 1] = mass_out[count - 1]
        for i in (0, 1):
            ghost_mass[i] = whole(halo[group + i], halo_swap[group + i])

    def node(row, x):
        if x == layers:
            return whole(halo[row], halo_swap[row])
        return whole(modes[start + row, x], modes_swap[start + row, x])

    ring = sums.shape[0]

    def transform(step):
        mode, i = divmod(step, count + 1)
        for comp in range(3):
            here = node(3 * mode + comp, low + i)
            above = shifted(here, 1, 1)
            for z, value in ((0, here + above), (1, above - here)):
                beside = shifted(value, 1, 0)
                sums[step % ring, 4 * comp + 2 * z] = value + beside
                sums[step % ring, 4 * comp + 2 * z + 1] = beside - value

    def energies(step, value):
        mode, i = divmod(step, count + 1)
        for row in range(0, width, 8):
            for lane in range(0, depth, 128):
                span = (pl.ds(row, 8), pl.ds(lane, 128))
                entries = [None] * 24
                for comp in range(3):
                    for z in (0, 1):
                        for y in (0, 1):
                            near = sums[(step % ring, 4 * comp + 2 * z + y) + span]
                            far = sums[((step + 1) % ring, 4 * comp + 2 * z + y) + span]
                            entries[3 * (2 * y + 4 * z) + comp] = near + far
                            entries[3 * (2 * y + 4 * z + 1) + comp] = far - near
                stiff, inert = element_energies(entries, squares, products)
                result = floats[(0, i) + span] * stiff - (value * floats[(1, i) + span]) * inert
                z_out[(mode * count + i,) + span] = result

    total = group // 3 * (count + 1)
    values = [eig[core * (group // 3) + mode] for mode in range(group // 3)]
    transform(0)
    transform(1)
    for step in range(total):
        if step + 2 < total:
            transform(step + 2)
        if step % (count + 1) < count:
            energies(step, values[step // (count + 1)])


class Layers:
    def __init__(self, *parts):
        self.where = {}
        for low, count, ref, offset, stride in parts:
            for i in range(count):
                self.where[low + i] = (ref, offset + i, stride)

    def __call__(self, mode, x):
        ref, offset, stride = self.where[x]
        return ref[mode * stride + offset]


def krylov_step(place, layers, modes, mass, zeroth, first_in, second_in, first_out, second_out, plan, moments, scratch):
    first, last = place[1], place[2]
    ones, twos, in_0, in_1, in_3, inner, ahead_of = plan
    width, depth = moments.shape[2], None
    inverse, count_of = scratch
    shape = inverse.shape[1:]
    width, depth = shape
    missing = missing_plane(shape)
    slot = {x: i for i, x in enumerate(sorted(set(ones) | set(twos) | set(in_0)))}
    for x, i in slot.items():
        count = neighbour_count(missing, x, layers, first, last)
        count_of[i] = count
        value = 1.0 / (mass(0, x) + RADIUS_SQ * count)
        if x < 0:
            value = value * (1.0 - scalar(first))
        if x >= layers:
            value = value * (1.0 - scalar(last))
        inverse[i] = value

    def apply(field, mode, x):
        here = field(mode, x)
        beside = field(mode, x - 1) + field(mode, x + 1)
        beside += shifted(here, 1, 1) + shifted(here, -1, 1)
        beside += shifted(here, 1, 0) + shifted(here, -1, 0)
        return mass(0, x) * here + RADIUS_SQ * (count_of[slot[x]] * here - beside)

    def fold(value):
        total = None
        for row in range(0, width, 8):
            for lane in range(0, depth, 128):
                piece = value[row : row + 8, lane : lane + 128]
                total = piece if total is None else total + piece
        return total

    row = lax.broadcasted_iota(jnp.int32, shape, 0)
    lane = lax.broadcasted_iota(jnp.int32, shape, 1)

    def one_mode(mode, carry):
        sums = [None] * 6

        def add(k, value):
            sums[k] = fold(value) if sums[k] is None else sums[k] + fold(value)

        for x in in_0:
            here = zeroth(mode, x)
            add(0, here * ((mass(0, x) + RADIUS_SQ * count_of[slot[x]]) * here))
        for x in ones:
            image = apply(zeroth, mode, x)
            one = image * inverse[slot[x]]
            first_out[mode * len(ones) + x - ones[0]] = one
            if x in in_1:
                add(1, zeroth(mode, x) * image)
                add(2, one * image)
        for x in twos:
            image = apply(first_in, mode, x)
            two = image * inverse[slot[x]]
            second_out[mode * len(twos) + x - twos[0]] = two
            if x in in_3:
                add(3, first_in(mode, x) * image)
                add(4, two * image)
        for x in inner:
            here = second_in(mode, x)
            add(5, mass(0, x) * here * here)
            aside = jnp.where(row == width - 1, 0.0, pltpu.roll(here, width - 1, 0) - here)
            above = jnp.where(lane == depth - 1, 0.0, pltpu.roll(here, depth - 1, 1) - here)
            add(5, RADIUS_SQ * (aside * aside + above * above))
        for x in ahead_of:
            edge = second_in(mode, x + 1) - second_in(mode, x)
            if x == layers - 1:
                edge = edge * (1.0 - scalar(last))
            add(5, RADIUS_SQ * (edge * edge))
        for k in range(6):
            if sums[k] is not None:
                moments[mode * 6 + k] = moments[mode * 6 + k] + sums[k]
        return carry

    lax.fori_loop(0, modes, one_mode, 0)


def send_halves(target, core, half, modes, parts, sems, used):
    _, other = halves(core, half)
    total = target.shape[0] // modes
    copies = []
    for mode in range(modes):
        for ref, offset, stride, count, at in parts:
            source = ref.at[pl.ds(mode * stride + offset, count), pl.ds(other, half), :]
            sem = sems.at[used + len(copies)]
            copies.append(pltpu.make_async_copy(source, target.at[pl.ds(mode * total + at, count)], sem))
            copies[-1].start()
    return copies


def plans(layers):
    ones, twos = list(range(1, layers + 2)), list(range(2, layers + 1))
    inner = twos[:-1]
    main = (ones, twos, list(range(layers)), list(range(1, layers)), inner, inner, inner)
    left = ([-1, 0], [0, 1], [], [0], [0, 1], [0, 1], [0, 1])
    return main, left


def main_kernel(modes, layers, cuts, place, za, zb, zc, ma, mb, mc, down, ghost_mass,
                ones, twos, moments, send, inverse, counts, sems):
    plan = plans(layers)[0]
    zeroth = z0_layers(cuts, layers, za, zb, zc)
    zeroth.where.update(Layers((layers, DOWN, down, 0, DOWN)).where)
    mass = mass_layers(cuts, layers, ma, mb, mc)
    mass.where.update(Layers((layers, 2, ghost_mass, 0, 0)).where)
    first = Layers((1, layers + 1, ones, 0, layers + 1))
    second = Layers((2, layers - 1, twos, 0, layers - 1))
    moments[...] = jnp.zeros(moments.shape, jnp.float32)
    a, b = cuts
    half = za.shape[1] // 2
    known = [(za, 0, a, a, 0), (zb, 0, b - a, b - a, a), (zc, 0, layers - b, layers - b, b)]
    copies = send_halves(send, place[0], half, modes, known, sems, 0)
    krylov_step(place, layers, modes, mass, zeroth, first, second, ones, twos, plan, moments, (inverse, counts))
    made = [(ones, 0, layers + 1, layers - 1, layers), (twos, 0, layers - 1, layers - 2, 2 * layers - 1)]
    copies += send_halves(send, place[0], half, modes, made, sems, len(copies))
    for copy in copies:
        copy.wait()


def z0_layers(cuts, layers, za, zb, zc):
    a, b = cuts
    return Layers((0, a, za, 0, a), (a, b - a, zb, 0, b - a), (b, layers - b, zc, 0, layers - b))


def mass_layers(cuts, layers, ma, mb, mc):
    a, b = cuts
    return Layers((0, a, ma, 0, 0), (a, b - a, mb, 0, 0), (b, layers - b, mc, 0, 0))


def left_kernel(modes, layers, cuts, place, za, ma, up, ones_in, twos_in, moments_in, _,
                ones, twos, send, parts, inverse, counts, moments):
    plan = plans(layers)[1]
    zeroth = Layers((-UP, UP, up, 0, UP), (0, cuts[0], za, 0, cuts[0]))
    mass = Layers((-1, 1, up, UP * modes, 0), (0, cuts[0], ma, 0, 0))
    first = Layers((-1, 2, ones, 0, 2), (1, layers - 1, ones_in, 0, layers + 1))
    second = Layers((0, 2, twos, 0, 2), (2, layers - 2, twos_in, 0, layers - 1))
    moments[...] = moments_in[...]
    krylov_step(place, layers, modes, mass, zeroth, first, second, ones, twos, plan, moments, (inverse, counts))
    half = za.shape[1] // 2
    _, other = halves(place[0], half)
    total = send.shape[0] // modes
    for mode in range(modes):
        at = (mode + 1) * total - 3
        send[at] = ones[2 * mode + 1, pl.ds(other, half), :]
        send[at + 1] = twos[2 * mode, pl.ds(other, half), :]
        send[at + 2] = twos[2 * mode + 1, pl.ds(other, half), :]
    lines = [jnp.sum(moments[i], axis=0, keepdims=True) for i in range(6 * modes)]
    lines = jnp.concatenate(lines + [jnp.zeros((-len(lines) % 8, 128), jnp.float32)], axis=0)
    totals = jnp.sum(lines, axis=1, keepdims=True)
    row = lax.broadcasted_iota(jnp.int32, lines.shape, 0)
    lane = lax.broadcasted_iota(jnp.int32, lines.shape, 1)
    line = jnp.sum(jnp.where(row == lane, totals, 0.0), axis=0, keepdims=True)
    block = jnp.broadcast_to(line, (8, 128))
    for i in range(parts.shape[0]):
        parts[i] = block


def combine_kernel(modes, layers, cuts, place, parts, za, zb, zc, ones_in, twos_in,
                   ones_left, twos_left, swap, out_hbm, out, sems):
    core = place[0]
    half, depth = out.shape[2:]
    mine, _ = halves(core, half)
    shape = (8, 128)
    lane = lax.broadcasted_iota(jnp.int32, shape, 1)
    row = lax.broadcasted_iota(jnp.int32, shape, 0)
    factors = []
    for c in (0, 1):
        block = parts[c]
        for i in range(2 + c, parts.shape[0], 2):
            block = block + parts[i]
        m = [jnp.sum(jnp.where(lane == 6 * row + k, block, 0.0), axis=1, keepdims=True) for k in range(6)]
        one, two = m[2] / m[1], m[3] / m[1]
        pivot = m[3] - one * m[2]
        cross = m[4] - two * m[2]
        slope = cross / pivot
        rest = m[5] - two * m[3] - slope * cross
        right_1 = m[1] - one * m[0]
        right_2 = m[2] - two * m[0] - slope * right_1
        c2 = right_2 / rest
        c1 = (right_1 - cross * c2) / pivot
        c0 = (m[0] - m[2] * c1 - m[3] * c2) / m[1]
        factors.append([jnp.broadcast_to(c, (8, depth)) for c in (c0, c1, c2)])

    zeroth = z0_layers(cuts, layers, za, zb, zc)
    first = Layers((0, 1, ones_left, 1, 2), (1, layers - 1, ones_in, 0, layers + 1))
    second = Layers((0, 2, twos_left, 0, 2), (2, layers - 2, twos_in, 0, layers - 1))
    total = swap.shape[0] // modes
    theirs = [
        Layers((0, layers, swap, 0, total)),
        Layers((0, 1, swap, 3 * layers - 3, total), (1, layers - 1, swap, layers, total)),
        Layers((0, 2, swap, 3 * layers - 2, total), (2, layers - 2, swap, 2 * layers - 1, total)),
    ]

    copies = []
    for slot in (0, 1):
        for mode in range(modes):
            target = slot * modes + mode
            a, b, c = (f[mode : mode + 1] for f in factors[slot])

            @pl.when(core == slot)
            def _():
                for x in range(layers):
                    planes = []
                    for field in (zeroth, first, second):
                        ref, offset, stride = field.where[x]
                        planes.append(ref[mode * stride + offset, pl.ds(mine, half), :])
                    out[target, x] = a * planes[0] + b * planes[1] + c * planes[2]

            @pl.when(core != slot)
            def _():
                for x in range(layers):
                    planes = [field(mode, x) for field in theirs]
                    out[target, x] = a * planes[0] + b * planes[1] + c * planes[2]

            copies.append(pltpu.make_async_copy(out.at[target], out_hbm.at[target], sems.at[target]))
            copies[-1].start()
    for copy in copies:
        copy.wait()


def local(mode_shapes, eigenvalues, density, filter_mass, passive):
    f32 = jnp.float32
    layers, half, depth = density.shape
    group = mode_shapes.shape[0] // 2
    modes = group // 3
    width = 2 * half
    core, at = lax.axis_index("gy"), lax.axis_index("gx")
    count = lax.axis_size("gx")
    place = jnp.stack([core, (at == 0).astype(jnp.int32), (at == count - 1).astype(jnp.int32)]).astype(jnp.int32)
    across = [(0, 1), (1, 0)]
    downward = [(i, i - 1) for i in range(1, count)]
    upward = [(i, i + 1) for i in range(count - 1)]
    smem = pl.BlockSpec(memory_space=pltpu.SMEM)
    vmem = pl.BlockSpec(memory_space=pltpu.VMEM)
    anywhere = pl.BlockSpec(memory_space=pl.ANY)

    def planes(n, rows=width):
        return jax.ShapeDtypeStruct((n, rows, depth), f32)

    def kernel(name, body, outs, in_specs, scratch, limit, work, out_spec=vmem, aliases={}):
        return pl.pallas_call(
            body,
            out_shape=outs,
            in_specs=in_specs,
            out_specs=jax.tree.map(lambda _: out_spec, outs),
            input_output_aliases=aliases,
            scratch_shapes=scratch,
            compiler_params=pltpu.CompilerParams(vmem_limit_bytes=limit * 2**20),
            cost_estimate=pl.CostEstimate(flops=work * 2**20, bytes_accessed=2**20, transcendentals=0),
            name=name,
        )

    stored = [pltpu.with_memory_space_constraint(x, pltpu.HBM) for x in (mode_shapes, density, filter_mass, passive)]
    node, node_crossed, fields = kernel(
        "first_layer",
        first_kernel,
        (planes(group + 2, half), planes(group + 2, half), planes(2 * layers, half)),
        [smem] + [anywhere] * 4,
        [
            pltpu.VMEM((layers, half, depth), f32),
            pltpu.VMEM((layers, half, depth), jnp.int32),
            pltpu.SemaphoreType.DMA((7,)),
        ],
        4,
        1,
    )(place, *stored)
    source, _ = lax.optimization_barrier((mode_shapes, node))
    operands = [source, lax.ppermute(source, "gy", across), fields, lax.ppermute(fields, "gy", across)]
    straight = [(2 * i + c, 2 * i - 2 + c) for i in range(1, count) for c in (0, 1)]
    crossed = [(2 * i + c, 2 * i - 1 - c) for i in range(1, count) for c in (0, 1)]
    halo = lax.ppermute(node, ("gx", "gy"), straight)
    halo_swap = lax.ppermute(node_crossed, ("gx", "gy"), crossed)

    cuts = (DOWN, layers - UP)

    def energies(name, low, high, *extra):
        end = high == layers
        n = high - low
        outs = (planes(modes * n + end), planes(n))
        return kernel(
            name,
            partial(energy_kernel, low, high, end),
            outs + (planes(2),) if end else outs,
            [smem, smem] + [vmem] * (4 + 2 * end) + [anywhere] * (len(extra) - 2 * end),
            [
                pltpu.VMEM((2, n, width, depth), f32),
                pltpu.VMEM((4, 12, width, depth), f32),
            ],
            12,
            n * 200,
        )(place, eigenvalues, *operands, *extra)

    za, ma = energies("energies_first", 0, cuts[0])
    down = lax.ppermute(za, "gx", downward)
    zb, mb = energies("energies_inner", cuts[0], cuts[1], ma)
    zc, mc, ghost_mass = energies("energies_last", cuts[1], layers, halo, halo_swap, mb)
    up = lax.ppermute(zc, "gx", upward)

    tables = [pltpu.VMEM((layers + 2, width, depth), f32)] * 2
    sums = jax.ShapeDtypeStruct((6 * modes, 8, 128), f32)
    ones_in, twos_in, moments, send = kernel(
        "krylov_main",
        partial(main_kernel, modes, layers, cuts),
        (planes(modes * (layers + 1)), planes(modes * (layers - 1)), sums, planes(modes * 3 * layers, half)),
        [smem] + [vmem] * 8,
        tables + [pltpu.SemaphoreType.DMA((5 * modes,))],
        12,
        400,
    )(place, za, zb, zc, ma, mb, mc, down, ghost_mass)
    ones_left, twos_left, send, parts = kernel(
        "krylov_left",
        partial(left_kernel, modes, layers, cuts),
        (
            planes(2 * modes),
            planes(2 * modes),
            planes(modes * 3 * layers, half),
            jax.ShapeDtypeStruct((2 * count, 8, 128), f32),
        ),
        [smem] + [vmem] * 7,
        tables + [pltpu.VMEM((6 * modes, 8, 128), f32)],
        12,
        200,
        aliases={7: 2},
    )(place, za, ma, up, ones_in, twos_in, moments, send)
    swap_in = lax.ppermute(send, "gy", across)
    parts = lax.all_to_all(parts, ("gx", "gy"), 0, 0, tiled=True)

    return kernel(
        "combine",
        partial(combine_kernel, modes, layers, cuts),
        jax.ShapeDtypeStruct((2 * modes, layers, half, depth), f32),
        [smem] + [vmem] * 9,
        [pltpu.VMEM((2 * modes, layers, half, depth), f32), pltpu.SemaphoreType.DMA((2 * modes,))],
        12,
        100,
        anywhere,
    )(place, parts, za, zb, zc, ones_in, twos_in, ones_left, twos_left, swap_in)


def solution(mesh):
    in_specs = (
        P("grp", "gx", "gy", None),
        P("grp"),
        P(("grp", "gx"), "gy", None),
        P(("grp", "gx"), "gy", None),
        P(("grp", "gx"), "gy", None),
    )
    out_specs = P("grp", "gx", "gy", None)
    return jax.shard_map(local, mesh=mesh, in_specs=in_specs, out_specs=out_specs, check_vma=False)
```

```python
import math
from functools import partial

import jax
import jax.numpy as jnp
import numpy as np
from jax import lax
from jax.experimental import pallas as pl
from jax.experimental.pallas import tpu as pltpu
from jax.sharding import PartitionSpec as P

ITERS = 3
RMIN = 4
RADIUS_SQ = RMIN * RMIN / 12.0
DOWN = 3
UP = 2
ROUNDING = 2.0**-24


void_floor = 0.001


def element_table():
    poisson = 0.3
    lame_first = poisson / ((1.0 + poisson) * (1.0 - 2.0 * poisson))
    shear_mod = 1.0 / (2.0 * (1.0 + poisson))
    elastic = np.zeros((6, 6))
    elastic[:3, :3] = lame_first
    for entry in range(3):
        elastic[entry, entry] += 2.0 * shear_mod
        elastic[entry + 3, entry + 3] = shear_mod
    offset = 1.0 / math.sqrt(3.0)
    gauss_points = [(1.0 - offset) / 2.0, (1.0 + offset) / 2.0]
    stiffness = np.zeros((24, 24))
    inertia = np.zeros((24, 24))
    for point_x in gauss_points:
        for point_y in gauss_points:
            for point_z in gauss_points:
                coords = [point_x, point_y, point_z]
                values = np.zeros(8)
                gradient = np.zeros((8, 3))
                for corner in range(8):
                    corner_bits = [corner % 2, corner // 2 % 2, corner // 4]
                    factors = [
                        coords[dimen] if corner_bits[dimen] else 1.0 - coords[dimen]
                        for dimen in range(3)
                    ]
                    sign_list = [1.0 if corner_bits[dimen] else -1.0 for dimen in range(3)]
                    values[corner] = factors[0] * factors[1] * factors[2]
                    for dimen in range(3):
                        others = [
                            factors[other_dim] for other_dim in range(3) if other_dim != dimen
                        ]
                        gradient[corner, dimen] = sign_list[dimen] * others[0] * others[1]
                strain = np.zeros((6, 24))
                for corner in range(8):
                    column = 3 * corner
                    grad_x, grad_y, grad_z = gradient[corner]
                    strain[0, column] = grad_x
                    strain[1, column + 1] = grad_y
                    strain[2, column + 2] = grad_z
                    strain[3, column] = grad_y
                    strain[3, column + 1] = grad_x
                    strain[4, column + 1] = grad_z
                    strain[4, column + 2] = grad_y
                    strain[5, column] = grad_z
                    strain[5, column + 2] = grad_x
                stiffness += 0.125 * strain.T @ elastic @ strain
                shape_matrix = np.kron(values[None, :], np.eye(3))
                inertia += 0.125 * shape_matrix.T @ shape_matrix
    return stiffness, inertia


def energy_classes():
    stiffness, inertia = element_table()
    pair = np.array([[1.0, 1.0], [-1.0, 1.0]])
    basis = np.kron(np.kron(np.kron(pair, pair), pair), np.eye(3))
    stiffness = basis @ stiffness @ basis.T / 64.0
    inertia = basis @ inertia @ basis.T / 64.0
    squares, products = {}, {}
    for i in range(24):
        key = (round(stiffness[i, i], 9), round(inertia[i, i], 9))
        squares.setdefault(key, []).append(i)
        for j in range(i + 1, 24):
            if abs(stiffness[i, j]) > 1e-9:
                products.setdefault(round(stiffness[i, j], 9), []).append((i, j))
    squares = [
        (float(stiffness[v[0], v[0]]) if abs(k[0]) > 1e-9 else 0.0, float(inertia[v[0], v[0]]), v)
        for k, v in squares.items()
    ]
    products = [(2.0 * float(stiffness[v[0]]), v) for v in products.values()]
    return squares, products


def element_energies(entries, squares, products):
    stiff, inert = None, {}
    for weight, mass, members in squares:
        total = entries[members[0]] * entries[members[0]]
        for i in members[1:]:
            total = total + entries[i] * entries[i]
        if weight:
            stiff = total * weight if stiff is None else stiff + total * weight
        inert[mass] = inert[mass] + total if mass in inert else total
    for weight, members in products:
        a, b = members[0]
        rest = [m for m in members[1:] if a in m]
        if len(members) == 3 and rest:
            (last,) = [m for m in members[1:] if a not in m]
            other = rest[0][0] if rest[0][1] == a else rest[0][1]
            total = entries[a] * (entries[b] + entries[other]) + entries[last[0]] * entries[last[1]]
        else:
            total = entries[a] * entries[b]
            for i, j in members[1:]:
                total = total + entries[i] * entries[j]
        stiff = stiff + weight * total
    return stiff, sum(total * mass for mass, total in inert.items())


def shifted(value, step, dim):
    tile, axis = (8, 0) if dim == 0 else (128, 1)
    count = value.shape[dim] // tile
    parts = [lax.slice_in_dim(value, i * tile, (i + 1) * tile, axis=axis) for i in range(count)]
    rolled = [pltpu.roll(part, (-step) % tile, axis) for part in parts]
    edge = lax.broadcasted_iota(jnp.int32, parts[0].shape, axis) == (tile - 1 if step > 0 else 0)
    result = []
    for i, part in enumerate(rolled):
        beyond = rolled[i + step] if 0 <= i + step < count else 0.0
        result.append(jnp.where(edge, beyond, part))
    return jnp.concatenate(result, axis=axis)


def missing_plane(shape):
    count = jnp.zeros(shape, jnp.float32)
    for dim in (0, 1):
        index = lax.broadcasted_iota(jnp.int32, shape, dim)
        count += (index == 0).astype(jnp.float32) + (index == shape[dim] - 1).astype(jnp.float32)
    return count


def scalar(flag):
    return jnp.where(flag, 1.0, 0.0).astype(jnp.float32)


def neighbour_count(missing, x, layers, first, last):
    count = 6.0 - missing
    if x == 0:
        count -= scalar(first)
    if x == layers - 1:
        count -= scalar(last)
    return count


def halves(core, half):
    return pl.multiple_of(core * half, half), pl.multiple_of((1 - core) * half, half)


def first_kernel(place, modes, density, mass, passive, straight, crossed, fields, signed, flags, sems):
    group = modes.shape[0] // 2
    layers = density.shape[0]
    moves = [(density, signed), (passive, flags), (mass, fields.at[pl.ds(layers, layers)])]
    for target, core in ((straight, place[0]), (crossed, 1 - place[0])):
        moves.append((modes.at[pl.ds(core * group, group), 0], target.at[pl.ds(0, group)]))
    moves.append((mass.at[pl.ds(0, 2)], straight.at[pl.ds(group, 2)]))
    copies = [pltpu.make_async_copy(*move, sems.at[i]) for i, move in enumerate(moves)]
    for copy in copies:
        copy.start()
    for copy in copies[:2]:
        copy.wait()
    for x in range(layers):
        fields[x] = jnp.where(flags[x] == 0, signed[x], -signed[x])
    for copy in copies[2:]:
        copy.wait()


def energy_kernel(low, high, end, *refs):
    place, eig, modes, modes_swap, fields, fields_swap = refs[:6]
    if end:
        halo, halo_swap = refs[6:8]
        z_out, mass_out, ghost_mass, floats, sums = refs[-5:]
    else:
        z_out, mass_out, floats, sums = refs[-4:]
    layers, half, depth = modes.shape[1:]
    group = modes.shape[0] // 2
    width, count = 2 * half, high - low
    core, first, last = place[0], place[1], place[2]
    start = core * group
    lower = core == 0

    def whole(own, other):
        return jnp.concatenate([jnp.where(lower, own, other), jnp.where(lower, other, own)], axis=0)

    squares, products = energy_classes()
    missing = missing_plane((width, depth))
    for i in range(count):
        x = low + i
        weight = whole(fields[layers + x], fields_swap[layers + x])
        mass_out[i] = weight
        inverse = 1.0 / (weight + RADIUS_SQ * neighbour_count(missing, x, layers, first, last))
        rho = whole(fields[x], fields_swap[x])
        design = jnp.where(rho > 0.0, inverse, 0.0)
        floats[0, i] = 3.0 * (1.0 - void_floor) * rho * rho * design
        floats[1, i] = design
    if end:
        z_out[z_out.shape[0] - 1] = mass_out[count - 1]
        for i in (0, 1):
            ghost_mass[i] = halo[group + i]

    def node(row, x):
        if x == layers:
            return whole(halo[row], halo_swap[row])
        return whole(modes[start + row, x], modes_swap[start + row, x])

    ring = sums.shape[0]

    def transform(step):
        mode, i = divmod(step, count + 1)
        for comp in range(3):
            here = node(3 * mode + comp, low + i)
            above = shifted(here, 1, 1)
            for z, value in ((0, here + above), (1, above - here)):
                beside = shifted(value, 1, 0)
                sums[step % ring, 4 * comp + 2 * z] = value + beside
                sums[step % ring, 4 * comp + 2 * z + 1] = beside - value

    def energies(step, value):
        mode, i = divmod(step, count + 1)
        for row in range(0, width, 8):
            for lane in range(0, depth, 128):
                span = (pl.ds(row, 8), pl.ds(lane, 128))
                entries = [None] * 24
                for comp in range(3):
                    for z in (0, 1):
                        for y in (0, 1):
                            near = sums[(step % ring, 4 * comp + 2 * z + y) + span]
                            far = sums[((step + 1) % ring, 4 * comp + 2 * z + y) + span]
                            entries[3 * (2 * y + 4 * z) + comp] = near + far
                            entries[3 * (2 * y + 4 * z + 1) + comp] = far - near
                stiff, inert = element_energies(entries, squares, products)
                result = floats[(0, i) + span] * stiff - (value * floats[(1, i) + span]) * inert
                z_out[(mode * count + i,) + span] = result

    total = group // 3 * (count + 1)
    values = [eig[core * (group // 3) + mode] for mode in range(group // 3)]
    transform(0)
    transform(1)
    for step in range(total):
        if step + 2 < total:
            transform(step + 2)
        if step % (count + 1) < count:
            energies(step, values[step // (count + 1)])


class Layers:
    def __init__(self, *parts):
        self.where = {}
        for low, count, ref, offset, stride in parts:
            for i in range(count):
                self.where[low + i] = (ref, offset + i, stride)

    def __call__(self, mode, x):
        ref, offset, stride = self.where[x]
        return ref[mode * stride + offset]


def krylov_step(place, layers, modes, mass, zeroth, first_in, second_in, first_out, second_out, plan, moments, scratch, unroll=False):
    first, last = place[1], place[2]
    ones, twos, in_0, in_1, in_3, inner, ahead_of = plan
    width, depth = moments.shape[2], None
    inverse, count_of = scratch
    shape = inverse.shape[1:]
    width, depth = shape
    missing = missing_plane(shape)
    slot = {x: i for i, x in enumerate(sorted(set(ones) | set(twos) | set(in_0)))}
    for x, i in slot.items():
        count = neighbour_count(missing, x, layers, first, last)
        count_of[i] = count
        value = 1.0 / (mass(0, x) + RADIUS_SQ * count)
        if x < 0:
            value = value * (1.0 - scalar(first))
        if x >= layers:
            value = value * (1.0 - scalar(last))
        inverse[i] = value

    def apply(field, mode, x):
        here = field(mode, x)
        beside = field(mode, x - 1) + field(mode, x + 1)
        beside += shifted(here, 1, 1) + shifted(here, -1, 1)
        beside += shifted(here, 1, 0) + shifted(here, -1, 0)
        return mass(0, x) * here + RADIUS_SQ * (count_of[slot[x]] * here - beside)

    def fold(value):
        total = None
        for row in range(0, width, 8):
            for lane in range(0, depth, 128):
                piece = value[row : row + 8, lane : lane + 128]
                total = piece if total is None else total + piece
        return total

    row = lax.broadcasted_iota(jnp.int32, shape, 0)
    lane = lax.broadcasted_iota(jnp.int32, shape, 1)

    def one_mode(mode, carry):
        sums = [None] * 6

        def add(k, value):
            sums[k] = fold(value) if sums[k] is None else sums[k] + fold(value)

        for x in in_0:
            here = zeroth(mode, x)
            add(0, here * ((mass(0, x) + RADIUS_SQ * count_of[slot[x]]) * here))
        for x in ones:
            image = apply(zeroth, mode, x)
            one = image * inverse[slot[x]]
            first_out[mode * len(ones) + x - ones[0]] = one
            if x in in_1:
                add(1, zeroth(mode, x) * image)
                add(2, one * image)
        for x in twos:
            image = apply(first_in, mode, x)
            two = image * inverse[slot[x]]
            second_out[mode * len(twos) + x - twos[0]] = two
            if x in in_3:
                add(3, first_in(mode, x) * image)
                add(4, two * image)
        for x in inner:
            here = second_in(mode, x)
            add(5, mass(0, x) * here * here)
            aside = jnp.where(row == width - 1, 0.0, pltpu.roll(here, width - 1, 0) - here)
            above = jnp.where(lane == depth - 1, 0.0, pltpu.roll(here, depth - 1, 1) - here)
            add(5, RADIUS_SQ * (aside * aside + above * above))
        for x in ahead_of:
            edge = second_in(mode, x + 1) - second_in(mode, x)
            if x == layers - 1:
                edge = edge * (1.0 - scalar(last))
            add(5, RADIUS_SQ * (edge * edge))
        for k in range(6):
            if sums[k] is not None:
                moments[mode * 6 + k] = moments[mode * 6 + k] + sums[k]
        return carry

    if unroll:
        for mode in range(modes):
            one_mode(mode, 0)
    else:
        lax.fori_loop(0, modes, one_mode, 0)


def send_halves(target, core, half, modes, parts, sems, used):
    _, other = halves(core, half)
    total = target.shape[0] // modes
    copies = []
    for mode in range(modes):
        for ref, offset, stride, count, at in parts:
            source = ref.at[pl.ds(mode * stride + offset, count), pl.ds(other, half), :]
            sem = sems.at[used + len(copies)]
            copies.append(pltpu.make_async_copy(source, target.at[pl.ds(mode * total + at, count)], sem))
            copies[-1].start()
    return copies


def plans(layers):
    ones, twos = list(range(1, layers + 2)), list(range(2, layers + 1))
    inner = twos[:-1]
    main = (ones, twos, list(range(layers)), list(range(1, layers)), inner, inner, inner)
    left = ([-1, 0], [0, 1], [], [0], [0, 1], [0, 1], [0, 1])
    return main, left


def main_kernel(modes, layers, cuts, place, za, zb, zc, ma, mb, mc, down, ghost_mass, ghost_swap,
                ones, twos, moments, send, inverse, counts, ghosts, sems):
    plan = plans(layers)[0]
    zeroth = z0_layers(cuts, layers, za, zb, zc)
    zeroth.where.update(Layers((layers, DOWN, down, 0, DOWN)).where)
    mass = mass_layers(cuts, layers, ma, mb, mc)
    lower = place[0] == 0
    for i in (0, 1):
        own, other = ghost_mass[i], ghost_swap[i]
        ghosts[i] = jnp.concatenate([jnp.where(lower, own, other), jnp.where(lower, other, own)], axis=0)
    mass.where.update(Layers((layers, 2, ghosts, 0, 0)).where)
    first = Layers((1, layers + 1, ones, 0, layers + 1))
    second = Layers((2, layers - 1, twos, 0, layers - 1))
    moments[...] = jnp.zeros(moments.shape, jnp.float32)
    a, b = cuts
    half = za.shape[1] // 2
    known = [(za, 0, a, a, 0), (zb, 0, b - a, b - a, a), (zc, 0, layers - b, layers - b, b)]
    copies = send_halves(send, place[0], half, modes, known, sems, 0)
    krylov_step(place, layers, modes, mass, zeroth, first, second, ones, twos, plan, moments, (inverse, counts))
    made = [(ones, 0, layers + 1, layers - 1, layers), (twos, 0, layers - 1, layers - 2, 2 * layers - 1)]
    copies += send_halves(send, place[0], half, modes, made, sems, len(copies))
    for copy in copies:
        copy.wait()


def z0_layers(cuts, layers, za, zb, zc):
    a, b = cuts
    return Layers((0, a, za, 0, a), (a, b - a, zb, 0, b - a), (b, layers - b, zc, 0, layers - b))


def mass_layers(cuts, layers, ma, mb, mc):
    a, b = cuts
    return Layers((0, a, ma, 0, 0), (a, b - a, mb, 0, 0), (b, layers - b, mc, 0, 0))


def left_kernel(modes, layers, cuts, place, za, ma, up, ones_in, twos_in, moments_in, _,
                ones, twos, send, parts, inverse, counts, moments):
    plan = plans(layers)[1]
    zeroth = Layers((-UP, UP, up, 0, UP), (0, cuts[0], za, 0, cuts[0]))
    mass = Layers((-1, 1, up, UP * modes, 0), (0, cuts[0], ma, 0, 0))
    first = Layers((-1, 2, ones, 0, 2), (1, layers - 1, ones_in, 0, layers + 1))
    second = Layers((0, 2, twos, 0, 2), (2, layers - 2, twos_in, 0, layers - 1))
    moments[...] = moments_in[...]
    krylov_step(place, layers, modes, mass, zeroth, first, second, ones, twos, plan, moments, (inverse, counts), True)
    half = za.shape[1] // 2
    _, other = halves(place[0], half)
    total = send.shape[0] // modes
    for mode in range(modes):
        at = (mode + 1) * total - 3
        send[at] = ones[2 * mode + 1, pl.ds(other, half), :]
        send[at + 1] = twos[2 * mode, pl.ds(other, half), :]
        send[at + 2] = twos[2 * mode + 1, pl.ds(other, half), :]
    lines = [jnp.sum(moments[i], axis=0, keepdims=True) for i in range(6 * modes)]
    lines = jnp.concatenate(lines + [jnp.zeros((-len(lines) % 8, 128), jnp.float32)], axis=0)
    totals = jnp.sum(lines, axis=1, keepdims=True)
    row = lax.broadcasted_iota(jnp.int32, lines.shape, 0)
    lane = lax.broadcasted_iota(jnp.int32, lines.shape, 1)
    line = jnp.sum(jnp.where(row == lane, totals, 0.0), axis=0, keepdims=True)
    block = jnp.broadcast_to(line, (8, 128))
    for i in range(parts.shape[0]):
        parts[i] = block


def combine_kernel(modes, layers, cuts, place, parts, za, zb, zc, ones_in, twos_in,
                   ones_left, twos_left, swap, out_hbm, out, sems):
    core = place[0]
    half, depth = out.shape[2:]
    mine, _ = halves(core, half)
    shape = (8, 128)
    lane = lax.broadcasted_iota(jnp.int32, shape, 1)
    row = lax.broadcasted_iota(jnp.int32, shape, 0)
    factors = []
    for c in (0, 1):
        block = parts[c]
        for i in range(2 + c, parts.shape[0], 2):
            block = block + parts[i]
        m = [jnp.sum(jnp.where(lane == 6 * row + k, block, 0.0), axis=1, keepdims=True) for k in range(6)]
        inverse = 1.0 / m[1]
        one, two = m[2] * inverse, m[3] * inverse
        pivot = jnp.maximum(m[3] - one * m[2], ROUNDING * m[3])
        cross = m[4] - two * m[2]
        over = 1.0 / pivot
        slope = cross * over
        rest = jnp.maximum(m[5] - two * m[3] - slope * cross, ROUNDING * m[5])
        right_1 = m[1] - one * m[0]
        right_2 = m[2] - two * m[0] - slope * right_1
        c2 = right_2 / rest
        c1 = (right_1 - cross * c2) * over
        c0 = (m[0] - m[2] * c1 - m[3] * c2) * inverse
        factors.append([jnp.broadcast_to(c, (8, depth)) for c in (c0, c1, c2)])

    zeroth = z0_layers(cuts, layers, za, zb, zc)
    first = Layers((0, 1, ones_left, 1, 2), (1, layers - 1, ones_in, 0, layers + 1))
    second = Layers((0, 2, twos_left, 0, 2), (2, layers - 2, twos_in, 0, layers - 1))
    total = swap.shape[0] // modes
    theirs = [
        Layers((0, layers, swap, 0, total)),
        Layers((0, 1, swap, 3 * layers - 3, total), (1, layers - 1, swap, layers, total)),
        Layers((0, 2, swap, 3 * layers - 2, total), (2, layers - 2, swap, 2 * layers - 1, total)),
    ]

    copies = []
    for is_own in (True, False):
        start = (core if is_own else 1 - core) * modes
        first_group = start == 0
        chosen = [jnp.where(first_group, f, g) for f, g in zip(*factors)]
        for mode in range(modes):
            a, b, c = (f[mode : mode + 1] for f in chosen)
            for x in range(layers):
                planes = []
                for field in (zeroth, first, second) if is_own else theirs:
                    ref, offset, stride = field.where[x]
                    rows = pl.ds(mine, half) if is_own else slice(None)
                    planes.append(ref[mode * stride + offset, rows, :])
                out[start + mode, x] = a * planes[0] + b * planes[1] + c * planes[2]
            copy = pltpu.make_async_copy(out.at[start + mode], out_hbm.at[start + mode], sems.at[len(copies)])
            copy.start()
            copies.append(copy)
    for copy in copies:
        copy.wait()


def local(mode_shapes, eigenvalues, density, filter_mass, passive):
    f32 = jnp.float32
    layers, half, depth = density.shape
    group = mode_shapes.shape[0] // 2
    modes = group // 3
    width = 2 * half
    core, at = lax.axis_index("gy"), lax.axis_index("gx")
    count = lax.axis_size("gx")
    place = jnp.stack([core, (at == 0).astype(jnp.int32), (at == count - 1).astype(jnp.int32)]).astype(jnp.int32)
    across = [(0, 1), (1, 0)]
    downward = [(i, i - 1) for i in range(1, count)]
    upward = [(i, i + 1) for i in range(count - 1)]
    smem = pl.BlockSpec(memory_space=pltpu.SMEM)
    vmem = pl.BlockSpec(memory_space=pltpu.VMEM)
    anywhere = pl.BlockSpec(memory_space=pl.ANY)

    def planes(n, rows=width):
        return jax.ShapeDtypeStruct((n, rows, depth), f32)

    def kernel(name, body, outs, in_specs, scratch, limit, work, out_spec=vmem, aliases={}):
        return pl.pallas_call(
            body,
            out_shape=outs,
            in_specs=in_specs,
            out_specs=jax.tree.map(lambda _: out_spec, outs),
            input_output_aliases=aliases,
            scratch_shapes=scratch,
            compiler_params=pltpu.CompilerParams(vmem_limit_bytes=limit * 2**20),
            cost_estimate=pl.CostEstimate(flops=work * 2**20, bytes_accessed=2**20, transcendentals=0),
            name=name,
        )

    stored = [pltpu.with_memory_space_constraint(x, pltpu.HBM) for x in (mode_shapes, density, filter_mass, passive)]
    node, node_crossed, fields = kernel(
        "first_layer",
        first_kernel,
        (planes(group + 2, half), planes(group, half), planes(2 * layers, half)),
        [smem] + [anywhere] * 4,
        [
            pltpu.VMEM((layers, half, depth), f32),
            pltpu.VMEM((layers, half, depth), jnp.int32),
            pltpu.SemaphoreType.DMA((6,)),
        ],
        4,
        1,
    )(place, *stored)
    source, _ = lax.optimization_barrier((mode_shapes, node))
    operands = [source, lax.ppermute(source, "gy", across), fields, lax.ppermute(fields, "gy", across)]
    straight = [(2 * i + c, 2 * i - 2 + c) for i in range(1, count) for c in (0, 1)]
    crossed = [(2 * i + c, 2 * i - 1 - c) for i in range(1, count) for c in (0, 1)]
    halo = lax.ppermute(node, ("gx", "gy"), straight)
    halo_swap = lax.ppermute(node_crossed, ("gx", "gy"), crossed)

    cuts = (DOWN, layers - UP)

    def energies(name, low, high, *extra):
        end = high == layers
        n = high - low
        outs = (planes(modes * n + end), planes(n))
        return kernel(
            name,
            partial(energy_kernel, low, high, end),
            outs + (planes(2, half),) if end else outs,
            [smem, smem] + [vmem] * (4 + 2 * end) + [anywhere] * (len(extra) - 2 * end),
            [
                pltpu.VMEM((2, n, width, depth), f32),
                pltpu.VMEM((4, 12, width, depth), f32),
            ],
            12,
            n * 200,
        )(place, eigenvalues, *operands, *extra)

    za, ma = energies("energies_first", 0, cuts[0])
    down = lax.ppermute(za, "gx", downward)
    zb, mb = energies("energies_inner", cuts[0], cuts[1], ma)
    zc, mc, ghost_mass = energies("energies_last", cuts[1], layers, halo, halo_swap, mb)
    up = lax.ppermute(zc, "gx", upward)
    ghost_swap = lax.ppermute(ghost_mass, "gy", across)

    tables = [pltpu.VMEM((layers + 2, width, depth), f32)] * 2
    sums = jax.ShapeDtypeStruct((6 * modes, 8, 128), f32)
    ones_in, twos_in, moments, send = kernel(
        "krylov_main",
        partial(main_kernel, modes, layers, cuts),
        (planes(modes * (layers + 1)), planes(modes * (layers - 1)), sums, planes(modes * 3 * layers, half)),
        [smem] + [vmem] * 9,
        tables + [pltpu.VMEM((2, width, depth), f32), pltpu.SemaphoreType.DMA((5 * modes,))],
        12,
        400,
    )(place, za, zb, zc, ma, mb, mc, down, ghost_mass, ghost_swap)
    ones_left, twos_left, send, parts = kernel(
        "krylov_left",
        partial(left_kernel, modes, layers, cuts),
        (
            planes(2 * modes),
            planes(2 * modes),
            planes(modes * 3 * layers, half),
            jax.ShapeDtypeStruct((2 * count, 8, 128), f32),
        ),
        [smem] + [vmem] * 7,
        tables + [pltpu.VMEM((6 * modes, 8, 128), f32)],
        12,
        200,
        aliases={7: 2},
    )(place, za, ma, up, ones_in, twos_in, moments, send)
    swap_in = lax.ppermute(send, "gy", across)
    parts = lax.all_to_all(parts, ("gx", "gy"), 0, 0, tiled=True)

    return kernel(
        "combine",
        partial(combine_kernel, modes, layers, cuts),
        jax.ShapeDtypeStruct((2 * modes, layers, half, depth), f32),
        [smem] + [vmem] * 9,
        [pltpu.VMEM((2 * modes, layers, half, depth), f32), pltpu.SemaphoreType.DMA((2 * modes,))],
        12,
        100,
        anywhere,
    )(place, parts, za, zb, zc, ones_in, twos_in, ones_left, twos_left, swap_in)


def solution(mesh):
    in_specs = (
        P("grp", "gx", "gy", None),
        P("grp"),
        P(("grp", "gx"), "gy", None),
        P(("grp", "gx"), "gy", None),
        P(("grp", "gx"), "gy", None),
    )
    out_specs = P("grp", "gx", "gy", None)
    return jax.shard_map(local, mesh=mesh, in_specs=in_specs, out_specs=out_specs, check_vma=False)
```

```python
import math
from functools import partial

import jax
import jax.numpy as jnp
import numpy as np
from jax import lax
from jax.experimental import pallas as pl
from jax.experimental.pallas import tpu as pltpu
from jax.sharding import PartitionSpec as P

ITERS = 3
RMIN = 4
RADIUS_SQ = RMIN * RMIN / 12.0
DOWN = 3
UP = 2
ROUNDING = 2.0**-24


void_floor = 0.001


def element_table():
    poisson = 0.3
    lame_first = poisson / ((1.0 + poisson) * (1.0 - 2.0 * poisson))
    shear_mod = 1.0 / (2.0 * (1.0 + poisson))
    elastic = np.zeros((6, 6))
    elastic[:3, :3] = lame_first
    for entry in range(3):
        elastic[entry, entry] += 2.0 * shear_mod
        elastic[entry + 3, entry + 3] = shear_mod
    offset = 1.0 / math.sqrt(3.0)
    gauss_points = [(1.0 - offset) / 2.0, (1.0 + offset) / 2.0]
    stiffness = np.zeros((24, 24))
    inertia = np.zeros((24, 24))
    for point_x in gauss_points:
        for point_y in gauss_points:
            for point_z in gauss_points:
                coords = [point_x, point_y, point_z]
                values = np.zeros(8)
                gradient = np.zeros((8, 3))
                for corner in range(8):
                    corner_bits = [corner % 2, corner // 2 % 2, corner // 4]
                    factors = [
                        coords[dimen] if corner_bits[dimen] else 1.0 - coords[dimen]
                        for dimen in range(3)
                    ]
                    sign_list = [1.0 if corner_bits[dimen] else -1.0 for dimen in range(3)]
                    values[corner] = factors[0] * factors[1] * factors[2]
                    for dimen in range(3):
                        others = [
                            factors[other_dim] for other_dim in range(3) if other_dim != dimen
                        ]
                        gradient[corner, dimen] = sign_list[dimen] * others[0] * others[1]
                strain = np.zeros((6, 24))
                for corner in range(8):
                    column = 3 * corner
                    grad_x, grad_y, grad_z = gradient[corner]
                    strain[0, column] = grad_x
                    strain[1, column + 1] = grad_y
                    strain[2, column + 2] = grad_z
                    strain[3, column] = grad_y
                    strain[3, column + 1] = grad_x
                    strain[4, column + 1] = grad_z
                    strain[4, column + 2] = grad_y
                    strain[5, column] = grad_z
                    strain[5, column + 2] = grad_x
                stiffness += 0.125 * strain.T @ elastic @ strain
                shape_matrix = np.kron(values[None, :], np.eye(3))
                inertia += 0.125 * shape_matrix.T @ shape_matrix
    return stiffness, inertia


def energy_classes():
    stiffness, inertia = element_table()
    pair = np.array([[1.0, 1.0], [-1.0, 1.0]])
    basis = np.kron(np.kron(np.kron(pair, pair), pair), np.eye(3))
    stiffness = basis @ stiffness @ basis.T / 64.0
    inertia = basis @ inertia @ basis.T / 64.0
    squares, products = {}, {}
    for i in range(24):
        key = (round(stiffness[i, i], 9), round(inertia[i, i], 9))
        squares.setdefault(key, []).append(i)
        for j in range(i + 1, 24):
            if abs(stiffness[i, j]) > 1e-9:
                products.setdefault(round(stiffness[i, j], 9), []).append((i, j))
    squares = [
        (float(stiffness[v[0], v[0]]) if abs(k[0]) > 1e-9 else 0.0, float(inertia[v[0], v[0]]), v)
        for k, v in squares.items()
    ]
    products = [(2.0 * float(stiffness[v[0]]), v) for v in products.values()]
    return squares, products


def element_energies(entries, squares, products):
    stiff, inert = None, {}
    for weight, mass, members in squares:
        total = entries[members[0]] * entries[members[0]]
        for i in members[1:]:
            total = total + entries[i] * entries[i]
        if weight:
            stiff = total * weight if stiff is None else stiff + total * weight
        inert[mass] = inert[mass] + total if mass in inert else total
    for weight, members in products:
        a, b = members[0]
        rest = [m for m in members[1:] if a in m]
        if len(members) == 3 and rest:
            (last,) = [m for m in members[1:] if a not in m]
            other = rest[0][0] if rest[0][1] == a else rest[0][1]
            total = entries[a] * (entries[b] + entries[other]) + entries[last[0]] * entries[last[1]]
        else:
            total = entries[a] * entries[b]
            for i, j in members[1:]:
                total = total + entries[i] * entries[j]
        stiff = stiff + weight * total
    return stiff, sum(total * mass for mass, total in inert.items())


def shifted(value, step, dim):
    tile, axis = (8, 0) if dim == 0 else (128, 1)
    count = value.shape[dim] // tile
    parts = [lax.slice_in_dim(value, i * tile, (i + 1) * tile, axis=axis) for i in range(count)]
    rolled = [pltpu.roll(part, (-step) % tile, axis) for part in parts]
    edge = lax.broadcasted_iota(jnp.int32, parts[0].shape, axis) == (tile - 1 if step > 0 else 0)
    result = []
    for i, part in enumerate(rolled):
        beyond = rolled[i + step] if 0 <= i + step < count else 0.0
        result.append(jnp.where(edge, beyond, part))
    return jnp.concatenate(result, axis=axis)


def missing_plane(shape):
    count = jnp.zeros(shape, jnp.float32)
    for dim in (0, 1):
        index = lax.broadcasted_iota(jnp.int32, shape, dim)
        count += (index == 0).astype(jnp.float32) + (index == shape[dim] - 1).astype(jnp.float32)
    return count


def scalar(flag):
    return jnp.where(flag, 1.0, 0.0).astype(jnp.float32)


def neighbour_count(missing, x, layers, first, last):
    count = 6.0 - missing
    if x == 0:
        count -= scalar(first)
    if x == layers - 1:
        count -= scalar(last)
    return count


def position():
    at = lax.axis_index("gx")
    return lax.axis_index("gy"), at == 0, at == lax.axis_size("gx") - 1


def halves(core, half):
    return pl.multiple_of(core * half, half), pl.multiple_of((1 - core) * half, half)


def first_kernel(modes, density, mass, passive, straight, crossed, fields, own, signed, flags, sems):
    group = modes.shape[0] // 2
    layers = density.shape[0]
    here, _, _ = position()
    moves = [(density, signed), (passive, flags), (mass, fields.at[pl.ds(layers, layers)])]
    for target, core in ((straight, here), (crossed, 1 - here)):
        moves.append((modes.at[pl.ds(core * group, group), 0], target.at[pl.ds(0, group)]))
    moves.append((mass.at[pl.ds(0, 2)], straight.at[pl.ds(group, 2)]))
    moves.append((modes.at[pl.ds(here * group, group)], own))
    copies = [pltpu.make_async_copy(*move, sems.at[i]) for i, move in enumerate(moves)]
    for copy in copies:
        copy.start()
    for copy in copies[:2]:
        copy.wait()
    for x in range(layers):
        fields[x] = jnp.where(flags[x] == 0, signed[x], -signed[x])
    for copy in copies[2:]:
        copy.wait()


def energy_kernel(low, high, end, *refs):
    eig, modes, modes_swap, fields, fields_swap = refs[:5]
    if end:
        halo, halo_swap = refs[5:7]
        z_out, mass_out, ghost_mass, floats, sums = refs[-5:]
    else:
        z_out, mass_out, floats, sums = refs[-4:]
    group, layers, half, depth = modes.shape
    width, count = 2 * half, high - low
    core, first, last = position()
    start = core * group
    lower = core == 0

    def whole(own, other):
        return jnp.concatenate([jnp.where(lower, own, other), jnp.where(lower, other, own)], axis=0)

    squares, products = energy_classes()
    missing = missing_plane((width, depth))
    for i in range(count):
        x = low + i
        weight = whole(fields[layers + x], fields_swap[layers + x])
        mass_out[i] = weight
        inverse = 1.0 / (weight + RADIUS_SQ * neighbour_count(missing, x, layers, first, last))
        rho = whole(fields[x], fields_swap[x])
        design = jnp.where(rho > 0.0, inverse, 0.0)
        floats[0, i] = 3.0 * (1.0 - void_floor) * rho * rho * design
        floats[1, i] = design
    if end:
        z_out[z_out.shape[0] - 1] = mass_out[count - 1]
        for i in (0, 1):
            ghost_mass[i] = halo[group + i]

    def node(row, x):
        if x == layers:
            return whole(halo[row], halo_swap[row])
        return whole(modes[row, x], modes_swap[start + row, x])

    ring = sums.shape[0]

    def transform(step):
        mode, i = divmod(step, count + 1)
        for comp in range(3):
            here = node(3 * mode + comp, low + i)
            above = shifted(here, 1, 1)
            for z, value in ((0, here + above), (1, above - here)):
                beside = shifted(value, 1, 0)
                sums[step % ring, 4 * comp + 2 * z] = value + beside
                sums[step % ring, 4 * comp + 2 * z + 1] = beside - value

    def energies(step, value):
        mode, i = divmod(step, count + 1)
        for row in range(0, width, 8):
            for lane in range(0, depth, 128):
                span = (pl.ds(row, 8), pl.ds(lane, 128))
                entries = [None] * 24
                for comp in range(3):
                    for z in (0, 1):
                        for y in (0, 1):
                            near = sums[(step % ring, 4 * comp + 2 * z + y) + span]
                            far = sums[((step + 1) % ring, 4 * comp + 2 * z + y) + span]
                            entries[3 * (2 * y + 4 * z) + comp] = near + far
                            entries[3 * (2 * y + 4 * z + 1) + comp] = far - near
                stiff, inert = element_energies(entries, squares, products)
                result = floats[(0, i) + span] * stiff - (value * floats[(1, i) + span]) * inert
                z_out[(mode * count + i,) + span] = result

    total = group // 3 * (count + 1)
    each = group // 3
    values = []
    for mode in range(each):
        value = jnp.where(lower, eig[:, mode : mode + 1], eig[:, each + mode : each + mode + 1])
        values.append(jnp.broadcast_to(value, (8, 128)))
    transform(0)
    transform(1)
    for step in range(total):
        if step + 2 < total:
            transform(step + 2)
        if step % (count + 1) < count:
            energies(step, values[step // (count + 1)])


class Layers:
    def __init__(self, *parts):
        self.where = {}
        for low, count, ref, offset, stride in parts:
            for i in range(count):
                self.where[low + i] = (ref, offset + i, stride)

    def __call__(self, mode, x):
        ref, offset, stride = self.where[x]
        return ref[mode * stride + offset]


def krylov_step(layers, modes, mass, zeroth, first_in, second_in, first_out, second_out, plan, moments, scratch, unroll=False):
    _, first, last = position()
    ones, twos, in_0, in_1, in_3, inner, ahead_of = plan
    width, depth = moments.shape[2], None
    inverse, count_of = scratch
    shape = inverse.shape[1:]
    width, depth = shape
    missing = missing_plane(shape)
    slot = {x: i for i, x in enumerate(sorted(set(ones) | set(twos) | set(in_0)))}
    for x, i in slot.items():
        count = neighbour_count(missing, x, layers, first, last)
        count_of[i] = count
        value = 1.0 / (mass(0, x) + RADIUS_SQ * count)
        if x < 0:
            value = value * (1.0 - scalar(first))
        if x >= layers:
            value = value * (1.0 - scalar(last))
        inverse[i] = value

    def apply(field, mode, x):
        here = field(mode, x)
        beside = field(mode, x - 1) + field(mode, x + 1)
        beside += shifted(here, 1, 1) + shifted(here, -1, 1)
        beside += shifted(here, 1, 0) + shifted(here, -1, 0)
        return mass(0, x) * here + RADIUS_SQ * (count_of[slot[x]] * here - beside)

    def fold(value):
        total = None
        for row in range(0, width, 8):
            for lane in range(0, depth, 128):
                piece = value[row : row + 8, lane : lane + 128]
                total = piece if total is None else total + piece
        return total

    row = lax.broadcasted_iota(jnp.int32, shape, 0)
    lane = lax.broadcasted_iota(jnp.int32, shape, 1)

    def one_mode(mode, carry):
        sums = [None] * 6

        def add(k, value):
            sums[k] = fold(value) if sums[k] is None else sums[k] + fold(value)

        for x in in_0:
            here = zeroth(mode, x)
            add(0, here * ((mass(0, x) + RADIUS_SQ * count_of[slot[x]]) * here))
        for x in ones:
            image = apply(zeroth, mode, x)
            one = image * inverse[slot[x]]
            first_out[mode * len(ones) + x - ones[0]] = one
            if x in in_1:
                add(1, zeroth(mode, x) * image)
                add(2, one * image)
        for x in twos:
            image = apply(first_in, mode, x)
            two = image * inverse[slot[x]]
            second_out[mode * len(twos) + x - twos[0]] = two
            if x in in_3:
                add(3, first_in(mode, x) * image)
                add(4, two * image)
        for x in inner:
            here = second_in(mode, x)
            add(5, mass(0, x) * here * here)
            aside = jnp.where(row == width - 1, 0.0, pltpu.roll(here, width - 1, 0) - here)
            above = jnp.where(lane == depth - 1, 0.0, pltpu.roll(here, depth - 1, 1) - here)
            add(5, RADIUS_SQ * (aside * aside + above * above))
        for x in ahead_of:
            edge = second_in(mode, x + 1) - second_in(mode, x)
            if x == layers - 1:
                edge = edge * (1.0 - scalar(last))
            add(5, RADIUS_SQ * (edge * edge))
        for k in range(6):
            if sums[k] is not None:
                moments[mode * 6 + k] = moments[mode * 6 + k] + sums[k]
        return carry

    if unroll:
        for mode in range(modes):
            one_mode(mode, 0)
    else:
        lax.fori_loop(0, modes, one_mode, 0)


def send_halves(target, core, half, modes, parts, sems, used):
    _, other = halves(core, half)
    total = target.shape[0] // modes
    copies = []
    for mode in range(modes):
        for ref, offset, stride, count, at in parts:
            source = ref.at[pl.ds(mode * stride + offset, count), pl.ds(other, half), :]
            sem = sems.at[used + len(copies)]
            copies.append(pltpu.make_async_copy(source, target.at[pl.ds(mode * total + at, count)], sem))
            copies[-1].start()
    return copies


def plans(layers):
    ones, twos = list(range(1, layers + 2)), list(range(2, layers + 1))
    inner = twos[:-1]
    main = (ones, twos, list(range(layers)), list(range(1, layers)), inner, inner, inner)
    left = ([-1, 0], [0, 1], [], [0], [0, 1], [0, 1], [0, 1])
    return main, left


def main_kernel(modes, layers, cuts, za, zb, zc, ma, mb, mc, down, ghost_mass, ghost_swap,
                ones, twos, moments, send, inverse, counts, ghosts, sems):
    plan = plans(layers)[0]
    zeroth = z0_layers(cuts, layers, za, zb, zc)
    zeroth.where.update(Layers((layers, DOWN, down, 0, DOWN)).where)
    mass = mass_layers(cuts, layers, ma, mb, mc)
    core, _, _ = position()
    lower = core == 0
    for i in (0, 1):
        own, other = ghost_mass[i], ghost_swap[i]
        ghosts[i] = jnp.concatenate([jnp.where(lower, own, other), jnp.where(lower, other, own)], axis=0)
    mass.where.update(Layers((layers, 2, ghosts, 0, 0)).where)
    first = Layers((1, layers + 1, ones, 0, layers + 1))
    second = Layers((2, layers - 1, twos, 0, layers - 1))
    moments[...] = jnp.zeros(moments.shape, jnp.float32)
    a, b = cuts
    half = za.shape[1] // 2
    known = [(za, 0, a, a, 0), (zb, 0, b - a, b - a, a), (zc, 0, layers - b, layers - b, b)]
    copies = send_halves(send, core, half, modes, known, sems, 0)
    krylov_step(layers, modes, mass, zeroth, first, second, ones, twos, plan, moments, (inverse, counts))
    made = [(ones, 0, layers + 1, layers - 1, layers), (twos, 0, layers - 1, layers - 2, 2 * layers - 1)]
    copies += send_halves(send, core, half, modes, made, sems, len(copies))
    for copy in copies:
        copy.wait()


def z0_layers(cuts, layers, za, zb, zc):
    a, b = cuts
    return Layers((0, a, za, 0, a), (a, b - a, zb, 0, b - a), (b, layers - b, zc, 0, layers - b))


def mass_layers(cuts, layers, ma, mb, mc):
    a, b = cuts
    return Layers((0, a, ma, 0, 0), (a, b - a, mb, 0, 0), (b, layers - b, mc, 0, 0))


def left_kernel(modes, layers, cuts, za, ma, up, ones_in, twos_in, moments_in, _,
                ones, twos, send, parts, inverse, counts, moments):
    plan = plans(layers)[1]
    zeroth = Layers((-UP, UP, up, 0, UP), (0, cuts[0], za, 0, cuts[0]))
    mass = Layers((-1, 1, up, UP * modes, 0), (0, cuts[0], ma, 0, 0))
    first = Layers((-1, 2, ones, 0, 2), (1, layers - 1, ones_in, 0, layers + 1))
    second = Layers((0, 2, twos, 0, 2), (2, layers - 2, twos_in, 0, layers - 1))
    moments[...] = moments_in[...]
    krylov_step(layers, modes, mass, zeroth, first, second, ones, twos, plan, moments, (inverse, counts), True)
    half = za.shape[1] // 2
    core, _, _ = position()
    _, other = halves(core, half)
    total = send.shape[0] // modes
    for mode in range(modes):
        at = (mode + 1) * total - 3
        send[at] = ones[2 * mode + 1, pl.ds(other, half), :]
        send[at + 1] = twos[2 * mode, pl.ds(other, half), :]
        send[at + 2] = twos[2 * mode + 1, pl.ds(other, half), :]
    row = lax.broadcasted_iota(jnp.int32, (8, 128), 0)
    lane = lax.broadcasted_iota(jnp.int32, (8, 128), 1)
    rows = []
    for mode in range(modes):
        lines = [jnp.sum(moments[6 * mode + k], axis=0, keepdims=True) for k in range(6)]
        totals = jnp.sum(jnp.concatenate(lines + [jnp.zeros((2, 128), jnp.float32)], axis=0), axis=1, keepdims=True)
        rows.append(jnp.sum(jnp.where(row == lane, totals, 0.0), axis=0, keepdims=True))
    block = jnp.concatenate(rows + [jnp.zeros((8 - modes, 128), jnp.float32)], axis=0)
    for i in range(parts.shape[0]):
        parts[i] = block


def combine_kernel(modes, layers, cuts, parts, za, zb, zc, ones_in, twos_in,
                   ones_left, twos_left, swap, out_hbm, out, sems):
    core, _, _ = position()
    half, depth = out.shape[2:]
    mine, _ = halves(core, half)
    blocks = []
    for c in (0, 1):
        block = parts[c]
        for i in range(2 + c, parts.shape[0], 2):
            block = block + parts[i]
        blocks.append(block)
    both = jnp.concatenate(blocks, axis=0)
    m = [jnp.broadcast_to(both[:, k : k + 1], both.shape) for k in range(6)]
    inverse = 1.0 / m[1]
    one, two = m[2] * inverse, m[3] * inverse
    pivot = jnp.maximum(m[3] - one * m[2], ROUNDING * m[3])
    cross = m[4] - two * m[2]
    over = 1.0 / pivot
    slope = cross * over
    rest = jnp.maximum(m[5] - two * m[3] - slope * cross, ROUNDING * m[5])
    right_1 = m[1] - one * m[0]
    right_2 = m[2] - two * m[0] - slope * right_1
    c2 = right_2 / rest
    c1 = (right_1 - cross * c2) * over
    c0 = (m[0] - m[2] * c1 - m[3] * c2) * inverse
    wide = [jnp.concatenate([c] * (depth // 128), axis=1) for c in (c0, c1, c2)]

    zeroth = z0_layers(cuts, layers, za, zb, zc)
    first = Layers((0, 1, ones_left, 1, 2), (1, layers - 1, ones_in, 0, layers + 1))
    second = Layers((0, 2, twos_left, 0, 2), (2, layers - 2, twos_in, 0, layers - 1))
    total = swap.shape[0] // modes
    theirs = [
        Layers((0, layers, swap, 0, total)),
        Layers((0, 1, swap, 3 * layers - 3, total), (1, layers - 1, swap, layers, total)),
        Layers((0, 2, swap, 3 * layers - 2, total), (2, layers - 2, swap, 2 * layers - 1, total)),
    ]

    copies = []
    for is_own in (True, False):
        start = (core if is_own else 1 - core) * modes
        first_group = start == 0
        chosen = [jnp.where(first_group, c[:8], c[8:]) for c in wide]
        for mode in range(modes):
            a, b, c = (f[mode : mode + 1] for f in chosen)
            for x in range(layers):
                planes = []
                for field in (zeroth, first, second) if is_own else theirs:
                    ref, offset, stride = field.where[x]
                    rows = pl.ds(mine, half) if is_own else slice(None)
                    planes.append(ref[mode * stride + offset, rows, :])
                out[start + mode, x] = a * planes[0] + b * planes[1] + c * planes[2]
            copy = pltpu.make_async_copy(out.at[start + mode], out_hbm.at[start + mode], sems.at[len(copies)])
            copy.start()
            copies.append(copy)
    for copy in copies:
        copy.wait()


def local(mode_shapes, eigenvalues, density, filter_mass, passive):
    f32 = jnp.float32
    layers, half, depth = density.shape
    group = mode_shapes.shape[0] // 2
    modes = group // 3
    width = 2 * half
    count = lax.axis_size("gx")
    across = [(0, 1), (1, 0)]
    downward = [(i, i - 1) for i in range(1, count)]
    upward = [(i, i + 1) for i in range(count - 1)]
    vmem = pl.BlockSpec(memory_space=pltpu.VMEM)
    anywhere = pl.BlockSpec(memory_space=pl.ANY)

    def planes(n, rows=width):
        return jax.ShapeDtypeStruct((n, rows, depth), f32)

    def kernel(name, body, outs, in_specs, scratch, limit, work, out_spec=vmem, aliases={}):
        return pl.pallas_call(
            body,
            out_shape=outs,
            in_specs=in_specs,
            out_specs=jax.tree.map(lambda _: out_spec, outs),
            input_output_aliases=aliases,
            scratch_shapes=scratch,
            compiler_params=pltpu.CompilerParams(vmem_limit_bytes=limit * 2**20),
            cost_estimate=pl.CostEstimate(flops=work * 2**20, bytes_accessed=2**20, transcendentals=0),
            name=name,
        )

    stored = [pltpu.with_memory_space_constraint(x, pltpu.HBM) for x in (mode_shapes, density, filter_mass, passive)]
    node, node_crossed, fields, own = kernel(
        "first_layer",
        first_kernel,
        (
            planes(group + 2, half),
            planes(group, half),
            planes(2 * layers, half),
            jax.ShapeDtypeStruct((group, layers, half, depth), f32),
        ),
        [anywhere] * 4,
        [
            pltpu.VMEM((layers, half, depth), f32),
            pltpu.VMEM((layers, half, depth), jnp.int32),
            pltpu.SemaphoreType.DMA((7,)),
        ],
        4,
        1,
    )(*stored)
    operands = [own, lax.ppermute(mode_shapes, "gy", across), fields, lax.ppermute(fields, "gy", across)]
    straight = [(2 * i + c, 2 * i - 2 + c) for i in range(1, count) for c in (0, 1)]
    crossed = [(2 * i + c, 2 * i - 1 - c) for i in range(1, count) for c in (0, 1)]
    halo = lax.ppermute(node, ("gx", "gy"), straight)
    halo_swap = lax.ppermute(node_crossed, ("gx", "gy"), crossed)

    cuts = (DOWN, layers - UP)

    def energies(name, low, high, *extra):
        end = high == layers
        n = high - low
        outs = (planes(modes * n + end), planes(n))
        return kernel(
            name,
            partial(energy_kernel, low, high, end),
            outs + (planes(2, half),) if end else outs,
            [vmem] * (5 + 2 * end) + [anywhere] * (len(extra) - 2 * end),
            [
                pltpu.VMEM((2, n, width, depth), f32),
                pltpu.VMEM((4, 12, width, depth), f32),
            ],
            12,
            n * 200,
        )(eigenvalues[None], *operands, *extra)

    za, ma = energies("energies_first", 0, cuts[0])
    down = lax.ppermute(za, "gx", downward)
    zb, mb = energies("energies_inner", cuts[0], cuts[1], ma)
    zc, mc, ghost_mass = energies("energies_last", cuts[1], layers, halo, halo_swap, mb)
    up = lax.ppermute(zc, "gx", upward)
    ghost_swap = lax.ppermute(ghost_mass, "gy", across)

    tables = [pltpu.VMEM((layers + 2, width, depth), f32)] * 2
    sums = jax.ShapeDtypeStruct((6 * modes, 8, 128), f32)
    ones_in, twos_in, moments, send = kernel(
        "krylov_main",
        partial(main_kernel, modes, layers, cuts),
        (planes(modes * (layers + 1)), planes(modes * (layers - 1)), sums, planes(modes * 3 * layers, half)),
        [vmem] * 9,
        tables + [pltpu.VMEM((2, width, depth), f32), pltpu.SemaphoreType.DMA((5 * modes,))],
        12,
        400,
    )(za, zb, zc, ma, mb, mc, down, ghost_mass, ghost_swap)
    ones_left, twos_left, send, parts = kernel(
        "krylov_left",
        partial(left_kernel, modes, layers, cuts),
        (
            planes(2 * modes),
            planes(2 * modes),
            planes(modes * 3 * layers, half),
            jax.ShapeDtypeStruct((2 * count, 8, 128), f32),
        ),
        [vmem] * 7,
        tables + [pltpu.VMEM((6 * modes, 8, 128), f32)],
        12,
        200,
        aliases={6: 2},
    )(za, ma, up, ones_in, twos_in, moments, send)
    swap_in = lax.ppermute(send, "gy", across)
    parts = lax.all_to_all(parts, ("gx", "gy"), 0, 0, tiled=True)

    return kernel(
        "combine",
        partial(combine_kernel, modes, layers, cuts),
        jax.ShapeDtypeStruct((2 * modes, layers, half, depth), f32),
        [vmem] * 9,
        [pltpu.VMEM((2 * modes, layers, half, depth), f32), pltpu.SemaphoreType.DMA((2 * modes,))],
        12,
        100,
        anywhere,
    )(parts, za, zb, zc, ones_in, twos_in, ones_left, twos_left, swap_in)


def solution(mesh):
    in_specs = (
        P("grp", "gx", "gy", None),
        P("grp"),
        P(("grp", "gx"), "gy", None),
        P(("grp", "gx"), "gy", None),
        P(("grp", "gx"), "gy", None),
    )
    out_specs = P("grp", "gx", "gy", None)
    return jax.shard_map(local, mesh=mesh, in_specs=in_specs, out_specs=out_specs, check_vma=False)
```

```python
import math
from functools import partial

import jax
import jax.numpy as jnp
import numpy as np
from jax import lax
from jax.experimental import pallas as pl
from jax.experimental.pallas import tpu as pltpu
from jax.sharding import PartitionSpec as P

ITERS = 3
RMIN = 4
RADIUS_SQ = RMIN * RMIN / 12.0
DOWN = 3
UP = 2
ROUNDING = 2.0**-24


void_floor = 0.001


def element_table():
    poisson = 0.3
    lame_first = poisson / ((1.0 + poisson) * (1.0 - 2.0 * poisson))
    shear_mod = 1.0 / (2.0 * (1.0 + poisson))
    elastic = np.zeros((6, 6))
    elastic[:3, :3] = lame_first
    for entry in range(3):
        elastic[entry, entry] += 2.0 * shear_mod
        elastic[entry + 3, entry + 3] = shear_mod
    offset = 1.0 / math.sqrt(3.0)
    gauss_points = [(1.0 - offset) / 2.0, (1.0 + offset) / 2.0]
    stiffness = np.zeros((24, 24))
    inertia = np.zeros((24, 24))
    for point_x in gauss_points:
        for point_y in gauss_points:
            for point_z in gauss_points:
                coords = [point_x, point_y, point_z]
                values = np.zeros(8)
                gradient = np.zeros((8, 3))
                for corner in range(8):
                    corner_bits = [corner % 2, corner // 2 % 2, corner // 4]
                    factors = [
                        coords[dimen] if corner_bits[dimen] else 1.0 - coords[dimen]
                        for dimen in range(3)
                    ]
                    sign_list = [1.0 if corner_bits[dimen] else -1.0 for dimen in range(3)]
                    values[corner] = factors[0] * factors[1] * factors[2]
                    for dimen in range(3):
                        others = [
                            factors[other_dim] for other_dim in range(3) if other_dim != dimen
                        ]
                        gradient[corner, dimen] = sign_list[dimen] * others[0] * others[1]
                strain = np.zeros((6, 24))
                for corner in range(8):
                    column = 3 * corner
                    grad_x, grad_y, grad_z = gradient[corner]
                    strain[0, column] = grad_x
                    strain[1, column + 1] = grad_y
                    strain[2, column + 2] = grad_z
                    strain[3, column] = grad_y
                    strain[3, column + 1] = grad_x
                    strain[4, column + 1] = grad_z
                    strain[4, column + 2] = grad_y
                    strain[5, column] = grad_z
                    strain[5, column + 2] = grad_x
                stiffness += 0.125 * strain.T @ elastic @ strain
                shape_matrix = np.kron(values[None, :], np.eye(3))
                inertia += 0.125 * shape_matrix.T @ shape_matrix
    return stiffness, inertia


def energy_classes():
    stiffness, inertia = element_table()
    pair = np.array([[1.0, 1.0], [-1.0, 1.0]])
    basis = np.kron(np.kron(np.kron(pair, pair), pair), np.eye(3))
    stiffness = basis @ stiffness @ basis.T / 64.0
    inertia = basis @ inertia @ basis.T / 64.0
    squares, products = {}, {}
    for i in range(24):
        key = (round(stiffness[i, i], 9), round(inertia[i, i], 9))
        squares.setdefault(key, []).append(i)
        for j in range(i + 1, 24):
            if abs(stiffness[i, j]) > 1e-9:
                products.setdefault(round(stiffness[i, j], 9), []).append((i, j))
    squares = [
        (float(stiffness[v[0], v[0]]) if abs(k[0]) > 1e-9 else 0.0, float(inertia[v[0], v[0]]), v)
        for k, v in squares.items()
    ]
    products = [(2.0 * float(stiffness[v[0]]), v) for v in products.values()]
    return squares, products


def element_energies(entries, squares, products):
    stiff, inert = None, {}
    for weight, mass, members in squares:
        total = entries[members[0]] * entries[members[0]]
        for i in members[1:]:
            total = total + entries[i] * entries[i]
        if weight:
            stiff = total * weight if stiff is None else stiff + total * weight
        inert[mass] = inert[mass] + total if mass in inert else total
    for weight, members in products:
        a, b = members[0]
        rest = [m for m in members[1:] if a in m]
        if len(members) == 3 and rest:
            (last,) = [m for m in members[1:] if a not in m]
            other = rest[0][0] if rest[0][1] == a else rest[0][1]
            total = entries[a] * (entries[b] + entries[other]) + entries[last[0]] * entries[last[1]]
        else:
            total = entries[a] * entries[b]
            for i, j in members[1:]:
                total = total + entries[i] * entries[j]
        stiff = stiff + weight * total
    return stiff, sum(total * mass for mass, total in inert.items())


def shifted(value, step, dim):
    tile, axis = (8, 0) if dim == 0 else (128, 1)
    count = value.shape[dim] // tile
    parts = [lax.slice_in_dim(value, i * tile, (i + 1) * tile, axis=axis) for i in range(count)]
    rolled = [pltpu.roll(part, (-step) % tile, axis) for part in parts]
    edge = lax.broadcasted_iota(jnp.int32, parts[0].shape, axis) == (tile - 1 if step > 0 else 0)
    result = []
    for i, part in enumerate(rolled):
        beyond = rolled[i + step] if 0 <= i + step < count else 0.0
        result.append(jnp.where(edge, beyond, part))
    return jnp.concatenate(result, axis=axis)


def missing_plane(shape):
    count = jnp.zeros(shape, jnp.float32)
    for dim in (0, 1):
        index = lax.broadcasted_iota(jnp.int32, shape, dim)
        count += (index == 0).astype(jnp.float32) + (index == shape[dim] - 1).astype(jnp.float32)
    return count


def scalar(flag):
    return jnp.where(flag, 1.0, 0.0).astype(jnp.float32)


def neighbour_count(missing, x, layers, first, last):
    count = 6.0 - missing
    if x == 0:
        count -= scalar(first)
    if x == layers - 1:
        count -= scalar(last)
    return count


def position():
    at = lax.axis_index("gx")
    return lax.axis_index("gy"), at == 0, at == lax.axis_size("gx") - 1


def halves(core, half):
    return pl.multiple_of(core * half, half), pl.multiple_of((1 - core) * half, half)


def first_kernel(modes, density, mass, passive, straight, crossed, fields, signed, flags, sems):
    group = modes.shape[0] // 2
    layers = density.shape[0]
    here, _, _ = position()
    moves = [(density, signed), (passive, flags), (mass, fields.at[pl.ds(layers, layers)])]
    for target, core in ((straight, here), (crossed, 1 - here)):
        moves.append((modes.at[pl.ds(core * group, group), 0], target.at[pl.ds(0, group)]))
    moves.append((mass.at[pl.ds(0, 2)], straight.at[pl.ds(group, 2)]))
    copies = [pltpu.make_async_copy(*move, sems.at[i]) for i, move in enumerate(moves)]
    for copy in copies:
        copy.start()
    for copy in copies[:2]:
        copy.wait()
    for x in range(layers):
        fields[x] = jnp.where(flags[x] == 0, signed[x], -signed[x])
    for copy in copies[2:]:
        copy.wait()


def energy_kernel(low, high, end, *refs):
    eig, modes, modes_swap, fields, fields_swap = refs[:5]
    if end:
        halo, halo_swap = refs[5:7]
        z_out, mass_out, ghost_mass, floats, sums = refs[-5:]
    else:
        z_out, mass_out, floats, sums = refs[-4:]
    layers, half, depth = modes.shape[1:]
    group = modes.shape[0] // 2
    width, count = 2 * half, high - low
    core, first, last = position()
    start = core * group
    lower = core == 0

    def whole(own, other):
        return jnp.concatenate([jnp.where(lower, own, other), jnp.where(lower, other, own)], axis=0)

    squares, products = energy_classes()
    missing = missing_plane((width, depth))
    for i in range(count):
        x = low + i
        weight = whole(fields[layers + x], fields_swap[layers + x])
        mass_out[i] = weight
        inverse = 1.0 / (weight + RADIUS_SQ * neighbour_count(missing, x, layers, first, last))
        rho = whole(fields[x], fields_swap[x])
        design = jnp.where(rho > 0.0, inverse, 0.0)
        floats[0, i] = 3.0 * (1.0 - void_floor) * rho * rho * design
        floats[1, i] = design
    if end:
        z_out[z_out.shape[0] - 1] = mass_out[count - 1]
        for i in (0, 1):
            ghost_mass[i] = halo[group + i]

    def node(row, x):
        if x == layers:
            return whole(halo[row], halo_swap[row])
        return whole(modes[start + row, x], modes_swap[start + row, x])

    ring = sums.shape[0]

    def transform(step):
        mode, i = divmod(step, count + 1)
        for comp in range(3):
            here = node(3 * mode + comp, low + i)
            above = shifted(here, 1, 1)
            for z, value in ((0, here + above), (1, above - here)):
                beside = shifted(value, 1, 0)
                sums[step % ring, 4 * comp + 2 * z] = value + beside
                sums[step % ring, 4 * comp + 2 * z + 1] = beside - value

    def energies(step, value):
        mode, i = divmod(step, count + 1)
        for row in range(0, width, 8):
            for lane in range(0, depth, 128):
                span = (pl.ds(row, 8), pl.ds(lane, 128))
                entries = [None] * 24
                for comp in range(3):
                    for z in (0, 1):
                        for y in (0, 1):
                            near = sums[(step % ring, 4 * comp + 2 * z + y) + span]
                            far = sums[((step + 1) % ring, 4 * comp + 2 * z + y) + span]
                            entries[3 * (2 * y + 4 * z) + comp] = near + far
                            entries[3 * (2 * y + 4 * z + 1) + comp] = far - near
                stiff, inert = element_energies(entries, squares, products)
                result = floats[(0, i) + span] * stiff - (value * floats[(1, i) + span]) * inert
                z_out[(mode * count + i,) + span] = result

    total = group // 3 * (count + 1)
    each = group // 3
    values = []
    for mode in range(each):
        value = jnp.where(lower, eig[:, mode : mode + 1], eig[:, each + mode : each + mode + 1])
        values.append(jnp.broadcast_to(value, (8, 128)))
    transform(0)
    transform(1)
    for step in range(total):
        if step + 2 < total:
            transform(step + 2)
        if step % (count + 1) < count:
            energies(step, values[step // (count + 1)])


class Layers:
    def __init__(self, *parts):
        self.where = {}
        for low, count, ref, offset, stride in parts:
            for i in range(count):
                self.where[low + i] = (ref, offset + i, stride)

    def __call__(self, mode, x):
        ref, offset, stride = self.where[x]
        return ref[mode * stride + offset]


def krylov_step(layers, modes, mass, zeroth, first_in, second_in, first_out, second_out, plan, moments, scratch, unroll=False):
    _, first, last = position()
    ones, twos, in_0, in_1, in_3, inner, ahead_of = plan
    width, depth = moments.shape[2], None
    inverse, count_of = scratch
    shape = inverse.shape[1:]
    width, depth = shape
    missing = missing_plane(shape)
    slot = {x: i for i, x in enumerate(sorted(set(ones) | set(twos) | set(in_0)))}
    for x, i in slot.items():
        count = neighbour_count(missing, x, layers, first, last)
        count_of[i] = count
        value = 1.0 / (mass(0, x) + RADIUS_SQ * count)
        if x < 0:
            value = value * (1.0 - scalar(first))
        if x >= layers:
            value = value * (1.0 - scalar(last))
        inverse[i] = value

    def apply(field, mode, x):
        here = field(mode, x)
        beside = field(mode, x - 1) + field(mode, x + 1)
        beside += shifted(here, 1, 1) + shifted(here, -1, 1)
        beside += shifted(here, 1, 0) + shifted(here, -1, 0)
        return mass(0, x) * here + RADIUS_SQ * (count_of[slot[x]] * here - beside)

    def fold(value):
        total = None
        for row in range(0, width, 8):
            for lane in range(0, depth, 128):
                piece = value[row : row + 8, lane : lane + 128]
                total = piece if total is None else total + piece
        return total

    row = lax.broadcasted_iota(jnp.int32, shape, 0)
    lane = lax.broadcasted_iota(jnp.int32, shape, 1)

    def one_mode(mode, carry):
        sums = [None] * 6

        def add(k, value):
            sums[k] = fold(value) if sums[k] is None else sums[k] + fold(value)

        for x in in_0:
            here = zeroth(mode, x)
            add(0, here * ((mass(0, x) + RADIUS_SQ * count_of[slot[x]]) * here))
        for x in ones:
            image = apply(zeroth, mode, x)
            one = image * inverse[slot[x]]
            first_out[mode * len(ones) + x - ones[0]] = one
            if x in in_1:
                add(1, zeroth(mode, x) * image)
                add(2, one * image)
        for x in twos:
            image = apply(first_in, mode, x)
            two = image * inverse[slot[x]]
            second_out[mode * len(twos) + x - twos[0]] = two
            if x in in_3:
                add(3, first_in(mode, x) * image)
                add(4, two * image)
        for x in inner:
            here = second_in(mode, x)
            add(5, mass(0, x) * here * here)
            aside = jnp.where(row == width - 1, 0.0, pltpu.roll(here, width - 1, 0) - here)
            above = jnp.where(lane == depth - 1, 0.0, pltpu.roll(here, depth - 1, 1) - here)
            add(5, RADIUS_SQ * (aside * aside + above * above))
        for x in ahead_of:
            edge = second_in(mode, x + 1) - second_in(mode, x)
            if x == layers - 1:
                edge = edge * (1.0 - scalar(last))
            add(5, RADIUS_SQ * (edge * edge))
        for k in range(6):
            if sums[k] is not None:
                moments[mode * 6 + k] = moments[mode * 6 + k] + sums[k]
        return carry

    if unroll:
        for mode in range(modes):
            one_mode(mode, 0)
    else:
        lax.fori_loop(0, modes, one_mode, 0)


def send_halves(target, core, half, modes, parts, sems, used):
    _, other = halves(core, half)
    total = target.shape[0] // modes
    copies = []
    for mode in range(modes):
        for ref, offset, stride, count, at in parts:
            source = ref.at[pl.ds(mode * stride + offset, count), pl.ds(other, half), :]
            sem = sems.at[used + len(copies)]
            copies.append(pltpu.make_async_copy(source, target.at[pl.ds(mode * total + at, count)], sem))
            copies[-1].start()
    return copies


def plans(layers):
    ones, twos = list(range(1, layers + 2)), list(range(2, layers + 1))
    inner = twos[:-1]
    main = (ones, twos, list(range(layers)), list(range(1, layers)), inner, inner, inner)
    left = ([-1, 0], [0, 1], [], [0], [0, 1], [0, 1], [0, 1])
    return main, left


def main_kernel(modes, layers, cuts, za, zb, zc, ma, mb, mc, down, ghost_mass, ghost_swap,
                ones, twos, moments, send, inverse, counts, ghosts, sems):
    plan = plans(layers)[0]
    zeroth = z0_layers(cuts, layers, za, zb, zc)
    zeroth.where.update(Layers((layers, DOWN, down, 0, DOWN)).where)
    mass = mass_layers(cuts, layers, ma, mb, mc)
    core, _, _ = position()
    lower = core == 0
    for i in (0, 1):
        own, other = ghost_mass[i], ghost_swap[i]
        ghosts[i] = jnp.concatenate([jnp.where(lower, own, other), jnp.where(lower, other, own)], axis=0)
    mass.where.update(Layers((layers, 2, ghosts, 0, 0)).where)
    first = Layers((1, layers + 1, ones, 0, layers + 1))
    second = Layers((2, layers - 1, twos, 0, layers - 1))
    moments[...] = jnp.zeros(moments.shape, jnp.float32)
    a, b = cuts
    half = za.shape[1] // 2
    known = [(za, 0, a, a, 0), (zb, 0, b - a, b - a, a), (zc, 0, layers - b, layers - b, b)]
    copies = send_halves(send, core, half, modes, known, sems, 0)
    krylov_step(layers, modes, mass, zeroth, first, second, ones, twos, plan, moments, (inverse, counts))
    made = [(ones, 0, layers + 1, layers - 1, layers), (twos, 0, layers - 1, layers - 2, 2 * layers - 1)]
    copies += send_halves(send, core, half, modes, made, sems, len(copies))
    for copy in copies:
        copy.wait()


def z0_layers(cuts, layers, za, zb, zc):
    a, b = cuts
    return Layers((0, a, za, 0, a), (a, b - a, zb, 0, b - a), (b, layers - b, zc, 0, layers - b))


def mass_layers(cuts, layers, ma, mb, mc):
    a, b = cuts
    return Layers((0, a, ma, 0, 0), (a, b - a, mb, 0, 0), (b, layers - b, mc, 0, 0))


def left_kernel(modes, layers, cuts, za, ma, up, ones_in, twos_in, moments_in, _,
                ones, twos, send, parts, inverse, counts, moments):
    plan = plans(layers)[1]
    zeroth = Layers((-UP, UP, up, 0, UP), (0, cuts[0], za, 0, cuts[0]))
    mass = Layers((-1, 1, up, UP * modes, 0), (0, cuts[0], ma, 0, 0))
    first = Layers((-1, 2, ones, 0, 2), (1, layers - 1, ones_in, 0, layers + 1))
    second = Layers((0, 2, twos, 0, 2), (2, layers - 2, twos_in, 0, layers - 1))
    moments[...] = moments_in[...]
    krylov_step(layers, modes, mass, zeroth, first, second, ones, twos, plan, moments, (inverse, counts), True)
    half = za.shape[1] // 2
    core, _, _ = position()
    _, other = halves(core, half)
    total = send.shape[0] // modes
    for mode in range(modes):
        at = (mode + 1) * total - 3
        send[at] = ones[2 * mode + 1, pl.ds(other, half), :]
        send[at + 1] = twos[2 * mode, pl.ds(other, half), :]
        send[at + 2] = twos[2 * mode + 1, pl.ds(other, half), :]
    row = lax.broadcasted_iota(jnp.int32, (8, 128), 0)
    lane = lax.broadcasted_iota(jnp.int32, (8, 128), 1)
    rows = []
    for mode in range(modes):
        lines = [jnp.sum(moments[6 * mode + k], axis=0, keepdims=True) for k in range(6)]
        totals = jnp.sum(jnp.concatenate(lines + [jnp.zeros((2, 128), jnp.float32)], axis=0), axis=1, keepdims=True)
        rows.append(jnp.sum(jnp.where(row == lane, totals, 0.0), axis=0, keepdims=True))
    block = jnp.concatenate(rows + [jnp.zeros((8 - modes, 128), jnp.float32)], axis=0)
    for i in range(parts.shape[0]):
        parts[i] = block


def combine_kernel(modes, layers, cuts, parts, za, zb, zc, ones_in, twos_in,
                   ones_left, twos_left, swap, out_hbm, out, sems):
    core, _, _ = position()
    half, depth = out.shape[2:]
    mine, _ = halves(core, half)
    blocks = []
    for c in (0, 1):
        block = parts[c]
        for i in range(2 + c, parts.shape[0], 2):
            block = block + parts[i]
        blocks.append(block)
    both = jnp.concatenate(blocks, axis=0)
    m = [jnp.broadcast_to(both[:, k : k + 1], both.shape) for k in range(6)]
    inverse = 1.0 / m[1]
    one, two = m[2] * inverse, m[3] * inverse
    pivot = jnp.maximum(m[3] - one * m[2], ROUNDING * m[3])
    cross = m[4] - two * m[2]
    over = 1.0 / pivot
    slope = cross * over
    rest = jnp.maximum(m[5] - two * m[3] - slope * cross, ROUNDING * m[5])
    right_1 = m[1] - one * m[0]
    right_2 = m[2] - two * m[0] - slope * right_1
    c2 = right_2 / rest
    c1 = (right_1 - cross * c2) * over
    c0 = (m[0] - m[2] * c1 - m[3] * c2) * inverse
    wide = [jnp.concatenate([c] * (depth // 128), axis=1) for c in (c0, c1, c2)]

    zeroth = z0_layers(cuts, layers, za, zb, zc)
    first = Layers((0, 1, ones_left, 1, 2), (1, layers - 1, ones_in, 0, layers + 1))
    second = Layers((0, 2, twos_left, 0, 2), (2, layers - 2, twos_in, 0, layers - 1))
    total = swap.shape[0] // modes
    theirs = [
        Layers((0, layers, swap, 0, total)),
        Layers((0, 1, swap, 3 * layers - 3, total), (1, layers - 1, swap, layers, total)),
        Layers((0, 2, swap, 3 * layers - 2, total), (2, layers - 2, swap, 2 * layers - 1, total)),
    ]

    copies = []
    for is_own in (True, False):
        start = (core if is_own else 1 - core) * modes
        first_group = start == 0
        chosen = [jnp.where(first_group, c[:8], c[8:]) for c in wide]
        for mode in range(modes):
            a, b, c = (f[mode : mode + 1] for f in chosen)
            for x in range(layers):
                planes = []
                for field in (zeroth, first, second) if is_own else theirs:
                    ref, offset, stride = field.where[x]
                    rows = pl.ds(mine, half) if is_own else slice(None)
                    planes.append(ref[mode * stride + offset, rows, :])
                out[start + mode, x] = a * planes[0] + b * planes[1] + c * planes[2]
            copy = pltpu.make_async_copy(out.at[start + mode], out_hbm.at[start + mode], sems.at[len(copies)])
            copy.start()
            copies.append(copy)
    for copy in copies:
        copy.wait()


def local(mode_shapes, eigenvalues, density, filter_mass, passive):
    f32 = jnp.float32
    layers, half, depth = density.shape
    group = mode_shapes.shape[0] // 2
    modes = group // 3
    width = 2 * half
    count = lax.axis_size("gx")
    across = [(0, 1), (1, 0)]
    downward = [(i, i - 1) for i in range(1, count)]
    upward = [(i, i + 1) for i in range(count - 1)]
    vmem = pl.BlockSpec(memory_space=pltpu.VMEM)
    anywhere = pl.BlockSpec(memory_space=pl.ANY)

    def planes(n, rows=width):
        return jax.ShapeDtypeStruct((n, rows, depth), f32)

    def kernel(name, body, outs, in_specs, scratch, limit, work, out_spec=vmem, aliases={}):
        return pl.pallas_call(
            body,
            out_shape=outs,
            in_specs=in_specs,
            out_specs=jax.tree.map(lambda _: out_spec, outs),
            input_output_aliases=aliases,
            scratch_shapes=scratch,
            compiler_params=pltpu.CompilerParams(vmem_limit_bytes=limit * 2**20),
            cost_estimate=pl.CostEstimate(flops=work * 2**20, bytes_accessed=2**20, transcendentals=0),
            name=name,
        )

    stored = [pltpu.with_memory_space_constraint(x, pltpu.HBM) for x in (mode_shapes, density, filter_mass, passive)]
    node, node_crossed, fields = kernel(
        "first_layer",
        first_kernel,
        (planes(group + 2, half), planes(group, half), planes(2 * layers, half)),
        [anywhere] * 4,
        [
            pltpu.VMEM((layers, half, depth), f32),
            pltpu.VMEM((layers, half, depth), jnp.int32),
            pltpu.SemaphoreType.DMA((6,)),
        ],
        4,
        1,
    )(*stored)
    operands = [mode_shapes, lax.ppermute(mode_shapes, "gy", across), fields, lax.ppermute(fields, "gy", across)]
    straight = [(2 * i + c, 2 * i - 2 + c) for i in range(1, count) for c in (0, 1)]
    crossed = [(2 * i + c, 2 * i - 1 - c) for i in range(1, count) for c in (0, 1)]
    halo = lax.ppermute(node, ("gx", "gy"), straight)
    halo_swap = lax.ppermute(node_crossed, ("gx", "gy"), crossed)

    cuts = (DOWN, layers - UP)

    def energies(name, low, high, *extra):
        end = high == layers
        n = high - low
        outs = (planes(modes * n + end), planes(n))
        return kernel(
            name,
            partial(energy_kernel, low, high, end),
            outs + (planes(2, half),) if end else outs,
            [vmem] * (5 + 2 * end) + [anywhere] * (len(extra) - 2 * end),
            [
                pltpu.VMEM((2, n, width, depth), f32),
                pltpu.VMEM((4, 12, width, depth), f32),
            ],
            12,
            n * 200,
        )(eigenvalues[None], *operands, *extra)

    za, ma = energies("energies_first", 0, cuts[0])
    down = lax.ppermute(za, "gx", downward)
    zb, mb = energies("energies_inner", cuts[0], cuts[1], ma)
    zc, mc, ghost_mass = energies("energies_last", cuts[1], layers, halo, halo_swap, mb)
    up = lax.ppermute(zc, "gx", upward)
    ghost_swap = lax.ppermute(ghost_mass, "gy", across)

    tables = [pltpu.VMEM((layers + 2, width, depth), f32)] * 2
    sums = jax.ShapeDtypeStruct((6 * modes, 8, 128), f32)
    ones_in, twos_in, moments, send = kernel(
        "krylov_main",
        partial(main_kernel, modes, layers, cuts),
        (planes(modes * (layers + 1)), planes(modes * (layers - 1)), sums, planes(modes * 3 * layers, half)),
        [vmem] * 9,
        tables + [pltpu.VMEM((2, width, depth), f32), pltpu.SemaphoreType.DMA((5 * modes,))],
        12,
        400,
    )(za, zb, zc, ma, mb, mc, down, ghost_mass, ghost_swap)
    ones_left, twos_left, send, parts = kernel(
        "krylov_left",
        partial(left_kernel, modes, layers, cuts),
        (
            planes(2 * modes),
            planes(2 * modes),
            planes(modes * 3 * layers, half),
            jax.ShapeDtypeStruct((2 * count, 8, 128), f32),
        ),
        [vmem] * 7,
        tables + [pltpu.VMEM((6 * modes, 8, 128), f32)],
        12,
        200,
        aliases={6: 2},
    )(za, ma, up, ones_in, twos_in, moments, send)
    swap_in = lax.ppermute(send, "gy", across)
    parts = lax.all_to_all(parts, ("gx", "gy"), 0, 0, tiled=True)

    return kernel(
        "combine",
        partial(combine_kernel, modes, layers, cuts),
        jax.ShapeDtypeStruct((2 * modes, layers, half, depth), f32),
        [vmem] * 9,
        [pltpu.VMEM((2 * modes, layers, half, depth), f32), pltpu.SemaphoreType.DMA((2 * modes,))],
        12,
        100,
        anywhere,
    )(parts, za, zb, zc, ones_in, twos_in, ones_left, twos_left, swap_in)


def solution(mesh):
    in_specs = (
        P("grp", "gx", "gy", None),
        P("grp"),
        P(("grp", "gx"), "gy", None),
        P(("grp", "gx"), "gy", None),
        P(("grp", "gx"), "gy", None),
    )
    out_specs = P("grp", "gx", "gy", None)
    return jax.shard_map(local, mesh=mesh, in_specs=in_specs, out_specs=out_specs, check_vma=False)
```
